256 devices in a mesh: dp: 32 (over z, x_lo, core), tensor: 8 (over y, x_hi).
Axes of the slice: x: 4 (x_hi: 2, x_lo: 2; x = x_hi * 2 + x_lo), y: 4, z: 8, core: 2. Of those that a mesh axis runs over, the one named last changes fastest.
Arguments:
- grad_out: bfloat16 [16384, 4096], P(('dp', 'tensor')), may hold values from -4 to 4
- x_act: bfloat16 [16384, 8192], P('dp', 'tensor'), may hold values from -6 to 6
- z_act: bfloat16 [16384, 8192], P('dp', 'tensor'), may hold values from -6 to 6
- b_act: bfloat16 [16384, 8, 128], P('dp', 'tensor'), may hold values from -2 to 2
- c_act: bfloat16 [16384, 8, 128], P('dp', 'tensor'), may hold values from -2 to 2
- step_size: float32 [16384, 128], P('dp', 'tensor'), may hold values from 0.001 to 0.3
- log_rate: float32 [128], P('tensor'), may hold values from -0.7 to 2.5
- skip_gain: float32 [128], P('tensor'), may hold values from 0.5 to 1.5
- norm_gain: float32 [8192], P('tensor'), may hold values from 0.5 to 1.5
- w_out: bfloat16 [4096, 8192], P('dp', 'tensor'), may hold values from -0.0625 to 0.0625
Outputs:
- grad_x: bfloat16 [16384, 8192], P('dp', 'tensor')
- grad_z: bfloat16 [16384, 8192], P('dp', 'tensor')
- grad_b: bfloat16 [16384, 8, 128], P('dp', 'tensor')
- grad_c: bfloat16 [16384, 8, 128], P('dp', 'tensor')
- grad_step: float32 [16384, 128], P('dp', 'tensor')
- grad_log_rate: float32 [128], P('tensor')
- grad_skip: float32 [128], P('tensor')
- grad_norm_gain: float32 [8192], P('tensor')
- grad_w_out: float32 [4096, 8192], P('dp', 'tensor')
The draws below stay inside these ranges and needn't reach their ends.
All inputs are finite; a program needn't handle non-finite values.
Results may differ from the reference program's by a relative error of at most 0.0029.
Values may be sent and summed in bfloat16 or wider, within the bound.
No kernel may reach another device: no remote copies, remote signals or barrier semaphores. Data moves between devices by JAX's collectives and lax.ppermute only.
A program may use at most 192 MiB of HBM per device.

```python
import math
import jax
import jax.numpy as jnp
from jax import lax

D = 4096
SCAN_HEADS = 128
HEAD_DIM = 64
STATE = 128
GROUPS = 8
SPAN = 256
TOK_DEV = 512
INNER = 8192
TOKEN_TOTAL = 16384
N_DP = 32


def draw_step_size(key, part):
    key = jax.random.fold_in(key, 7)
    decay_random_key, jitter_random_key, spike_random_key, magnitude_random_key = jax.random.split(key, 4)
    head_baseline = jnp.exp(jax.random.uniform(decay_random_key, (1, SCAN_HEADS), jnp.float32, math.log(0.002), math.log(0.08)))
    jitter_amplitude = jnp.exp(jax.random.uniform(jitter_random_key, (TOKEN_TOTAL, SCAN_HEADS), jnp.float32, -0.69, 0.69))
    spike_values = jnp.where(jax.random.uniform(spike_random_key, (TOKEN_TOTAL, 1), jnp.float32) < 0.01, 1.0, 0.0)
    spike_magnitude = jax.random.uniform(magnitude_random_key, (TOKEN_TOTAL, SCAN_HEADS), jnp.float32, 0.03, 0.12)
    return (head_baseline * jitter_amplitude + spike_values * spike_magnitude).astype(jnp.float32)


def with_spikes(values, rng, source, target, shards_of, factor):
    owner, partner = [(jnp.arange(values.shape[position]) // (values.shape[position] // shards_of)).reshape([-1 if axis == position else 1 for axis in range(values.ndim)]) for position in (source, target)]
    chosen = jax.random.permutation(rng, shards_of)[partner]
    strong = (owner == chosen) | (owner == (partner + shards_of // 2) % shards_of)
    return jnp.where(strong, factor * values, values)


def level_of(key, dims, cuts, low, largest):
    gain = 1.0
    for axis_at, shards_of in cuts:
        draws = jax.random.uniform(jax.random.fold_in(jax.random.fold_in(key, 6), axis_at), (shards_of,), jnp.float32, low / len(cuts), largest / len(cuts))
        gain = gain * jnp.repeat(jnp.exp(draws), dims[axis_at] // shards_of).reshape((-1,) + (1,) * (len(dims) - 1 - axis_at))
    return gain


def centred(stream_key, shape, deviation, limit, cuts=(), kind=jnp.bfloat16):
    entries = jax.random.normal(stream_key, shape, jnp.float32) * deviation
    if len(cuts) > 0:
        entries = level_of(stream_key, shape, cuts, -0.22, 0.18) * entries
    return jnp.clip(entries, min=-limit, max=limit).astype(kind)


def noise_with(rng, shape, width, reach, shards, heavy, kind=jnp.bfloat16):
    values = width * jax.random.normal(rng, shape, jnp.float32)
    if shards:
        values = values * level_of(rng, shape, shards, -0.22, 0.18)
    return jnp.clip(with_spikes(values, jax.random.fold_in(rng, 3), *heavy), -reach, reach).astype(kind)


def setup_inputs(seed: int = 0) -> dict:
    arg_keys = jax.random.split(jax.random.key(seed), 11)
    grad_out = noise_with(arg_keys[0], (TOKEN_TOTAL, D), 0.15, 4.0, ((0, 256),), (0, 1, 256, 6.0))
    x_act = centred(arg_keys[1], (TOKEN_TOTAL, INNER), 1.0, 6.0, ((0, 32), (1, 8)))
    z_act = centred(arg_keys[2], (TOKEN_TOTAL, INNER), 1.0, 6.0, ((0, 32), (1, 8)))
    b_act = centred(arg_keys[3], (TOKEN_TOTAL, GROUPS, STATE), 0.3, 2.0, ((0, 32), (1, 8)))
    c_act = centred(arg_keys[4], (TOKEN_TOTAL, GROUPS, STATE), 0.3, 2.0, ((0, 32), (1, 8)))
    step_size = draw_step_size(jax.random.fold_in(arg_keys[10], 71), 0)
    log_rate = jnp.clip(-0.7 + 3.2 * jax.random.uniform(arg_keys[6], (SCAN_HEADS,), jnp.float32) ** level_of(arg_keys[6], (SCAN_HEADS,), ((0, 8),), -0.2, 0.2), -0.7, 2.5)
    skip_gain = jnp.clip(0.5 + 1.0 * jax.random.uniform(arg_keys[7], (SCAN_HEADS,), jnp.float32) ** level_of(arg_keys[7], (SCAN_HEADS,), ((0, 8),), -0.2, 0.2), 0.5, 1.5)
    norm_gain = jnp.clip(1.0 + 0.1 * jax.random.normal(arg_keys[8], (INNER,), jnp.float32), 0.5, 1.5)
    w_out = centred(arg_keys[9], (D, INNER), INNER ** -0.5, 0.0625, ((0, 32), (1, 8)))
    return dict(grad_out=grad_out, x_act=x_act, z_act=z_act, b_act=b_act, c_act=c_act, step_size=step_size, log_rate=log_rate, skip_gain=skip_gain, norm_gain=norm_gain, w_out=w_out)


HIGH = lax.Precision.HIGHEST

def ssd_scan(inputs, step_in, log_in, b_in, c_in, skip_in):
    length, head_count, head_width = inputs.shape
    groups = b_in.shape[1]
    per_group = head_count // groups
    blocks = length // SPAN
    neg_rate = -jnp.exp(log_in)
    cumulative = jnp.cumsum((step_in * neg_rate[None, :]).reshape(blocks, SPAN, head_count), axis=1)
    cum_heads = jnp.transpose(cumulative.reshape(blocks, SPAN, groups, per_group), (0, 2, 3, 1))
    scaled = (inputs * step_in[:, :, None]).reshape(blocks, SPAN, groups, per_group, head_width)
    b_block = b_in.reshape(blocks, SPAN, groups, -1)
    c_block = c_in.reshape(blocks, SPAN, groups, -1)
    scores = jnp.einsum('kign,kjgn->kgij', c_block, b_block, precision=HIGH)
    causal = lax.broadcasted_iota(jnp.int32, (SPAN, SPAN), 0) >= lax.broadcasted_iota(jnp.int32, (SPAN, SPAN), 1)
    log_gap = cum_heads[..., :, None] - cum_heads[..., None, :]
    decays = jnp.exp(jnp.where(causal, log_gap, -10000.0))
    weighted = scores[:, :, None] * decays
    within = jnp.einsum('kghij,kjghp->kighp', weighted, scaled, precision=HIGH)
    to_end = jnp.exp(cum_heads[..., -1:] - cum_heads)
    states = jnp.einsum('kjgn,kghj,kjghp->kghnp', b_block, to_end, scaled, precision=HIGH)
    fading = jnp.exp(cum_heads[..., -1])

    def advance(carried, pieces):
        return (pieces[0][..., None, None] * carried + pieces[1], carried)
    _, entering = lax.scan(advance, jnp.zeros(states.shape[1:], jnp.float32), (fading, states))
    across = jnp.einsum('kign,kghnp,kghi->kighp', c_block, entering, jnp.exp(cum_heads), precision=HIGH)
    return (within + across).reshape(length, head_count, head_width) + skip_in[None, :, None] * inputs

def gate_norm(mixed_out, gate_in, gain_in, groups):
    length = mixed_out.shape[0]
    gated_out = mixed_out.reshape(length, groups, -1) * jax.nn.silu(gate_in).reshape(length, groups, -1)
    inverse = lax.rsqrt(lax.optimization_barrier(jnp.mean(gated_out * gated_out, axis=-1, keepdims=True)) + 1e-05)
    return (gated_out * inverse).reshape(length, -1) * gain_in[None, :]

def layer_grads(x_rows, z_rows, b_rows, c_rows, step_rows, log_in, skip_in, gain_in, upstream):
    head_count = x_rows.shape[1] // HEAD_DIM
    groups = b_rows.shape[1]

    def forward(inputs, gate_in, b_in, c_in, step_in, log_arg, skip_arg, gain_arg):
        mixed_out = ssd_scan(inputs.reshape(-1, head_count, HEAD_DIM), step_in, log_arg, b_in, c_in, skip_arg)
        return gate_norm(mixed_out, gate_in, gain_arg, groups)
    normed, pull_back = jax.vjp(forward, x_rows.astype(jnp.float32), z_rows.astype(jnp.float32), b_rows.astype(jnp.float32), c_rows.astype(jnp.float32), step_rows, log_in, skip_in, gain_in)
    return (normed.astype(jnp.bfloat16), pull_back(upstream))

def reference(grad_out, x_act, z_act, b_act, c_act, step_size, log_rate, skip_gain, norm_gain, w_out):
    contract = (((0,), (0,)), ((), ()))

    def one_block(totals, block_index):
        row_start = block_index * TOK_DEV

        def take_rows(array):
            return lax.dynamic_slice_in_dim(array, row_start, TOK_DEV, 0)
        upstream_rows = take_rows(grad_out)
        upstream = jnp.dot(upstream_rows, w_out, preferred_element_type=jnp.float32)
        normed, all_grads = layer_grads(take_rows(x_act), take_rows(z_act), take_rows(b_act), take_rows(c_act), take_rows(step_size), log_rate, skip_gain, norm_gain, upstream)
        weight_term = lax.dot_general(upstream_rows, normed, contract, preferred_element_type=jnp.float32)
        totals = (totals[0] + weight_term, totals[1] + all_grads[5], totals[2] + all_grads[6], totals[3] + all_grads[7])
        per_block = (all_grads[0].astype(jnp.bfloat16), all_grads[1].astype(jnp.bfloat16), all_grads[2].astype(jnp.bfloat16), all_grads[3].astype(jnp.bfloat16), all_grads[4])
        return (totals, per_block)
    initial = (jnp.zeros((D, INNER), jnp.float32), jnp.zeros((SCAN_HEADS,), jnp.float32), jnp.zeros((SCAN_HEADS,), jnp.float32), jnp.zeros((INNER,), jnp.float32))
    totals, per_block = lax.scan(one_block, initial, jnp.arange(N_DP, dtype=jnp.int32))
    return (per_block[0].reshape(TOKEN_TOTAL, INNER), per_block[1].reshape(TOKEN_TOTAL, INNER), per_block[2].reshape(TOKEN_TOTAL, GROUPS, STATE), per_block[3].reshape(TOKEN_TOTAL, GROUPS, STATE), per_block[4].reshape(TOKEN_TOTAL, SCAN_HEADS), totals[1], totals[2], totals[3], totals[0])
```

```python
import jax
import jax.numpy as jnp
from jax import lax
from jax.experimental import pallas as pl
from jax.experimental.pallas import tpu as pltpu
from jax.sharding import PartitionSpec as P

F32, BF16 = jnp.float32, jnp.bfloat16
HEADS = 16
SPAN = 256
TOK = 512
CH = 1024
HALF = 128
LOG2E = 1.4426950408889634
BIG = 126.0
VMEM_LIMIT = 48 * 1024 * 1024


def dot(a, b):
    return jnp.dot(a, b, preferred_element_type=F32)


def dot_nt(a, b):
    return lax.dot_general(a, b, (((1,), (1,)), ((), ())), preferred_element_type=F32)


def split2(v):
    hi = v.astype(BF16)
    return hi, (v - hi.astype(F32)).astype(BF16)


def dot3(a, b, fn):
    ah, al = split2(a)
    bh, bl = split2(b)
    return fn(ah, bh) + (fn(ah, bl) + fn(al, bh))


def spread_matrix(width):
    row = lax.broadcasted_iota(jnp.int32, (128, HEADS * width), 0)
    col = lax.broadcasted_iota(jnp.int32, (128, HEADS * width), 1)
    return jnp.where((row < 48) & ((row & 15) == col // width), 1.0, 0.0).astype(BF16)


def parts3(v):
    lane = lax.broadcasted_iota(jnp.int32, v.shape, 1)
    v = jnp.where(lane < HEADS, v, 0.0)
    one = v.astype(BF16).astype(F32)
    rest = v - one
    two = rest.astype(BF16).astype(F32)
    three = rest - two
    return (one + pltpu.roll(two, 16, 1) + pltpu.roll(three, 32, 1)).astype(BF16)


def cumulate(tri, v):
    one = v.astype(BF16)
    rest = v - one.astype(F32)
    two = rest.astype(BF16)
    three = (rest - two.astype(F32)).astype(BF16)
    return dot(tri, one) + (dot(tri, two) + dot(tri, three))


def triangle(n, lower):
    row = lax.broadcasted_iota(jnp.int32, (n, n), 0)
    col = lax.broadcasted_iota(jnp.int32, (n, n), 1)
    return jnp.where(row >= col if lower else row <= col, 1.0, 0.0).astype(BF16)


def prepare(dt_ref, rate_ref, pad_ref, ratepad_ref):
    pad_ref[...] = jnp.ones((TOK, 128), F32)
    pad_ref[:, :HEADS] = dt_ref[...]
    ratepad_ref[...] = jnp.zeros((8, 128), F32)
    ratepad_ref[0:1, :HEADS] = rate_ref[...]
    rate = -jnp.exp(ratepad_ref[0:1, :])
    tri = triangle(SPAN, True)
    cums, rs = [], []
    for k in range(2):
        dt = pad_ref[k * SPAN:(k + 1) * SPAN, :]
        cum = cumulate(tri, dt * (rate * LOG2E))
        cums.append(cum)
        rs.append(jnp.log2(dt) - cum)
    return rate, cums, rs


def fwd_kernel(x_ref, z_ref, b_ref, c_ref, dt_ref, rate_ref, skip_ref, gain_ref,
               ys_ref, n_ref, pad_ref, ratepad_ref, cexp_ref, rt_ref, s_ref, coef_ref):
    rate, cums, rs = prepare(dt_ref, rate_ref, pad_ref, ratepad_ref)
    wide = spread_matrix(HALF)
    narrow = spread_matrix(64)
    row = lax.broadcasted_iota(jnp.int32, (SPAN, SPAN), 0)
    col = lax.broadcasted_iota(jnp.int32, (SPAN, SPAN), 1)
    ratepad_ref[0:1, :HEADS] = skip_ref[...]
    skip = ratepad_ref[0:1, :]
    for k in range(2):
        rows = slice(k * SPAN, (k + 1) * SPAN)
        cexp_ref[rows, :] = dot(parts3(cums[k]), wide)
        rt_ref[k] = rs[k].T
        bk, ck = b_ref[rows, :], c_ref[rows, :]
        s_ref[k] = jnp.where(row > col, dot_nt(ck, bk), 0.0)
        diag = jnp.sum(bk.astype(F32) * ck.astype(F32), axis=1, keepdims=True)
        coef_ref[rows, :] = dot(parts3(diag * pad_ref[rows, :] + skip), narrow)
    lane = lax.broadcasted_iota(jnp.int32, (SPAN, 128), 1)

    def pair(hp, _):
        cols = pl.ds(pl.multiple_of(hp * 128, 128), 128)
        for k in range(2):
            rows = slice(k * SPAN, (k + 1) * SPAN)
            xp = x_ref[rows, cols]
            ys = []
            for half in range(2):
                h = hp * 2 + half
                rrow = rt_ref[k, pl.ds(h, 1), :]
                hcols = pl.ds(pl.multiple_of(h * 128, 128), 128)
                top = cexp_ref[k * SPAN:k * SPAN + HALF, hcols]
                bot = cexp_ref[k * SPAN + HALF:(k + 1) * SPAN, hcols]
                wt = s_ref[k, :HALF, :HALF] * jnp.exp2(jnp.minimum(top + rrow[:, :HALF], BIG))
                wb = s_ref[k, HALF:, :] * jnp.exp2(
                    jnp.minimum(jnp.concatenate([bot, bot], axis=1) + rrow, BIG))
                th, tl = split2(wt)
                bh, bl = split2(wb)
                yt = dot(th, xp[:HALF]) + dot(tl, xp[:HALF])
                yb = dot(bh, xp) + dot(bl, xp)
                ys.append(jnp.concatenate([yt, yb], axis=0))
            ys_ref[rows, cols] = jnp.where(lane < 64, ys[0], ys[1])
        return 0

    lax.fori_loop(0, 8, pair, 0)

    s10 = dot_nt(c_ref[SPAN:, :], b_ref[:SPAN, :])
    qdt = parts3(jnp.exp2(cums[0][SPAN - 1:SPAN, :] + rs[0]))
    p = parts3(jnp.exp2(cums[1]))
    for j in range(4):
        cols = slice(j * 256, (j + 1) * 256)
        xq = dot(qdt, narrow[:, cols]) * x_ref[:SPAN, cols].astype(F32)
        ys_ref[SPAN:, cols] += dot(p, narrow[:, cols]) * dot3(s10, xq, dot)

    gain = gain_ref[...]

    def norm(i, _):
        rows = pl.ds(pl.multiple_of(i * 32, 32), 32)
        z = z_ref[rows, :].astype(F32)
        y = ys_ref[rows, :] + coef_ref[rows, :] * x_ref[rows, :].astype(F32)
        gated = y * (z / (1.0 + jnp.exp(-z)))
        inv = lax.rsqrt(jnp.mean(gated * gated, axis=1, keepdims=True) + 1e-05)
        n_ref[rows, :] = (gated * inv * gain).astype(BF16)
        return 0

    lax.fori_loop(0, TOK // 32, norm, 0)


def bwd_kernel(u_ref, ys_ref, x_ref, z_ref, b_ref, c_ref, dt_ref, rate_ref, skip_ref, gain_ref,
               dx_ref, dz_ref, db_ref, dc_ref, ddt_ref, small_ref,
               pad_ref, ratepad_ref, rexp_ref, ct_ref, s_ref, coef_ref, dy_ref, dxs_ref, ds_ref, dg_ref):
    rate, cums, rs = prepare(dt_ref, rate_ref, pad_ref, ratepad_ref)
    wide = spread_matrix(HALF)
    narrow = spread_matrix(64)
    row = lax.broadcasted_iota(jnp.int32, (SPAN, SPAN), 0)
    col = lax.broadcasted_iota(jnp.int32, (SPAN, SPAN), 1)
    ratepad_ref[0:1, :HEADS] = skip_ref[...]
    skip = ratepad_ref[0:1, :]
    diags = []
    for k in range(2):
        rows = slice(k * SPAN, (k + 1) * SPAN)
        rexp_ref[rows, :] = dot(parts3(rs[k]), wide)
        ct_ref[k] = cums[k].T
        bk, ck = b_ref[rows, :], c_ref[rows, :]
        s_ref[k] = jnp.where(row < col, dot_nt(bk, ck), 0.0)
        diag = jnp.sum(bk.astype(F32) * ck.astype(F32), axis=1, keepdims=True)
        diags.append(diag)
        coef_ref[rows, :] = dot(parts3(diag * pad_ref[rows, :] + skip), narrow)

    gain = gain_ref[...]
    dg_ref[...] = jnp.zeros((8, CH), F32)

    def gate(i, _):
        rows = pl.ds(pl.multiple_of(i * 32, 32), 32)
        z = z_ref[rows, :].astype(F32)
        y = ys_ref[rows, :] + coef_ref[rows, :] * x_ref[rows, :].astype(F32)
        sig = 1.0 / (1.0 + jnp.exp(-z))
        sz = z * sig
        gated = y * sz
        inv = lax.rsqrt(jnp.mean(gated * gated, axis=1, keepdims=True) + 1e-05)
        unit = gated * inv
        u = u_ref[rows, :]
        ug = u * unit
        dg_ref[...] += (ug[0:8] + ug[8:16]) + (ug[16:24] + ug[24:32])
        v = u * gain
        dgated = inv * (v - unit * jnp.mean(v * unit, axis=1, keepdims=True))
        dy_ref[rows, :] = dgated * sz
        dz_ref[rows, :] = (dgated * y * (sig * (1.0 + z * (1.0 - sig)))).astype(BF16)
        return 0

    lax.fori_loop(0, TOK // 32, gate, 0)

    ds_ref[...] = jnp.zeros((2, SPAN, SPAN), F32)
    lane = lax.broadcasted_iota(jnp.int32, (SPAN, 128), 1)

    def pair(hp, _):
        cols = pl.ds(pl.multiple_of(hp * 128, 128), 128)
        for k in range(2):
            rows = slice(k * SPAN, (k + 1) * SPAN)
            xp = x_ref[rows, cols].astype(F32)
            dh, dl = split2(dy_ref[rows, cols])
            dhl = jnp.concatenate([dh, dl], axis=1)
            outs = []
            for half in range(2):
                h = hp * 2 + half
                xm = jnp.where((lane < 64) if half == 0 else (lane >= 64), xp, 0.0).astype(BF16)
                xx = jnp.concatenate([xm, xm], axis=1)
                gt = dot_nt(xx[:HALF], dhl)
                gb = dot_nt(xx[HALF:], dhl[HALF:])
                crow = ct_ref[k, pl.ds(h, 1), :]
                hcols = pl.ds(pl.multiple_of(h * 128, 128), 128)
                top = rexp_ref[k * SPAN:k * SPAN + HALF, hcols]
                bot = rexp_ref[k * SPAN + HALF:(k + 1) * SPAN, hcols]
                et = jnp.exp2(jnp.minimum(jnp.concatenate([top, top], axis=1) + crow, BIG))
                eb = jnp.exp2(jnp.minimum(bot + crow[:, HALF:], BIG))
                ds_ref[k, :HALF, :] += et * gt
                ds_ref[k, HALF:, HALF:] += eb * gb
                th, tl = split2(s_ref[k, :HALF, :] * et)
                bh, bl = split2(s_ref[k, HALF:, HALF:] * eb)
                ot = dot(th, dhl)
                ob = dot(bh, dhl[HALF:])
                ot = (ot[:, :128] + ot[:, 128:]) + dot(tl, dh)
                ob = (ob[:, :128] + ob[:, 128:]) + dot(bl, dh[HALF:])
                outs.append(jnp.concatenate([ot, ob], axis=0))
            dxs_ref[rows, cols] = jnp.where(lane < 64, outs[0], outs[1])
        return 0

    lax.fori_loop(0, 8, pair, 0)

    st = dot_nt(b_ref[:SPAN, :], c_ref[SPAN:, :])
    qdt = parts3(jnp.exp2(cums[0][SPAN - 1:SPAN, :] + rs[0]))
    p = parts3(jnp.exp2(cums[1]))
    dst = jnp.zeros((SPAN, SPAN), F32)
    for j in range(4):
        cols = slice(j * 256, (j + 1) * 256)
        qx = dot(qdt, narrow[:, cols])
        xq = qx * x_ref[:SPAN, cols].astype(F32)
        pdy = dot(p, narrow[:, cols]) * dy_ref[SPAN:, cols]
        dxs_ref[:SPAN, cols] += qx * dot3(st, pdy, dot)
        dst = dst + dot3(xq, pdy, dot_nt)

    seg_row = lax.broadcasted_iota(jnp.int32, (CH, 128), 0)
    seg_col = lax.broadcasted_iota(jnp.int32, (CH, 128), 1)
    seg = jnp.where(seg_row // 64 == seg_col, 1.0, 0.0).astype(BF16)

    def heads_sum(v):
        hi, lo = split2(v)
        return dot(hi, seg) + dot(lo, seg)

    tri = triangle(SPAN, False)
    later = jnp.zeros((1, 128), F32)
    rate_sum = jnp.zeros((1, 128), F32)
    skip_sum = jnp.zeros((1, 128), F32)
    for k in (1, 0):
        rows = slice(k * SPAN, (k + 1) * SPAN)
        xf = x_ref[rows, :].astype(F32)
        dy = dy_ref[rows, :]
        dxs = dxs_ref[rows, :]
        kx = heads_sum(dy * xf)
        r = heads_sum(dy * ys_ref[rows, :])
        q = heads_sum(xf * dxs)
        suffix = cumulate(tri, r - q) + later
        later = suffix[0:1, :]
        dt = pad_ref[rows, :]
        ddt = q / dt + kx * diags[k] + rate * suffix
        ddt_ref[rows, :] = ddt[:, :HEADS]
        rate_sum = rate_sum + rate * jnp.sum(dt * suffix, axis=0, keepdims=True)
        skip_sum = skip_sum + jnp.sum(kx, axis=0, keepdims=True)
        sd = jnp.sum(dt * kx, axis=1, keepdims=True)
        dsk = jnp.where(row < col, ds_ref[k], 0.0)
        bk, ck = b_ref[rows, :], c_ref[rows, :]
        sh, sl = split2(dsk)
        db = dot(sh, ck) + dot(sl, ck) + sd * ck.astype(F32)
        sh, sl = split2(dsk.T)
        dc = dot(sh, bk) + dot(sl, bk) + sd * bk.astype(F32)
        if k == 0:
            oh, ol = split2(dst)
            db = db + dot(oh, c_ref[SPAN:, :]) + dot(ol, c_ref[SPAN:, :])
        else:
            oh, ol = split2(dst.T)
            dc = dc + dot(oh, b_ref[:SPAN, :]) + dot(ol, b_ref[:SPAN, :])
        db_ref[rows, :] = db.astype(BF16)
        dc_ref[rows, :] = dc.astype(BF16)
        dx_ref[rows, :] = (dxs + coef_ref[rows, :] * dy).astype(BF16)

    dg = jnp.sum(dg_ref[...], axis=0, keepdims=True)
    for j in range(8):
        small_ref[j:j + 1, :] = dg[:, j * 128:(j + 1) * 128]
    small_ref[8:9, :] = rate_sum
    small_ref[9:10, :] = skip_sum
    small_ref[10:16, :] = jnp.zeros((6, 128), F32)


def scan_forward(x, z, b, c, dt, rate, skip, gain):
    return pl.pallas_call(
        fwd_kernel,
        out_shape=(jax.ShapeDtypeStruct((TOK, CH), F32), jax.ShapeDtypeStruct((TOK, CH), BF16)),
        scratch_shapes=[
            pltpu.VMEM((TOK, 128), F32),
            pltpu.VMEM((8, 128), F32),
            pltpu.VMEM((TOK, HEADS * HALF), F32),
            pltpu.VMEM((2, 128, SPAN), F32),
            pltpu.VMEM((2, SPAN, SPAN), F32),
            pltpu.VMEM((TOK, CH), F32),
        ],
        compiler_params=pltpu.CompilerParams(vmem_limit_bytes=VMEM_LIMIT),
        cost_estimate=pl.CostEstimate(flops=3_000_000_000, bytes_accessed=8_000_000, transcendentals=3_000_000),
        name="scan_forward",
    )(x, z, b, c, dt, rate, skip, gain)


def scan_backward(u, ys, x, z, b, c, dt, rate, skip, gain):
    return pl.pallas_call(
        bwd_kernel,
        out_shape=(
            jax.ShapeDtypeStruct((TOK, CH), BF16),
            jax.ShapeDtypeStruct((TOK, CH), BF16),
            jax.ShapeDtypeStruct((TOK, 128), BF16),
            jax.ShapeDtypeStruct((TOK, 128), BF16),
            jax.ShapeDtypeStruct((TOK, HEADS), F32),
            jax.ShapeDtypeStruct((16, 128), F32),
        ),
        scratch_shapes=[
            pltpu.VMEM((TOK, 128), F32),
            pltpu.VMEM((8, 128), F32),
            pltpu.VMEM((TOK, HEADS * HALF), F32),
            pltpu.VMEM((2, 128, SPAN), F32),
            pltpu.VMEM((2, SPAN, SPAN), F32),
            pltpu.VMEM((TOK, CH), F32),
            pltpu.VMEM((TOK, CH), F32),
            pltpu.VMEM((TOK, CH), F32),
            pltpu.VMEM((2, SPAN, SPAN), F32),
            pltpu.VMEM((8, CH), F32),
        ],
        compiler_params=pltpu.CompilerParams(vmem_limit_bytes=VMEM_LIMIT),
        cost_estimate=pl.CostEstimate(flops=10_000_000_000, bytes_accessed=12_000_000, transcendentals=3_000_000),
        name="scan_backward",
    )(u, ys, x, z, b, c, dt, rate, skip, gain)


AXES = {"z": 8, "xl": 2, "c": 2, "y": 4, "xh": 2}
DP = ("z", "xl", "c")
TP = ("y", "xh")


def send(v, axis, shift):
    n = AXES[axis]
    return lax.ppermute(v, axis, [(i, (i + shift) % n) for i in range(n)])


def gather_tokens(rows):
    xh, y = lax.axis_index("xh"), lax.axis_index("y")
    other = send(rows, "xh", 1)
    first = jnp.where(xh == 0, rows, other)
    second = jnp.where(xh == 0, other, rows)
    own = jnp.concatenate([first, second], axis=0)
    below = send(own, "y", 1)
    above = send(own, "y", -1)
    far_a = send(below[:64], "y", 1)
    far_b = send(above[64:], "y", -1)
    far = jnp.concatenate([far_a, far_b], axis=0)
    out = jnp.zeros((TOK, rows.shape[1]), rows.dtype)
    for k, v in ((0, own), (3, below), (1, above), (2, far)):
        out = lax.dynamic_update_slice_in_dim(out, v, ((y + k) % 4) * 128, 0)
    return out


def scatter_sum(part):
    z = lax.axis_index("z")

    def mine(shift):
        return lax.dynamic_index_in_dim(part, (z + shift) % 8, 0, keepdims=False)

    half = CH // 2
    far = mine(4).astype(BF16)
    down, up = far[:, :half], far[:, half:]
    down = send(down, "z", -1)
    up = send(up, "z", 1)
    v = mine(-3)
    down = send(jnp.concatenate([v[:, :half] + down.astype(F32), v[:, half:]], axis=1).astype(BF16), "z", -1)
    v = mine(3)
    up = send(jnp.concatenate([v[:, :half], v[:, half:] + up.astype(F32)], axis=1).astype(BF16), "z", 1)
    for k in (2, 1):
        down = send((mine(-k) + down.astype(F32)).astype(BF16), "z", -1)
        up = send((mine(k) + up.astype(F32)).astype(BF16), "z", 1)
    return mine(0) + (down.astype(F32) + up.astype(F32))


def on_device(grad_out, x, z, b, c, dt, rate, skip, gain, w_out):
    contract = (((0,), (0,)), ((), ()))
    xl, core = lax.axis_index("xl"), lax.axis_index("c")
    scan = (x, z, b.reshape(TOK, 128), c.reshape(TOK, 128), dt, rate[None], skip[None], gain[None])
    w = lax.all_gather(w_out, DP, axis=0, tiled=True)
    rows = gather_tokens(grad_out)
    ys, normed = scan_forward(*scan)
    halves = rows.reshape(TOK, 16, 2, 128)
    keep = lax.dynamic_index_in_dim(halves, core, 2, keepdims=False)
    give = lax.dynamic_index_in_dim(halves, 1 - core, 2, keepdims=False)
    both_rows = jnp.concatenate([keep, send(give, "c", 1)], axis=0).reshape(2 * TOK, 2048)
    both_normed = jnp.concatenate([normed, send(normed, "c", 1)], axis=0)
    part = lax.dot_general(both_rows, both_normed, contract, preferred_element_type=F32)
    total = scatter_sum(part.reshape(8, 256, CH)).reshape(2, 128, CH)
    stay = lax.dynamic_index_in_dim(total, xl, 0, keepdims=False)
    leave = lax.dynamic_index_in_dim(total, 1 - xl, 0, keepdims=False).astype(BF16)
    grad_weight = stay + send(leave, "xl", 1).astype(F32)
    upstream = jnp.dot(rows, w, preferred_element_type=F32)
    dx, dz, db, dc, ddt, small = scan_backward(upstream, ys, *scan)
    small = lax.psum(small, DP)
    return (dx, dz, db[:, None], dc[:, None], ddt, small[8, :HEADS], small[9, :HEADS],
            small[:8].reshape(CH), grad_weight)


def solution(mesh):
    fine = jax.sharding.Mesh(mesh.devices.reshape(tuple(AXES.values())), tuple(AXES))
    part = P(DP, TP)
    part3 = P(DP, TP, None)
    head = P(TP)
    return jax.shard_map(
        on_device,
        mesh=fine,
        in_specs=(P(DP + TP, None), part, part, part3, part3, part, head, head, head, part),
        out_specs=(part, part, part3, part3, part, head, head, head, part),
        check_vma=False,
    )
```

```python
import jax
import jax.numpy as jnp
from jax import lax
from jax.experimental import pallas as pl
from jax.experimental.pallas import tpu as pltpu
from jax.sharding import PartitionSpec as P

F32, BF16 = jnp.float32, jnp.bfloat16
HEADS = 16
SPAN = 256
TOK = 512
CH = 1024
HALF = 128
LOG2E = 1.4426950408889634
BIG = 126.0
VMEM_LIMIT = 48 * 1024 * 1024


def dot(a, b):
    return jnp.dot(a, b, preferred_element_type=F32)


def dot_nt(a, b):
    return lax.dot_general(a, b, (((1,), (1,)), ((), ())), preferred_element_type=F32)


def split2(v):
    hi = v.astype(BF16)
    return hi, (v - hi.astype(F32)).astype(BF16)


def dot3(a, b, fn):
    ah, al = split2(a)
    bh, bl = split2(b)
    return fn(ah, bh) + (fn(ah, bl) + fn(al, bh))


def spread_matrix(width):
    row = lax.broadcasted_iota(jnp.int32, (128, HEADS * width), 0)
    col = lax.broadcasted_iota(jnp.int32, (128, HEADS * width), 1)
    return jnp.where((row < 48) & ((row & 15) == col // width), 1.0, 0.0).astype(BF16)


def parts3(v):
    lane = lax.broadcasted_iota(jnp.int32, v.shape, 1)
    v = jnp.where(lane < HEADS, v, 0.0)
    one = v.astype(BF16).astype(F32)
    rest = v - one
    two = rest.astype(BF16).astype(F32)
    three = rest - two
    return (one + pltpu.roll(two, 16, 1) + pltpu.roll(three, 32, 1)).astype(BF16)


def cumulate(tri, v):
    one = v.astype(BF16)
    rest = v - one.astype(F32)
    two = rest.astype(BF16)
    three = (rest - two.astype(F32)).astype(BF16)
    return dot(tri, one) + (dot(tri, two) + dot(tri, three))


def triangle(n, lower):
    row = lax.broadcasted_iota(jnp.int32, (n, n), 0)
    col = lax.broadcasted_iota(jnp.int32, (n, n), 1)
    return jnp.where(row >= col if lower else row <= col, 1.0, 0.0).astype(BF16)


def prepare(dt_ref, rate_ref, pad_ref, ratepad_ref):
    pad_ref[...] = jnp.ones((TOK, 128), F32)
    pad_ref[:, :HEADS] = dt_ref[...]
    ratepad_ref[...] = jnp.zeros((8, 128), F32)
    ratepad_ref[0:1, :HEADS] = rate_ref[...]
    rate = -jnp.exp(ratepad_ref[0:1, :])
    tri = triangle(SPAN, True)
    cums, rs = [], []
    for k in range(2):
        dt = pad_ref[k * SPAN:(k + 1) * SPAN, :]
        cum = cumulate(tri, dt * (rate * LOG2E))
        cums.append(cum)
        rs.append(jnp.log2(dt) - cum)
    return rate, cums, rs


def fwd_kernel(x_ref, z_ref, b_ref, c_ref, dt_ref, rate_ref, skip_ref, gain_ref,
               ys_ref, n_ref, pad_ref, ratepad_ref, cexp_ref, rt_ref, s_ref, coef_ref):
    rate, cums, rs = prepare(dt_ref, rate_ref, pad_ref, ratepad_ref)
    wide = spread_matrix(HALF)
    narrow = spread_matrix(64)
    row = lax.broadcasted_iota(jnp.int32, (SPAN, SPAN), 0)
    col = lax.broadcasted_iota(jnp.int32, (SPAN, SPAN), 1)
    ratepad_ref[0:1, :HEADS] = skip_ref[...]
    skip = ratepad_ref[0:1, :]
    for k in range(2):
        rows = slice(k * SPAN, (k + 1) * SPAN)
        cexp_ref[rows, :] = dot(parts3(cums[k]), wide)
        rt_ref[k] = rs[k].T
        bk, ck = b_ref[rows, :], c_ref[rows, :]
        s_ref[k] = jnp.where(row > col, dot_nt(ck, bk), 0.0)
        diag = jnp.sum(bk.astype(F32) * ck.astype(F32), axis=1, keepdims=True)
        coef_ref[rows, :] = dot(parts3(diag * pad_ref[rows, :] + skip), narrow)
    lane = lax.broadcasted_iota(jnp.int32, (SPAN, 128), 1)

    def pair(hp, _):
        cols = pl.ds(pl.multiple_of(hp * 128, 128), 128)
        for k in range(2):
            rows = slice(k * SPAN, (k + 1) * SPAN)
            xp = x_ref[rows, cols]
            ys = []
            for half in range(2):
                h = hp * 2 + half
                rrow = rt_ref[k, pl.ds(h, 1), :]
                hcols = pl.ds(pl.multiple_of(h * 128, 128), 128)
                top = cexp_ref[k * SPAN:k * SPAN + HALF, hcols]
                bot = cexp_ref[k * SPAN + HALF:(k + 1) * SPAN, hcols]
                wt = s_ref[k, :HALF, :HALF] * jnp.exp2(jnp.minimum(top + rrow[:, :HALF], BIG))
                wb = s_ref[k, HALF:, :] * jnp.exp2(
                    jnp.minimum(jnp.concatenate([bot, bot], axis=1) + rrow, BIG))
                th, tl = split2(wt)
                bh, bl = split2(wb)
                yt = dot(th, xp[:HALF]) + dot(tl, xp[:HALF])
                yb = dot(bh, xp) + dot(bl, xp)
                ys.append(jnp.concatenate([yt, yb], axis=0))
            ys_ref[rows, cols] = jnp.where(lane < 64, ys[0], ys[1])
        return 0

    lax.fori_loop(0, 8, pair, 0)

    s10 = dot_nt(c_ref[SPAN:, :], b_ref[:SPAN, :])
    qdt = parts3(jnp.exp2(cums[0][SPAN - 1:SPAN, :] + rs[0]))
    p = parts3(jnp.exp2(cums[1]))
    for j in range(4):
        cols = slice(j * 256, (j + 1) * 256)
        xq = dot(qdt, narrow[:, cols]) * x_ref[:SPAN, cols].astype(F32)
        ys_ref[SPAN:, cols] += dot(p, narrow[:, cols]) * dot3(s10, xq, dot)

    gain = gain_ref[...]

    def norm(i, _):
        rows = pl.ds(pl.multiple_of(i * 32, 32), 32)
        z = z_ref[rows, :].astype(F32)
        y = ys_ref[rows, :] + coef_ref[rows, :] * x_ref[rows, :].astype(F32)
        gated = y * (z / (1.0 + jnp.exp(-z)))
        inv = lax.rsqrt(jnp.mean(gated * gated, axis=1, keepdims=True) + 1e-05)
        n_ref[rows, :] = (gated * inv * gain).astype(BF16)
        return 0

    lax.fori_loop(0, TOK // 32, norm, 0)


def bwd_kernel(u_ref, ys_ref, x_ref, z_ref, b_ref, c_ref, dt_ref, rate_ref, skip_ref, gain_ref,
               dx_ref, dz_ref, db_ref, dc_ref, ddt_ref, small_ref,
               pad_ref, ratepad_ref, rexp_ref, ct_ref, s_ref, coef_ref, dy_ref, dxs_ref, ds_ref, dg_ref):
    rate, cums, rs = prepare(dt_ref, rate_ref, pad_ref, ratepad_ref)
    wide = spread_matrix(HALF)
    narrow = spread_matrix(64)
    row = lax.broadcasted_iota(jnp.int32, (SPAN, SPAN), 0)
    col = lax.broadcasted_iota(jnp.int32, (SPAN, SPAN), 1)
    ratepad_ref[0:1, :HEADS] = skip_ref[...]
    skip = ratepad_ref[0:1, :]
    diags = []
    for k in range(2):
        rows = slice(k * SPAN, (k + 1) * SPAN)
        rexp_ref[rows, :] = dot(parts3(rs[k]), wide)
        ct_ref[k] = cums[k].T
        bk, ck = b_ref[rows, :], c_ref[rows, :]
        s_ref[k] = jnp.where(row < col, dot_nt(bk, ck), 0.0)
        diag = jnp.sum(bk.astype(F32) * ck.astype(F32), axis=1, keepdims=True)
        diags.append(diag)
        coef_ref[rows, :] = dot(parts3(diag * pad_ref[rows, :] + skip), narrow)

    gain = gain_ref[...]
    dg_ref[...] = jnp.zeros((8, CH), F32)

    def gate(i, _):
        rows = pl.ds(pl.multiple_of(i * 32, 32), 32)
        z = z_ref[rows, :].astype(F32)
        y = ys_ref[rows, :] + coef_ref[rows, :] * x_ref[rows, :].astype(F32)
        sig = 1.0 / (1.0 + jnp.exp(-z))
        sz = z * sig
        gated = y * sz
        inv = lax.rsqrt(jnp.mean(gated * gated, axis=1, keepdims=True) + 1e-05)
        unit = gated * inv
        u = u_ref[rows, :]
        ug = u * unit
        dg_ref[...] += (ug[0:8] + ug[8:16]) + (ug[16:24] + ug[24:32])
        v = u * gain
        dgated = inv * (v - unit * jnp.mean(v * unit, axis=1, keepdims=True))
        dy_ref[rows, :] = dgated * sz
        dz_ref[rows, :] = (dgated * y * (sig * (1.0 + z * (1.0 - sig)))).astype(BF16)
        return 0

    lax.fori_loop(0, TOK // 32, gate, 0)

    ds_ref[...] = jnp.zeros((2, SPAN, SPAN), F32)
    lane = lax.broadcasted_iota(jnp.int32, (SPAN, 128), 1)

    def pair(hp, _):
        cols = pl.ds(pl.multiple_of(hp * 128, 128), 128)
        for k in range(2):
            rows = slice(k * SPAN, (k + 1) * SPAN)
            xp = x_ref[rows, cols].astype(F32)
            dh, dl = split2(dy_ref[rows, cols])
            dhl = jnp.concatenate([dh, dl], axis=1)
            outs = []
            for half in range(2):
                h = hp * 2 + half
                xm = jnp.where((lane < 64) if half == 0 else (lane >= 64), xp, 0.0).astype(BF16)
                xx = jnp.concatenate([xm, xm], axis=1)
                gt = dot_nt(xx[:HALF], dhl)
                gb = dot_nt(xx[HALF:], dhl[HALF:])
                crow = ct_ref[k, pl.ds(h, 1), :]
                hcols = pl.ds(pl.multiple_of(h * 128, 128), 128)
                top = rexp_ref[k * SPAN:k * SPAN + HALF, hcols]
                bot = rexp_ref[k * SPAN + HALF:(k + 1) * SPAN, hcols]
                et = jnp.exp2(jnp.minimum(jnp.concatenate([top, top], axis=1) + crow, BIG))
                eb = jnp.exp2(jnp.minimum(bot + crow[:, HALF:], BIG))
                ds_ref[k, :HALF, :] += et * gt
                ds_ref[k, HALF:, HALF:] += eb * gb
                th, tl = split2(s_ref[k, :HALF, :] * et)
                bh, bl = split2(s_ref[k, HALF:, HALF:] * eb)
                ot = dot(th, dhl)
                ob = dot(bh, dhl[HALF:])
                ot = (ot[:, :128] + ot[:, 128:]) + dot(tl, dh)
                ob = (ob[:, :128] + ob[:, 128:]) + dot(bl, dh[HALF:])
                outs.append(jnp.concatenate([ot, ob], axis=0))
            dxs_ref[rows, cols] = jnp.where(lane < 64, outs[0], outs[1])
        return 0

    lax.fori_loop(0, 8, pair, 0)

    st = dot_nt(b_ref[:SPAN, :], c_ref[SPAN:, :])
    qdt = parts3(jnp.exp2(cums[0][SPAN - 1:SPAN, :] + rs[0]))
    p = parts3(jnp.exp2(cums[1]))
    dst = jnp.zeros((SPAN, SPAN), F32)
    for j in range(4):
        cols = slice(j * 256, (j + 1) * 256)
        qx = dot(qdt, narrow[:, cols])
        xq = qx * x_ref[:SPAN, cols].astype(F32)
        pdy = dot(p, narrow[:, cols]) * dy_ref[SPAN:, cols]
        dxs_ref[:SPAN, cols] += qx * dot3(st, pdy, dot)
        dst = dst + dot3(xq, pdy, dot_nt)

    seg_row = lax.broadcasted_iota(jnp.int32, (CH, 128), 0)
    seg_col = lax.broadcasted_iota(jnp.int32, (CH, 128), 1)
    seg = jnp.where(seg_row // 64 == seg_col, 1.0, 0.0).astype(BF16)

    def heads_sum(v):
        hi, lo = split2(v)
        return dot(hi, seg) + dot(lo, seg)

    tri = triangle(SPAN, False)
    later = jnp.zeros((1, 128), F32)
    rate_sum = jnp.zeros((1, 128), F32)
    skip_sum = jnp.zeros((1, 128), F32)
    for k in (1, 0):
        rows = slice(k * SPAN, (k + 1) * SPAN)
        xf = x_ref[rows, :].astype(F32)
        dy = dy_ref[rows, :]
        dxs = dxs_ref[rows, :]
        kx = heads_sum(dy * xf)
        r = heads_sum(dy * ys_ref[rows, :])
        q = heads_sum(xf * dxs)
        suffix = cumulate(tri, r - q) + later
        later = suffix[0:1, :]
        dt = pad_ref[rows, :]
        ddt = q / dt + kx * diags[k] + rate * suffix
        ddt_ref[rows, :] = ddt[:, :HEADS]
        rate_sum = rate_sum + rate * jnp.sum(dt * suffix, axis=0, keepdims=True)
        skip_sum = skip_sum + jnp.sum(kx, axis=0, keepdims=True)
        sd = jnp.sum(dt * kx, axis=1, keepdims=True)
        dsk = jnp.where(row < col, ds_ref[k], 0.0)
        bk, ck = b_ref[rows, :], c_ref[rows, :]
        sh, sl = split2(dsk)
        db = dot(sh, ck) + dot(sl, ck) + sd * ck.astype(F32)
        sh, sl = split2(dsk.T)
        dc = dot(sh, bk) + dot(sl, bk) + sd * bk.astype(F32)
        if k == 0:
            oh, ol = split2(dst)
            db = db + dot(oh, c_ref[SPAN:, :]) + dot(ol, c_ref[SPAN:, :])
        else:
            oh, ol = split2(dst.T)
            dc = dc + dot(oh, b_ref[:SPAN, :]) + dot(ol, b_ref[:SPAN, :])
        db_ref[rows, :] = db.astype(BF16)
        dc_ref[rows, :] = dc.astype(BF16)
        dx_ref[rows, :] = (dxs + coef_ref[rows, :] * dy).astype(BF16)

    dg = jnp.sum(dg_ref[...], axis=0, keepdims=True)
    for j in range(8):
        small_ref[j:j + 1, :] = dg[:, j * 128:(j + 1) * 128]
    small_ref[8:9, :] = rate_sum
    small_ref[9:10, :] = skip_sum
    small_ref[10:16, :] = jnp.zeros((6, 128), F32)


def scan_forward(x, z, b, c, dt, rate, skip, gain):
    return pl.pallas_call(
        fwd_kernel,
        out_shape=(jax.ShapeDtypeStruct((TOK, CH), F32), jax.ShapeDtypeStruct((TOK, CH), BF16)),
        scratch_shapes=[
            pltpu.VMEM((TOK, 128), F32),
            pltpu.VMEM((8, 128), F32),
            pltpu.VMEM((TOK, HEADS * HALF), F32),
            pltpu.VMEM((2, 128, SPAN), F32),
            pltpu.VMEM((2, SPAN, SPAN), F32),
            pltpu.VMEM((TOK, CH), F32),
        ],
        compiler_params=pltpu.CompilerParams(vmem_limit_bytes=VMEM_LIMIT),
        cost_estimate=pl.CostEstimate(flops=3_000_000_000, bytes_accessed=8_000_000, transcendentals=3_000_000),
        name="scan_forward",
    )(x, z, b, c, dt, rate, skip, gain)


def scan_backward(u, ys, x, z, b, c, dt, rate, skip, gain):
    return pl.pallas_call(
        bwd_kernel,
        out_shape=(
            jax.ShapeDtypeStruct((TOK, CH), BF16),
            jax.ShapeDtypeStruct((TOK, CH), BF16),
            jax.ShapeDtypeStruct((TOK, 128), BF16),
            jax.ShapeDtypeStruct((TOK, 128), BF16),
            jax.ShapeDtypeStruct((TOK, HEADS), F32),
            jax.ShapeDtypeStruct((16, 128), F32),
        ),
        scratch_shapes=[
            pltpu.VMEM((TOK, 128), F32),
            pltpu.VMEM((8, 128), F32),
            pltpu.VMEM((TOK, HEADS * HALF), F32),
            pltpu.VMEM((2, 128, SPAN), F32),
            pltpu.VMEM((2, SPAN, SPAN), F32),
            pltpu.VMEM((TOK, CH), F32),
            pltpu.VMEM((TOK, CH), F32),
            pltpu.VMEM((TOK, CH), F32),
            pltpu.VMEM((2, SPAN, SPAN), F32),
            pltpu.VMEM((8, CH), F32),
        ],
        compiler_params=pltpu.CompilerParams(vmem_limit_bytes=VMEM_LIMIT),
        cost_estimate=pl.CostEstimate(flops=10_000_000_000, bytes_accessed=12_000_000, transcendentals=3_000_000),
        name="scan_backward",
    )(u, ys, x, z, b, c, dt, rate, skip, gain)


AXES = {"z": 8, "xl": 2, "c": 2, "y": 4, "xh": 2}
DP = ("z", "xl", "c")
TP = ("y", "xh")


def send(v, axis, shift):
    n = AXES[axis]
    return lax.ppermute(v, axis, [(i, (i + shift) % n) for i in range(n)])


def both_ways(up, down, axis):
    return send(up, axis, 1), send(down, axis, -1)


def tie(values, *first):
    got = lax.optimization_barrier((tuple(values),) + tuple(first))
    return got[0]


def own_first(rows, core):
    blocks = rows.reshape(rows.shape[0], 16, 2, 128)
    even, odd = (blocks[:, :, k].reshape(rows.shape[0], 2048) for k in range(2))
    first = jnp.where(core == 0, even, odd)
    second = jnp.where(core == 0, odd, even)
    return jnp.concatenate([first, second], axis=1)


def on_device(grad_out, x, z, b, c, dt, rate, skip, gain, w_out):
    contract = (((0,), (0,)), ((), ()))
    zi, xl, core, yi, xh = (lax.axis_index(a) for a in ("z", "xl", "c", "y", "xh"))
    scan = (x, z, b.reshape(TOK, 128), c.reshape(TOK, 128), dt, rate[None], skip[None], gain[None])

    w_other = send(w_out, "xl", 1)
    own = own_first(grad_out, core)
    below, above = both_ways(own, own, "y")
    other = send(own, "xh", 1)
    ys, normed = scan_forward(*scan)
    (below, above, other, w_other), normed = tie(((below, above, other, w_other), normed), normed)
    w_pair = jnp.concatenate([jnp.where(xl == 0, w_out, w_other), jnp.where(xl == 0, w_other, w_out)], axis=0)

    normed_other = send(normed, "c", 1)
    below2, above2 = both_ways(jnp.concatenate([other, below[:32]], axis=0),
                               jnp.concatenate([other, above[32:]], axis=0), "y")
    wb, wa = both_ways(w_pair, w_pair, "z")
    below2, above2, wb, wa = tie((below2, above2, wb, wa), normed_other)

    far_b, far_a = both_ways(below2[:32], above2[32:64], "y")
    wb2, wa2 = both_ways(wb, wa, "z")

    def placed(first, second):
        return jnp.concatenate([jnp.where(xh == 0, first, second), jnp.where(xh == 0, second, first)], axis=0)

    own2 = placed(own, other)
    prev2 = placed(below, below2[:64])
    next2 = placed(above, above2[:64])
    far2 = placed(jnp.concatenate([below2[64:], above2[64:]], axis=0), jnp.concatenate([far_b, far_a], axis=0))
    turn = jnp.concatenate([own2, next2, far2, prev2] * 2, axis=0)
    rows = lax.dynamic_slice_in_dim(turn, ((4 - yi) % 4) * 128, TOK, 0)
    keep, give = rows[:, :2048], rows[:, 2048:]
    rows_other = send(give, "c", 1)
    wb3, wa3 = both_ways(wb2, wa2, "z")
    wfar_b, wfar_a = both_ways(wb3[:128], wa3[128:], "z")

    mine_part = lax.dot_general(keep, normed, contract, preferred_element_type=F32).reshape(8, 256, CH)
    theirs = rows_other.reshape(TOK, 8, 256)

    def mine(shift):
        at = (zi + shift) % 8
        col = lax.dynamic_index_in_dim(theirs, at, 1, keepdims=False)
        term = lax.dot_general(col, normed_other, contract, preferred_element_type=F32)
        return term + lax.dynamic_index_in_dim(mine_part, at, 0, keepdims=False)

    half = CH // 2
    far = mine(4).astype(BF16)
    up, down = both_ways(far[:, half:], far[:, :half], "z")

    w_near = [w_pair, wa, wa2, wa3, jnp.concatenate([wfar_b, wfar_a], axis=0), wb3, wb2, wb]
    w_turn = jnp.concatenate(w_near + w_near, axis=0)
    w_keep = lax.dynamic_slice_in_dim(w_turn, ((8 - zi) % 8) * 256, 2048, 0)
    w_give = send(w_keep, "c", 1)

    v = mine(3)
    up = jnp.concatenate([v[:, :half], v[:, half:] + up.astype(F32)], axis=1).astype(BF16)
    v = mine(-3)
    down = jnp.concatenate([v[:, :half] + down.astype(F32), v[:, half:]], axis=1).astype(BF16)
    up, down = both_ways(up, down, "z")

    upstream = jnp.dot(keep, w_keep, preferred_element_type=F32) + jnp.dot(give, w_give, preferred_element_type=F32)
    up, down = tie((up, down), upstream)

    up, down = both_ways((mine(2) + up.astype(F32)).astype(BF16), (mine(-2) + down.astype(F32)).astype(BF16), "z")
    dx, dz, db, dc, ddt, small = scan_backward(upstream, ys, *scan)
    up, down, small = tie((up, down, small), dx)

    up, down = both_ways((mine(1) + up.astype(F32)).astype(BF16), (mine(-1) + down.astype(F32)).astype(BF16), "z")
    small = small + send(small, "c", 1)
    small = small + send(small, "xl", 1)
    up, down, small = tie((up, down, small))
    total = (mine(0) + (up.astype(F32) + down.astype(F32))).reshape(2, 128, CH)
    stay = lax.dynamic_index_in_dim(total, xl, 0, keepdims=False)
    leave = lax.dynamic_index_in_dim(total, 1 - xl, 0, keepdims=False)
    grad_weight = stay + send(leave, "xl", 1)
    small = lax.psum(small, "z")
    return (dx, dz, db[:, None], dc[:, None], ddt, small[8, :HEADS], small[9, :HEADS],
            small[:8].reshape(CH), grad_weight)


def solution(mesh):
    fine = jax.sharding.Mesh(mesh.devices.reshape(tuple(AXES.values())), tuple(AXES))
    part = P(DP, TP)
    part3 = P(DP, TP, None)
    head = P(TP)
    return jax.shard_map(
        on_device,
        mesh=fine,
        in_specs=(P(DP + TP, None), part, part, part3, part3, part, head, head, head, part),
        out_specs=(part, part, part3, part3, part, head, head, head, part),
        check_vma=False,
    )
```

```python
import math

import jax
import jax.numpy as jnp
from jax import lax
from jax.experimental import pallas as pl
from jax.experimental.pallas import tpu as pltpu
from jax.sharding import PartitionSpec as P

F32, BF16 = jnp.float32, jnp.bfloat16
HEADS = 16
SPAN = 256
TOK = 512
CH = 1024
HALF = 128
LOG2E = 1.4426950408889634
BIG = 126.0
VMEM_LIMIT = 48 * 1024 * 1024


def dot(a, b):
    return jnp.dot(a, b, preferred_element_type=F32)


def dot_nt(a, b):
    return lax.dot_general(a, b, (((1,), (1,)), ((), ())), preferred_element_type=F32)


def split2(v):
    hi = v.astype(BF16)
    return hi, (v - hi.astype(F32)).astype(BF16)


def dot3(a, b, fn):
    ah, al = split2(a)
    bh, bl = split2(b)
    return fn(ah, bh) + (fn(ah, bl) + fn(al, bh))


def spread_matrix(width):
    row = lax.broadcasted_iota(jnp.int32, (128, HEADS * width), 0)
    col = lax.broadcasted_iota(jnp.int32, (128, HEADS * width), 1)
    return jnp.where((row < 48) & ((row & 15) == col // width), 1.0, 0.0).astype(BF16)


def parts3(v):
    lane = lax.broadcasted_iota(jnp.int32, v.shape, 1)
    v = jnp.where(lane < HEADS, v, 0.0)
    one = v.astype(BF16).astype(F32)
    rest = v - one
    two = rest.astype(BF16).astype(F32)
    three = rest - two
    return (one + pltpu.roll(two, 16, 1) + pltpu.roll(three, 32, 1)).astype(BF16)


def cumulate(tri, v):
    one = v.astype(BF16)
    rest = v - one.astype(F32)
    two = rest.astype(BF16)
    three = (rest - two.astype(F32)).astype(BF16)
    return dot(tri, one) + (dot(tri, two) + dot(tri, three))


def triangle(n, lower):
    row = lax.broadcasted_iota(jnp.int32, (n, n), 0)
    col = lax.broadcasted_iota(jnp.int32, (n, n), 1)
    return jnp.where(row >= col if lower else row <= col, 1.0, 0.0).astype(BF16)


def prepare(dt_ref, rate_ref, pad_ref, ratepad_ref):
    pad_ref[...] = jnp.ones((TOK, 128), F32)
    pad_ref[:, :HEADS] = dt_ref[...]
    ratepad_ref[...] = jnp.zeros((8, 128), F32)
    ratepad_ref[0:1, :HEADS] = rate_ref[...]
    rate = -jnp.exp(ratepad_ref[0:1, :])
    tri = triangle(SPAN, True)
    cums, rs = [], []
    for k in range(2):
        dt = pad_ref[k * SPAN:(k + 1) * SPAN, :]
        cum = cumulate(tri, dt * (rate * LOG2E))
        cums.append(cum)
        rs.append(jnp.log2(dt) - cum)
    return rate, cums, rs


def fwd_kernel(x_ref, z_ref, b_ref, c_ref, dt_ref, rate_ref, skip_ref, gain_ref,
               ys_ref, n_ref, pad_ref, ratepad_ref, cexp_ref, rt_ref, s_ref, coef_ref):
    rate, cums, rs = prepare(dt_ref, rate_ref, pad_ref, ratepad_ref)
    wide = spread_matrix(HALF)
    narrow = spread_matrix(64)
    row = lax.broadcasted_iota(jnp.int32, (SPAN, SPAN), 0)
    col = lax.broadcasted_iota(jnp.int32, (SPAN, SPAN), 1)
    ratepad_ref[0:1, :HEADS] = skip_ref[...]
    skip = ratepad_ref[0:1, :]
    for k in range(2):
        rows = slice(k * SPAN, (k + 1) * SPAN)
        cexp_ref[rows, :] = dot(parts3(cums[k]), wide)
        rt_ref[k] = rs[k].T
        bk, ck = b_ref[rows, :], c_ref[rows, :]
        s_ref[k] = jnp.where(row > col, dot_nt(ck, bk), 0.0)
        diag = jnp.sum(bk.astype(F32) * ck.astype(F32), axis=1, keepdims=True)
        coef_ref[rows, :] = dot(parts3(diag * pad_ref[rows, :] + skip), narrow)
    lane = lax.broadcasted_iota(jnp.int32, (SPAN, 128), 1)

    def pair(hp, _):
        cols = pl.ds(pl.multiple_of(hp * 128, 128), 128)
        for k in range(2):
            rows = slice(k * SPAN, (k + 1) * SPAN)
            xp = x_ref[rows, cols]
            tops, bots = [], []
            for half in range(2):
                h = hp * 2 + half
                rrow = rt_ref[k, pl.ds(h, 1), :]
                hcols = pl.ds(pl.multiple_of(h * 128, 128), 128)
                top = cexp_ref[k * SPAN:k * SPAN + HALF, hcols]
                bot = cexp_ref[k * SPAN + HALF:(k + 1) * SPAN, hcols]
                wt = s_ref[k, :HALF, :HALF] * jnp.exp2(jnp.minimum(top + rrow[:, :HALF], BIG))
                wb = s_ref[k, HALF:, :] * jnp.exp2(
                    jnp.minimum(jnp.concatenate([bot, bot], axis=1) + rrow, BIG))
                tops += split2(wt)
                bots += split2(wb)
            yt = dot(jnp.concatenate(tops, axis=0), xp[:HALF])
            yb = dot(jnp.concatenate(bots, axis=0), xp)
            ys = [jnp.concatenate([v[256 * h:256 * h + 128] + v[256 * h + 128:256 * h + 256] for v in (yt, yb)], axis=0)
                  for h in range(2)]
            ys_ref[rows, cols] = jnp.where(lane < 64, ys[0], ys[1])
        return 0

    lax.fori_loop(0, 8, pair, 0)

    s10 = dot_nt(c_ref[SPAN:, :], b_ref[:SPAN, :])
    qdt = parts3(jnp.exp2(cums[0][SPAN - 1:SPAN, :] + rs[0]))
    p = parts3(jnp.exp2(cums[1]))
    for j in range(4):
        cols = slice(j * 256, (j + 1) * 256)
        xq = dot(qdt, narrow[:, cols]) * x_ref[:SPAN, cols].astype(F32)
        ys_ref[SPAN:, cols] += dot(p, narrow[:, cols]) * dot3(s10, xq, dot)

    gain = gain_ref[...]

    def norm(i, _):
        rows = pl.ds(pl.multiple_of(i * 32, 32), 32)
        z = z_ref[rows, :].astype(F32)
        y = ys_ref[rows, :] + coef_ref[rows, :] * x_ref[rows, :].astype(F32)
        gated = y * (z / (1.0 + jnp.exp(-z)))
        inv = lax.rsqrt(jnp.mean(gated * gated, axis=1, keepdims=True) + 1e-05)
        n_ref[rows, :] = (gated * inv * gain).astype(BF16)
        return 0

    lax.fori_loop(0, TOK // 32, norm, 0)


def bwd_kernel(u_ref, ys_ref, x_ref, z_ref, b_ref, c_ref, dt_ref, rate_ref, skip_ref, gain_ref,
               dx_ref, dz_ref, db_ref, dc_ref, ddt_ref, small_ref,
               pad_ref, ratepad_ref, rexp_ref, ct_ref, s_ref, coef_ref, dy_ref, dxs_ref, ds_ref, dg_ref):
    rate, cums, rs = prepare(dt_ref, rate_ref, pad_ref, ratepad_ref)
    wide = spread_matrix(HALF)
    narrow = spread_matrix(64)
    row = lax.broadcasted_iota(jnp.int32, (SPAN, SPAN), 0)
    col = lax.broadcasted_iota(jnp.int32, (SPAN, SPAN), 1)
    ratepad_ref[0:1, :HEADS] = skip_ref[...]
    skip = ratepad_ref[0:1, :]
    diags = []
    for k in range(2):
        rows = slice(k * SPAN, (k + 1) * SPAN)
        rexp_ref[rows, :] = dot(parts3(rs[k]), wide)
        ct_ref[k] = cums[k].T
        bk, ck = b_ref[rows, :], c_ref[rows, :]
        s_ref[k] = jnp.where(row < col, dot_nt(bk, ck), 0.0)
        diag = jnp.sum(bk.astype(F32) * ck.astype(F32), axis=1, keepdims=True)
        diags.append(diag)
        coef_ref[rows, :] = dot(parts3(diag * pad_ref[rows, :] + skip), narrow)

    gain = gain_ref[...]
    dg_ref[...] = jnp.zeros((8, CH), F32)

    def gate(i, _):
        rows = pl.ds(pl.multiple_of(i * 32, 32), 32)
        z = z_ref[rows, :].astype(F32)
        y = ys_ref[rows, :] + coef_ref[rows, :] * x_ref[rows, :].astype(F32)
        sig = 1.0 / (1.0 + jnp.exp(-z))
        sz = z * sig
        gated = y * sz
        inv = lax.rsqrt(jnp.mean(gated * gated, axis=1, keepdims=True) + 1e-05)
        unit = gated * inv
        u = u_ref[rows, :]
        ug = u * unit
        dg_ref[...] += (ug[0:8] + ug[8:16]) + (ug[16:24] + ug[24:32])
        v = u * gain
        dgated = inv * (v - unit * jnp.mean(v * unit, axis=1, keepdims=True))
        dy_ref[rows, :] = dgated * sz
        dz_ref[rows, :] = (dgated * y * (sig * (1.0 + z * (1.0 - sig)))).astype(BF16)
        return 0

    lax.fori_loop(0, TOK // 32, gate, 0)

    ds_ref[...] = jnp.zeros((2, SPAN, SPAN), F32)
    lane = lax.broadcasted_iota(jnp.int32, (SPAN, 128), 1)

    def pair(hp, _):
        cols = pl.ds(pl.multiple_of(hp * 128, 128), 128)
        for k in range(2):
            rows = slice(k * SPAN, (k + 1) * SPAN)
            xp = x_ref[rows, cols].astype(F32)
            dh, dl = split2(dy_ref[rows, cols])
            dhl = jnp.concatenate([dh, dl], axis=1)
            xx = []
            for half in range(2):
                xm = jnp.where((lane < 64) if half == 0 else (lane >= 64), xp, 0.0).astype(BF16)
                xx.append(jnp.concatenate([xm, xm], axis=1))
            gts = dot_nt(jnp.concatenate([v[:HALF] for v in xx], axis=0), dhl)
            gbs = dot_nt(jnp.concatenate([v[HALF:] for v in xx], axis=0), dhl[HALF:])
            ths, tls, bhs, bls = [], [], [], []
            dst, dsb = ds_ref[k, :HALF, :], ds_ref[k, HALF:, HALF:]
            for half in range(2):
                h = hp * 2 + half
                part = slice(half * HALF, (half + 1) * HALF)
                crow = ct_ref[k, pl.ds(h, 1), :]
                hcols = pl.ds(pl.multiple_of(h * 128, 128), 128)
                top = rexp_ref[k * SPAN:k * SPAN + HALF, hcols]
                bot = rexp_ref[k * SPAN + HALF:(k + 1) * SPAN, hcols]
                et = jnp.exp2(jnp.minimum(jnp.concatenate([top, top], axis=1) + crow, BIG))
                eb = jnp.exp2(jnp.minimum(bot + crow[:, HALF:], BIG))
                dst = dst + et * gts[part]
                dsb = dsb + eb * gbs[part]
                hi, lo = split2(s_ref[k, :HALF, :] * et)
                ths.append(hi)
                tls.append(lo)
                hi, lo = split2(s_ref[k, HALF:, HALF:] * eb)
                bhs.append(hi)
                bls.append(lo)
            ds_ref[k, :HALF, :] = dst
            ds_ref[k, HALF:, HALF:] = dsb
            ot = dot(jnp.concatenate(ths, axis=0), dhl)
            ob = dot(jnp.concatenate(bhs, axis=0), dhl[HALF:])
            ot = (ot[:, :128] + ot[:, 128:]) + dot(jnp.concatenate(tls, axis=0), dh)
            ob = (ob[:, :128] + ob[:, 128:]) + dot(jnp.concatenate(bls, axis=0), dh[HALF:])
            outs = [jnp.concatenate([v[h * HALF:(h + 1) * HALF] for v in (ot, ob)], axis=0) for h in range(2)]
            dxs_ref[rows, cols] = jnp.where(lane < 64, outs[0], outs[1])
        return 0

    lax.fori_loop(0, 8, pair, 0)

    st = dot_nt(b_ref[:SPAN, :], c_ref[SPAN:, :])
    qdt = parts3(jnp.exp2(cums[0][SPAN - 1:SPAN, :] + rs[0]))
    p = parts3(jnp.exp2(cums[1]))
    dst = jnp.zeros((SPAN, SPAN), F32)
    for j in range(4):
        cols = slice(j * 256, (j + 1) * 256)
        qx = dot(qdt, narrow[:, cols])
        xq = qx * x_ref[:SPAN, cols].astype(F32)
        pdy = dot(p, narrow[:, cols]) * dy_ref[SPAN:, cols]
        dxs_ref[:SPAN, cols] += qx * dot3(st, pdy, dot)
        dst = dst + dot3(xq, pdy, dot_nt)

    seg_row = lax.broadcasted_iota(jnp.int32, (CH, 128), 0)
    seg_col = lax.broadcasted_iota(jnp.int32, (CH, 128), 1)
    seg = jnp.where(seg_row // 64 == seg_col, 1.0, 0.0).astype(BF16)

    def heads_sum(v):
        hi, lo = split2(v)
        return dot(hi, seg) + dot(lo, seg)

    tri = triangle(SPAN, False)
    later = jnp.zeros((1, 128), F32)
    rate_sum = jnp.zeros((1, 128), F32)
    skip_sum = jnp.zeros((1, 128), F32)
    for k in (1, 0):
        rows = slice(k * SPAN, (k + 1) * SPAN)
        xf = x_ref[rows, :].astype(F32)
        dy = dy_ref[rows, :]
        dxs = dxs_ref[rows, :]
        kx = heads_sum(dy * xf)
        r = heads_sum(dy * ys_ref[rows, :])
        q = heads_sum(xf * dxs)
        suffix = cumulate(tri, r - q) + later
        later = suffix[0:1, :]
        dt = pad_ref[rows, :]
        ddt = q / dt + kx * diags[k] + rate * suffix
        ddt_ref[rows, :] = ddt[:, :HEADS]
        rate_sum = rate_sum + rate * jnp.sum(dt * suffix, axis=0, keepdims=True)
        skip_sum = skip_sum + jnp.sum(kx, axis=0, keepdims=True)
        sd = jnp.sum(dt * kx, axis=1, keepdims=True)
        dsk = jnp.where(row < col, ds_ref[k], 0.0)
        bk, ck = b_ref[rows, :], c_ref[rows, :]
        sh, sl = split2(dsk)
        db = dot(sh, ck) + dot(sl, ck) + sd * ck.astype(F32)
        sh, sl = split2(dsk.T)
        dc = dot(sh, bk) + dot(sl, bk) + sd * bk.astype(F32)
        if k == 0:
            oh, ol = split2(dst)
            db = db + dot(oh, c_ref[SPAN:, :]) + dot(ol, c_ref[SPAN:, :])
        else:
            oh, ol = split2(dst.T)
            dc = dc + dot(oh, b_ref[:SPAN, :]) + dot(ol, b_ref[:SPAN, :])
        db_ref[rows, :] = db.astype(BF16)
        dc_ref[rows, :] = dc.astype(BF16)
        dx_ref[rows, :] = (dxs + coef_ref[rows, :] * dy).astype(BF16)

    dg = jnp.sum(dg_ref[...], axis=0, keepdims=True)
    for j in range(8):
        small_ref[j:j + 1, :] = dg[:, j * 128:(j + 1) * 128]
    small_ref[8:9, :] = rate_sum
    small_ref[9:10, :] = skip_sum
    small_ref[10:16, :] = jnp.zeros((6, 128), F32)


def scan_forward(x, z, b, c, dt, rate, skip, gain):
    return pl.pallas_call(
        fwd_kernel,
        out_shape=(jax.ShapeDtypeStruct((TOK, CH), F32), jax.ShapeDtypeStruct((TOK, CH), BF16)),
        scratch_shapes=[
            pltpu.VMEM((TOK, 128), F32),
            pltpu.VMEM((8, 128), F32),
            pltpu.VMEM((TOK, HEADS * HALF), F32),
            pltpu.VMEM((2, 128, SPAN), F32),
            pltpu.VMEM((2, SPAN, SPAN), F32),
            pltpu.VMEM((TOK, CH), F32),
        ],
        compiler_params=pltpu.CompilerParams(vmem_limit_bytes=VMEM_LIMIT),
        cost_estimate=pl.CostEstimate(flops=3_000_000_000, bytes_accessed=8_000_000, transcendentals=3_000_000),
        name="scan_forward",
    )(x, z, b, c, dt, rate, skip, gain)


def scan_backward(u, ys, x, z, b, c, dt, rate, skip, gain):
    return pl.pallas_call(
        bwd_kernel,
        out_shape=(
            jax.ShapeDtypeStruct((TOK, CH), BF16),
            jax.ShapeDtypeStruct((TOK, CH), BF16),
            jax.ShapeDtypeStruct((TOK, 128), BF16),
            jax.ShapeDtypeStruct((TOK, 128), BF16),
            jax.ShapeDtypeStruct((TOK, HEADS), F32),
            jax.ShapeDtypeStruct((16, 128), F32),
        ),
        scratch_shapes=[
            pltpu.VMEM((TOK, 128), F32),
            pltpu.VMEM((8, 128), F32),
            pltpu.VMEM((TOK, HEADS * HALF), F32),
            pltpu.VMEM((2, 128, SPAN), F32),
            pltpu.VMEM((2, SPAN, SPAN), F32),
            pltpu.VMEM((TOK, CH), F32),
            pltpu.VMEM((TOK, CH), F32),
            pltpu.VMEM((TOK, CH), F32),
            pltpu.VMEM((2, SPAN, SPAN), F32),
            pltpu.VMEM((8, CH), F32),
        ],
        compiler_params=pltpu.CompilerParams(vmem_limit_bytes=VMEM_LIMIT),
        cost_estimate=pl.CostEstimate(flops=10_000_000_000, bytes_accessed=12_000_000, transcendentals=3_000_000),
        name="scan_backward",
    )(u, ys, x, z, b, c, dt, rate, skip, gain)


AXES = {"z": 8, "xl": 2, "c": 2, "y": 4, "xh": 2}
DP = ("z", "xl", "c")
TP = ("y", "xh")


def send(v, axis, shift):
    n = AXES[axis]
    return lax.ppermute(v, axis, [(i, (i + shift) % n) for i in range(n)])


def swap(v, axis, mask):
    return lax.ppermute(v, axis, [(i, i ^ mask) for i in range(AXES[axis])])


def both_ways(up, down, axis):
    return send(up, axis, 1), send(down, axis, -1)


def tie(values, *first):
    return lax.optimization_barrier((tuple(values),) + tuple(first))[0]


def shuffle(name, shapes, plan, scalars, *arrays):
    count = len(plan([0] * len(scalars)))

    def kernel(s_ref, *refs):
        src, dst, sem = refs[:len(arrays)], refs[len(arrays):-1], refs[-1]
        copies = [
            pltpu.make_async_copy(src[i].at[a], dst[o].at[b], sem.at[k])
            for k, (i, a, o, b) in enumerate(plan([s_ref[j] for j in range(len(scalars))]))
        ]
        for copy in copies:
            copy.start()
        for copy in copies:
            copy.wait()

    size = sum(math.prod(s) for s in shapes) * 2
    return pl.pallas_call(
        kernel,
        out_shape=tuple(jax.ShapeDtypeStruct(s, BF16) for s in shapes),
        in_specs=[pl.BlockSpec(memory_space=pltpu.SMEM)] + [pl.BlockSpec(memory_space=pl.ANY)] * len(arrays),
        out_specs=tuple(pl.BlockSpec(memory_space=pl.ANY) for _ in shapes),
        scratch_shapes=[pltpu.SemaphoreType.DMA((count,))],
        cost_estimate=pl.CostEstimate(flops=0, bytes_accessed=2 * size, transcendentals=0),
        name=name,
    )(jnp.stack([s.astype(jnp.int32) for s in scalars]), *arrays)


def own_first(rows, core):
    def kernel(core_ref, in_ref, out_ref):
        for j in range(16):
            even = in_ref[:, 256 * j:256 * j + 128]
            odd = in_ref[:, 256 * j + 128:256 * j + 256]
            first = core_ref[0] == 0
            out_ref[:, 128 * j:128 * j + 128] = jnp.where(first, even, odd)
            out_ref[:, 2048 + 128 * j:2048 + 128 * j + 128] = jnp.where(first, odd, even)

    return pl.pallas_call(
        kernel,
        out_shape=jax.ShapeDtypeStruct(rows.shape, rows.dtype),
        in_specs=[pl.BlockSpec(memory_space=pltpu.SMEM), pl.BlockSpec(memory_space=pltpu.VMEM)],
        out_specs=pl.BlockSpec(memory_space=pltpu.VMEM),
        name="own_first",
    )(core.astype(jnp.int32).reshape(1), rows)


def at_rows(start, size):
    return (pl.ds(pl.multiple_of(start, 32), size), slice(None)) if not isinstance(start, int) else (slice(start, start + size), slice(None))


def place_tokens(yi, xh, *pieces):
    sizes = (64, 64, 64, 64, 64, 64, 64, 32, 32)
    turns = (0, 0, 3, 3, 1, 1, 2, 2, 2)
    other = (0, 1, 0, 1, 0, 1, 0, 1, 1)

    def plan(s):
        moves = []
        for i in range(9):
            start = ((s[0] + turns[i]) % 4) * 128 + (1 - s[1] if other[i] else s[1]) * 64 + (32 if i == 8 else 0)
            for o in range(2):
                moves.append((i, (slice(None), slice(2048 * o, 2048 * o + 2048)), o, at_rows(start, sizes[i])))
        return moves

    return shuffle("place_tokens", [(TOK, 2048)] * 2, plan, (yi, xh), *pieces)


def place_pair(xl, first, other):
    def plan(s):
        return [(0, at_rows(0, 128), 0, at_rows(s[0] * 128, 128)), (1, at_rows(0, 128), 0, at_rows((1 - s[0]) * 128, 128))]

    return shuffle("place_pair", [(256, CH)], plan, (xl,), first, other)[0]


def place_weights(zi, *pieces):
    turns = (0, 1, 2, 3, 7, 6, 5, 4, 4)

    def plan(s):
        moves = []
        for i in range(9):
            size = 256 if i < 7 else 128
            start = ((s[0] + turns[i]) % 8) * 256 + (128 if i == 8 else 0)
            moves.append((i, at_rows(0, size), 0, at_rows(start, size)))
        return moves

    return shuffle("place_weights", [(2048, CH)], plan, (zi,), *pieces)[0]


def on_device(grad_out, x, z, b, c, dt, rate, skip, gain, w_out):
    contract = (((0,), (0,)), ((), ()))
    zi, xl, core, yi, xh = (lax.axis_index(a) for a in ("z", "xl", "c", "y", "xh"))
    scan = (x, z, b.reshape(TOK, 128), c.reshape(TOK, 128), dt, rate[None], skip[None], gain[None])

    w_other = send(w_out, "xl", 1)
    own = own_first(grad_out, core)
    below, above = both_ways(own, own, "y")
    other = send(own, "xh", 1)
    w_pair = place_pair(xl, w_out, w_other)
    wb, wa = both_ways(w_pair, w_pair, "z")
    below, above, other, wb, wa = tie((below, above, other, wb, wa), w_pair)

    b_other = send(other, "y", 1)
    far_own = send(above, "y", -1)
    a_other = send(above, "xh", 1)
    late, = tie((scan[6],), below, above, other)
    ys, normed = scan_forward(*scan[:6], late, scan[7])
    b_other, far_own, a_other, wb, wa = tie((b_other, far_own, a_other, wb, wa), normed)

    far_b, far_a = both_ways(b_other[:32], a_other[32:], "y")
    normed_other = send(normed, "c", 1)
    wb2, wa2 = both_ways(wb, wa, "z")
    far_b, far_a = tie((far_b, far_a), normed_other)
    keep, give = place_tokens(yi, xh, own, other, below, b_other, above, a_other, far_own, far_b, far_a)
    theirs = send(give, "c", 1)
    wb2, wa2 = tie((wb2, wa2), keep)
    wb3, wa3 = both_ways(wb2, wa2, "z")

    def mine(shift):
        at = ((zi + shift) % 8) * 256
        terms = [
            lax.dot_general(lax.dynamic_slice_in_dim(r, at, 256, 1), n, contract, preferred_element_type=F32)
            for r, n in ((keep, normed), (theirs, normed_other))
        ]
        return terms[0] + terms[1]

    half = CH // 2
    far = mine(4).astype(BF16)
    up, down = both_ways(far[:, half:], far[:, :half], "z")
    wb3, wa3 = tie((wb3, wa3), far)
    wfar_b, wfar_a = both_ways(wb3[:128], wa3[128:], "z")

    v = mine(3)
    up = jnp.concatenate([v[:, :half], v[:, half:] + up.astype(F32)], axis=1).astype(BF16)
    v = mine(-3)
    down = jnp.concatenate([v[:, :half] + down.astype(F32), v[:, half:]], axis=1).astype(BF16)
    wfar_b, wfar_a = tie((wfar_b, wfar_a), up, down)
    up, down = both_ways(up, down, "z")

    w_keep = place_weights(zi, w_pair, wa, wa2, wa3, wb, wb2, wb3, wfar_b, wfar_a)
    w_give = send(w_keep, "c", 1)
    upstream = jnp.dot(keep, w_keep, preferred_element_type=F32) + jnp.dot(give, w_give, preferred_element_type=F32)
    up, down = tie((up, down), upstream)

    up, down = both_ways((mine(2) + up.astype(F32)).astype(BF16), (mine(-2) + down.astype(F32)).astype(BF16), "z")
    dx, dz, db, dc, ddt, small = scan_backward(upstream, ys, *scan)
    up, down, small = tie((up, down, small), dx)

    up, down = both_ways((mine(1) + up.astype(F32)).astype(BF16), (mine(-1) + down.astype(F32)).astype(BF16), "z")
    small = small + send(small, "c", 1)
    small = small + send(small, "xl", 1)
    up, down, small = tie((up, down, small))
    total = (mine(0) + (up.astype(F32) + down.astype(F32))).reshape(2, 128, CH)
    stay = lax.dynamic_index_in_dim(total, xl, 0, keepdims=False)
    leave = lax.dynamic_index_in_dim(total, 1 - xl, 0, keepdims=False)
    small, leave = tie((small, leave))
    arrived = send(leave, "xl", 1)
    for mask in (1, 2, 4):
        small = small + swap(small, "z", mask)
    arrived, = tie((arrived,), small)
    grad_weight = stay + arrived
    return (dx, dz, db[:, None], dc[:, None], ddt, small[8, :HEADS], small[9, :HEADS],
            small[:8].reshape(CH), grad_weight)


def solution(mesh):
    fine = jax.sharding.Mesh(mesh.devices.reshape(tuple(AXES.values())), tuple(AXES))
    part = P(DP, TP)
    part3 = P(DP, TP, None)
    head = P(TP)
    return jax.shard_map(
        on_device,
        mesh=fine,
        in_specs=(P(DP + TP, None), part, part, part3, part3, part, head, head, head, part),
        out_specs=(part, part, part3, part3, part, head, head, head, part),
        check_vma=False,
    )
```

```python
import jax
import jax.numpy as jnp
from jax import lax
from jax.experimental import pallas as pl
from jax.experimental.pallas import tpu as pltpu
from jax.sharding import PartitionSpec as P

F32, BF16 = jnp.float32, jnp.bfloat16
HEADS = 16
SPAN = 256
TOK = 512
CH = 1024
HALF = 128
LOG2E = 1.4426950408889634
BIG = 126.0
VMEM_LIMIT = 48 * 1024 * 1024
SMALL = pl.CostEstimate(flops=1000, bytes_accessed=1000, transcendentals=0)


def dot(a, b):
    return jnp.dot(a, b, preferred_element_type=F32)


def dot_nt(a, b):
    return lax.dot_general(a, b, (((1,), (1,)), ((), ())), preferred_element_type=F32)


def split2(v):
    hi = v.astype(BF16)
    return hi, (v - hi.astype(F32)).astype(BF16)


def dot3(a, b, fn):
    ah, al = split2(a)
    bh, bl = split2(b)
    return fn(ah, bh) + (fn(ah, bl) + fn(al, bh))


def spread_matrix(width):
    row = lax.broadcasted_iota(jnp.int32, (128, HEADS * width), 0)
    col = lax.broadcasted_iota(jnp.int32, (128, HEADS * width), 1)
    return jnp.where((row < 48) & ((row & 15) == col // width), 1.0, 0.0).astype(BF16)


def parts3(v):
    lane = lax.broadcasted_iota(jnp.int32, v.shape, 1)
    v = jnp.where(lane < HEADS, v, 0.0)
    one = v.astype(BF16).astype(F32)
    rest = v - one
    two = rest.astype(BF16).astype(F32)
    three = rest - two
    return (one + pltpu.roll(two, 16, 1) + pltpu.roll(three, 32, 1)).astype(BF16)


def cumulate(tri, v):
    one = v.astype(BF16)
    rest = v - one.astype(F32)
    two = rest.astype(BF16)
    three = (rest - two.astype(F32)).astype(BF16)
    return dot(tri, one) + (dot(tri, two) + dot(tri, three))


def triangle(n, lower):
    row = lax.broadcasted_iota(jnp.int32, (n, n), 0)
    col = lax.broadcasted_iota(jnp.int32, (n, n), 1)
    return jnp.where(row >= col if lower else row <= col, 1.0, 0.0).astype(BF16)


def prepare(dt_ref, rate_ref, pad_ref, ratepad_ref):
    pad_ref[...] = jnp.ones((TOK, 128), F32)
    pad_ref[:, :HEADS] = dt_ref[...]
    ratepad_ref[...] = jnp.zeros((8, 128), F32)
    ratepad_ref[0:1, :HEADS] = rate_ref[...]
    rate = -jnp.exp(ratepad_ref[0:1, :])
    tri = triangle(SPAN, True)
    cums, rs = [], []
    for k in range(2):
        dt = pad_ref[k * SPAN:(k + 1) * SPAN, :]
        cum = cumulate(tri, dt * (rate * LOG2E))
        cums.append(cum)
        rs.append(jnp.log2(dt) - cum)
    return rate, cums, rs


def fwd_kernel(x_ref, z_ref, b_ref, c_ref, dt_ref, rate_ref, skip_ref, gain_ref,
               ys_ref, n_ref, pad_ref, ratepad_ref, cexp_ref, rt_ref, s_ref, coef_ref):
    rate, cums, rs = prepare(dt_ref, rate_ref, pad_ref, ratepad_ref)
    wide = spread_matrix(HALF)
    narrow = spread_matrix(64)
    row = lax.broadcasted_iota(jnp.int32, (SPAN, SPAN), 0)
    col = lax.broadcasted_iota(jnp.int32, (SPAN, SPAN), 1)
    ratepad_ref[0:1, :HEADS] = skip_ref[...]
    skip = ratepad_ref[0:1, :]
    for k in range(2):
        rows = slice(k * SPAN, (k + 1) * SPAN)
        cexp_ref[rows, :] = dot(parts3(cums[k]), wide)
        rt_ref[k] = rs[k].T
        bk, ck = b_ref[rows, :], c_ref[rows, :]
        s_ref[k] = jnp.where(row > col, dot_nt(ck, bk), 0.0)
        diag = jnp.sum(bk.astype(F32) * ck.astype(F32), axis=1, keepdims=True)
        coef_ref[rows, :] = dot(parts3(diag * pad_ref[rows, :] + skip), narrow)
    lane = lax.broadcasted_iota(jnp.int32, (SPAN, 128), 1)

    def pair(hp, _):
        cols = pl.ds(pl.multiple_of(hp * 128, 128), 128)
        for k in range(2):
            rows = slice(k * SPAN, (k + 1) * SPAN)
            xp = x_ref[rows, cols]
            tops, bots = [], []
            for half in range(2):
                h = hp * 2 + half
                rrow = rt_ref[k, pl.ds(h, 1), :]
                hcols = pl.ds(pl.multiple_of(h * 128, 128), 128)
                top = cexp_ref[k * SPAN:k * SPAN + HALF, hcols]
                bot = cexp_ref[k * SPAN + HALF:(k + 1) * SPAN, hcols]
                wt = s_ref[k, :HALF, :HALF] * jnp.exp2(jnp.minimum(top + rrow[:, :HALF], BIG))
                wb = s_ref[k, HALF:, :] * jnp.exp2(
                    jnp.minimum(jnp.concatenate([bot, bot], axis=1) + rrow, BIG))
                tops += split2(wt)
                bots += split2(wb)
            yt = dot(jnp.concatenate(tops, axis=0), xp[:HALF])
            yb = dot(jnp.concatenate(bots, axis=0), xp)
            ys = [jnp.concatenate([v[256 * h:256 * h + 128] + v[256 * h + 128:256 * h + 256] for v in (yt, yb)], axis=0)
                  for h in range(2)]
            ys_ref[rows, cols] = jnp.where(lane < 64, ys[0], ys[1])
        return 0

    lax.fori_loop(0, 8, pair, 0)

    s10 = dot_nt(c_ref[SPAN:, :], b_ref[:SPAN, :])
    qdt = parts3(jnp.exp2(cums[0][SPAN - 1:SPAN, :] + rs[0]))
    p = parts3(jnp.exp2(cums[1]))
    for j in range(4):
        cols = slice(j * 256, (j + 1) * 256)
        xq = dot(qdt, narrow[:, cols]) * x_ref[:SPAN, cols].astype(F32)
        ys_ref[SPAN:, cols] += dot(p, narrow[:, cols]) * dot3(s10, xq, dot)

    gain = gain_ref[...]

    def norm(i, _):
        rows = pl.ds(pl.multiple_of(i * 32, 32), 32)
        z = z_ref[rows, :].astype(F32)
        y = ys_ref[rows, :] + coef_ref[rows, :] * x_ref[rows, :].astype(F32)
        gated = y * (z / (1.0 + jnp.exp(-z)))
        inv = lax.rsqrt(jnp.mean(gated * gated, axis=1, keepdims=True) + 1e-05)
        n_ref[rows, :] = (gated * inv * gain).astype(BF16)
        return 0

    lax.fori_loop(0, TOK // 32, norm, 0)


def bwd_kernel(u_ref, ys_ref, x_ref, z_ref, b_ref, c_ref, dt_ref, rate_ref, skip_ref, gain_ref,
               dx_ref, dz_ref, db_ref, dc_ref, ddt_ref, small_ref,
               pad_ref, ratepad_ref, rexp_ref, ct_ref, s_ref, coef_ref, dy_ref, dxs_ref, ds_ref, dg_ref):
    rate, cums, rs = prepare(dt_ref, rate_ref, pad_ref, ratepad_ref)
    wide = spread_matrix(HALF)
    narrow = spread_matrix(64)
    row = lax.broadcasted_iota(jnp.int32, (SPAN, SPAN), 0)
    col = lax.broadcasted_iota(jnp.int32, (SPAN, SPAN), 1)
    ratepad_ref[0:1, :HEADS] = skip_ref[...]
    skip = ratepad_ref[0:1, :]
    diags = []
    for k in range(2):
        rows = slice(k * SPAN, (k + 1) * SPAN)
        rexp_ref[rows, :] = dot(parts3(rs[k]), wide)
        ct_ref[k] = cums[k].T
        bk, ck = b_ref[rows, :], c_ref[rows, :]
        s_ref[k] = jnp.where(row < col, dot_nt(bk, ck), 0.0)
        diag = jnp.sum(bk.astype(F32) * ck.astype(F32), axis=1, keepdims=True)
        diags.append(diag)
        coef_ref[rows, :] = dot(parts3(diag * pad_ref[rows, :] + skip), narrow)

    gain = gain_ref[...]
    dg_ref[...] = jnp.zeros((8, CH), F32)

    def gate(i, _):
        rows = pl.ds(pl.multiple_of(i * 32, 32), 32)
        z = z_ref[rows, :].astype(F32)
        y = ys_ref[rows, :] + coef_ref[rows, :] * x_ref[rows, :].astype(F32)
        sig = 1.0 / (1.0 + jnp.exp(-z))
        sz = z * sig
        gated = y * sz
        inv = lax.rsqrt(jnp.mean(gated * gated, axis=1, keepdims=True) + 1e-05)
        unit = gated * inv
        u = u_ref[rows, :]
        ug = u * unit
        dg_ref[...] += (ug[0:8] + ug[8:16]) + (ug[16:24] + ug[24:32])
        v = u * gain
        dgated = inv * (v - unit * jnp.mean(v * unit, axis=1, keepdims=True))
        dy_ref[rows, :] = dgated * sz
        dz_ref[rows, :] = (dgated * y * (sig * (1.0 + z * (1.0 - sig)))).astype(BF16)
        return 0

    lax.fori_loop(0, TOK // 32, gate, 0)

    ds_ref[...] = jnp.zeros((2, SPAN, SPAN), F32)
    lane = lax.broadcasted_iota(jnp.int32, (SPAN, 128), 1)

    def pair(hp, _):
        cols = pl.ds(pl.multiple_of(hp * 128, 128), 128)
        for k in range(2):
            rows = slice(k * SPAN, (k + 1) * SPAN)
            xp = x_ref[rows, cols].astype(F32)
            dh, dl = split2(dy_ref[rows, cols])
            dhl = jnp.concatenate([dh, dl], axis=1)
            xx = []
            for half in range(2):
                xm = jnp.where((lane < 64) if half == 0 else (lane >= 64), xp, 0.0).astype(BF16)
                xx.append(jnp.concatenate([xm, xm], axis=1))
            gts = dot_nt(jnp.concatenate([v[:HALF] for v in xx], axis=0), dhl)
            gbs = dot_nt(jnp.concatenate([v[HALF:] for v in xx], axis=0), dhl[HALF:])
            ths, tls, bhs, bls = [], [], [], []
            dst, dsb = ds_ref[k, :HALF, :], ds_ref[k, HALF:, HALF:]
            for half in range(2):
                h = hp * 2 + half
                part = slice(half * HALF, (half + 1) * HALF)
                crow = ct_ref[k, pl.ds(h, 1), :]
                hcols = pl.ds(pl.multiple_of(h * 128, 128), 128)
                top = rexp_ref[k * SPAN:k * SPAN + HALF, hcols]
                bot = rexp_ref[k * SPAN + HALF:(k + 1) * SPAN, hcols]
                et = jnp.exp2(jnp.minimum(jnp.concatenate([top, top], axis=1) + crow, BIG))
                eb = jnp.exp2(jnp.minimum(bot + crow[:, HALF:], BIG))
                dst = dst + et * gts[part]
                dsb = dsb + eb * gbs[part]
                hi, lo = split2(s_ref[k, :HALF, :] * et)
                ths.append(hi)
                tls.append(lo)
                hi, lo = split2(s_ref[k, HALF:, HALF:] * eb)
                bhs.append(hi)
                bls.append(lo)
            ds_ref[k, :HALF, :] = dst
            ds_ref[k, HALF:, HALF:] = dsb
            ot = dot(jnp.concatenate(ths, axis=0), dhl)
            ob = dot(jnp.concatenate(bhs, axis=0), dhl[HALF:])
            ot = (ot[:, :128] + ot[:, 128:]) + dot(jnp.concatenate(tls, axis=0), dh)
            ob = (ob[:, :128] + ob[:, 128:]) + dot(jnp.concatenate(bls, axis=0), dh[HALF:])
            outs = [jnp.concatenate([v[h * HALF:(h + 1) * HALF] for v in (ot, ob)], axis=0) for h in range(2)]
            dxs_ref[rows, cols] = jnp.where(lane < 64, outs[0], outs[1])
        return 0

    lax.fori_loop(0, 8, pair, 0)

    st = dot_nt(b_ref[:SPAN, :], c_ref[SPAN:, :])
    qdt = parts3(jnp.exp2(cums[0][SPAN - 1:SPAN, :] + rs[0]))
    p = parts3(jnp.exp2(cums[1]))
    dst = jnp.zeros((SPAN, SPAN), F32)
    for j in range(4):
        cols = slice(j * 256, (j + 1) * 256)
        qx = dot(qdt, narrow[:, cols])
        xq = qx * x_ref[:SPAN, cols].astype(F32)
        pdy = dot(p, narrow[:, cols]) * dy_ref[SPAN:, cols]
        dxs_ref[:SPAN, cols] += qx * dot3(st, pdy, dot)
        dst = dst + dot3(xq, pdy, dot_nt)

    seg_row = lax.broadcasted_iota(jnp.int32, (CH, 128), 0)
    seg_col = lax.broadcasted_iota(jnp.int32, (CH, 128), 1)
    seg = jnp.where(seg_row // 64 == seg_col, 1.0, 0.0).astype(BF16)

    def heads_sum(v):
        hi, lo = split2(v)
        return dot(hi, seg) + dot(lo, seg)

    tri = triangle(SPAN, False)
    later = jnp.zeros((1, 128), F32)
    rate_sum = jnp.zeros((1, 128), F32)
    skip_sum = jnp.zeros((1, 128), F32)
    for k in (1, 0):
        rows = slice(k * SPAN, (k + 1) * SPAN)
        xf = x_ref[rows, :].astype(F32)
        dy = dy_ref[rows, :]
        dxs = dxs_ref[rows, :]
        kx = heads_sum(dy * xf)
        r = heads_sum(dy * ys_ref[rows, :])
        q = heads_sum(xf * dxs)
        suffix = cumulate(tri, r - q) + later
        later = suffix[0:1, :]
        dt = pad_ref[rows, :]
        ddt = q / dt + kx * diags[k] + rate * suffix
        ddt_ref[rows, :] = ddt[:, :HEADS]
        rate_sum = rate_sum + rate * jnp.sum(dt * suffix, axis=0, keepdims=True)
        skip_sum = skip_sum + jnp.sum(kx, axis=0, keepdims=True)
        sd = jnp.sum(dt * kx, axis=1, keepdims=True)
        dsk = jnp.where(row < col, ds_ref[k], 0.0)
        bk, ck = b_ref[rows, :], c_ref[rows, :]
        sh, sl = split2(dsk)
        db = dot(sh, ck) + dot(sl, ck) + sd * ck.astype(F32)
        sh, sl = split2(dsk.T)
        dc = dot(sh, bk) + dot(sl, bk) + sd * bk.astype(F32)
        if k == 0:
            oh, ol = split2(dst)
            db = db + dot(oh, c_ref[SPAN:, :]) + dot(ol, c_ref[SPAN:, :])
        else:
            oh, ol = split2(dst.T)
            dc = dc + dot(oh, b_ref[:SPAN, :]) + dot(ol, b_ref[:SPAN, :])
        db_ref[rows, :] = db.astype(BF16)
        dc_ref[rows, :] = dc.astype(BF16)
        dx_ref[rows, :] = (dxs + coef_ref[rows, :] * dy).astype(BF16)

    dg = jnp.sum(dg_ref[...], axis=0, keepdims=True)
    for j in range(8):
        small_ref[j:j + 1, :] = dg[:, j * 128:(j + 1) * 128]
    small_ref[8:9, :] = rate_sum
    small_ref[9:10, :] = skip_sum
    small_ref[10:16, :] = jnp.zeros((6, 128), F32)


def scan_forward(x, z, b, c, dt, rate, skip, gain):
    return pl.pallas_call(
        fwd_kernel,
        out_shape=(jax.ShapeDtypeStruct((TOK, CH), F32), jax.ShapeDtypeStruct((TOK, CH), BF16)),
        scratch_shapes=[
            pltpu.VMEM((TOK, 128), F32),
            pltpu.VMEM((8, 128), F32),
            pltpu.VMEM((TOK, HEADS * HALF), F32),
            pltpu.VMEM((2, 128, SPAN), F32),
            pltpu.VMEM((2, SPAN, SPAN), F32),
            pltpu.VMEM((TOK, CH), F32),
        ],
        compiler_params=pltpu.CompilerParams(vmem_limit_bytes=VMEM_LIMIT),
        cost_estimate=SMALL,
        name="scan_forward",
    )(x, z, b, c, dt, rate, skip, gain)


def scan_backward(u, ys, x, z, b, c, dt, rate, skip, gain):
    return pl.pallas_call(
        bwd_kernel,
        out_shape=(
            jax.ShapeDtypeStruct((TOK, CH), BF16),
            jax.ShapeDtypeStruct((TOK, CH), BF16),
            jax.ShapeDtypeStruct((TOK, 128), BF16),
            jax.ShapeDtypeStruct((TOK, 128), BF16),
            jax.ShapeDtypeStruct((TOK, HEADS), F32),
            jax.ShapeDtypeStruct((16, 128), F32),
        ),
        scratch_shapes=[
            pltpu.VMEM((TOK, 128), F32),
            pltpu.VMEM((8, 128), F32),
            pltpu.VMEM((TOK, HEADS * HALF), F32),
            pltpu.VMEM((2, 128, SPAN), F32),
            pltpu.VMEM((2, SPAN, SPAN), F32),
            pltpu.VMEM((TOK, CH), F32),
            pltpu.VMEM((TOK, CH), F32),
            pltpu.VMEM((TOK, CH), F32),
            pltpu.VMEM((2, SPAN, SPAN), F32),
            pltpu.VMEM((8, CH), F32),
        ],
        compiler_params=pltpu.CompilerParams(vmem_limit_bytes=VMEM_LIMIT),
        cost_estimate=SMALL,
        name="scan_backward",
    )(u, ys, x, z, b, c, dt, rate, skip, gain)


AXES = {"z": 8, "xl": 2, "c": 2, "y": 4, "xh": 2}
DP = ("z", "xl", "c")
TP = ("y", "xh")


def send(v, axis, shift):
    n = AXES[axis]
    return lax.ppermute(v, axis, [(i, (i + shift) % n) for i in range(n)])


def swap(v, axis, mask):
    return lax.ppermute(v, axis, [(i, i ^ mask) for i in range(AXES[axis])])


def both_ways(up, down, axis):
    return send(up, axis, 1), send(down, axis, -1)


def tie(values, *first):
    return lax.optimization_barrier((tuple(values),) + tuple(first))[0]


def shuffle(name, shapes, plan, scalars, *arrays):
    count = len(plan([0] * len(scalars)))

    def kernel(s_ref, *refs):
        src, dst, sem = refs[:len(arrays)], refs[len(arrays):-1], refs[-1]
        copies = [
            pltpu.make_async_copy(src[i].at[a], dst[o].at[b], sem.at[k])
            for k, (i, a, o, b) in enumerate(plan([s_ref[j] for j in range(len(scalars))]))
        ]
        for copy in copies:
            copy.start()
        for copy in copies:
            copy.wait()

    return pl.pallas_call(
        kernel,
        out_shape=tuple(jax.ShapeDtypeStruct(s, BF16) for s in shapes),
        in_specs=[pl.BlockSpec(memory_space=pltpu.SMEM)] + [pl.BlockSpec(memory_space=pl.ANY)] * len(arrays),
        out_specs=tuple(pl.BlockSpec(memory_space=pltpu.VMEM) for _ in shapes),
        scratch_shapes=[pltpu.SemaphoreType.DMA((count,))],
        cost_estimate=SMALL,
        name=name,
    )(jnp.stack([s.astype(jnp.int32) for s in scalars]), *arrays)


def own_first(rows, core):
    def kernel(core_ref, in_ref, out_ref):
        for j in range(16):
            even = in_ref[:, 256 * j:256 * j + 128]
            odd = in_ref[:, 256 * j + 128:256 * j + 256]
            first = core_ref[0] == 0
            out_ref[:, 128 * j:128 * j + 128] = jnp.where(first, even, odd)
            out_ref[:, 2048 + 128 * j:2048 + 128 * j + 128] = jnp.where(first, odd, even)

    return pl.pallas_call(
        kernel,
        out_shape=jax.ShapeDtypeStruct(rows.shape, rows.dtype),
        in_specs=[pl.BlockSpec(memory_space=pltpu.SMEM), pl.BlockSpec(memory_space=pltpu.VMEM)],
        out_specs=pl.BlockSpec(memory_space=pltpu.VMEM),
        cost_estimate=SMALL,
        name="own_first",
    )(core.astype(jnp.int32).reshape(1), rows)


def at_rows(start, size):
    return (pl.ds(pl.multiple_of(start, 32), size), slice(None)) if not isinstance(start, int) else (slice(start, start + size), slice(None))


def place_tokens(yi, xh, *pieces):
    turns = (0, 0, 3, 3, 1, 1, 2, 2)

    def plan(s):
        moves = []
        for i in range(8):
            start = ((s[0] + turns[i]) % 4) * 128 + (1 - s[1] if i % 2 else s[1]) * 64
            for o in range(2):
                moves.append((i, (slice(None), slice(2048 * o, 2048 * o + 2048)), o, at_rows(start, 64)))
        return moves

    return shuffle("place_tokens", [(TOK, 2048)] * 2, plan, (yi, xh), *pieces)


def place_weights(zi, xl, *arrays):
    parts = (
        (0, 0, 128, 0, 0, 0), (1, 0, 128, 0, 1, 0),
        (2, 0, 128, 7, 0, 0), (3, 0, 128, 1, 0, 0),
        (4, 0, 128, 7, 1, 0), (4, 128, 128, 6, 0, 0), (5, 0, 128, 2, 0, 0), (5, 128, 128, 1, 1, 0),
        (6, 0, 128, 6, 1, 0), (6, 128, 128, 5, 0, 0), (7, 0, 128, 3, 0, 0), (7, 128, 128, 2, 1, 0),
        (8, 0, 128, 5, 1, 0), (8, 128, 64, 4, 0, 0), (9, 0, 64, 4, 0, 64), (9, 64, 128, 3, 1, 0),
        (10, 0, 128, 4, 1, 0),
    )

    def plan(s):
        moves = []
        for array, first, size, turn, other, offset in parts:
            block = ((s[0] + turn) % 8) * 2 + (1 - s[1] if other else s[1])
            moves.append((array, at_rows(first, size), 0, at_rows(block * 128 + offset, size)))
        return moves

    return shuffle("place_weights", [(2048, CH)], plan, (zi, xl), *arrays)[0]


def weight_blocks(zi, shifts, keep, theirs, normed, normed_other):
    def kernel(at_ref, a_ref, b_ref, n_ref, m_ref, out_ref):
        def term(r, n):
            return lax.dot_general(r[...], n[...], (((0,), (0,)), ((), ())), preferred_element_type=F32)

        out_ref[0] = term(a_ref, n_ref) + term(b_ref, m_ref)

    columns = pl.BlockSpec((TOK, 256), lambda i, at: (0, at[i]))
    whole = pl.BlockSpec((TOK, CH), lambda i, at: (0, 0))
    return pl.pallas_call(
        kernel,
        grid_spec=pltpu.PrefetchScalarGridSpec(
            num_scalar_prefetch=1,
            grid=(len(shifts),),
            in_specs=[columns, columns, whole, whole],
            out_specs=pl.BlockSpec((1, 256, CH), lambda i, at: (i, 0, 0)),
        ),
        out_shape=jax.ShapeDtypeStruct((len(shifts), 256, CH), F32),
        compiler_params=pltpu.CompilerParams(vmem_limit_bytes=VMEM_LIMIT),
        cost_estimate=SMALL,
        name="weight_blocks",
    )(jnp.stack([(zi + k + 8) % 8 for k in shifts]).astype(jnp.int32), keep, theirs, normed, normed_other)


def back_project(keep, give, w_keep, w_give):
    def kernel(a_ref, b_ref, v_ref, w_ref, out_ref):
        out_ref[...] = dot(a_ref[...], v_ref[...]) + dot(b_ref[...], w_ref[...])

    rows = pl.BlockSpec((TOK, 2048), lambda i: (0, 0))
    columns = pl.BlockSpec((2048, 256), lambda i: (0, i))
    return pl.pallas_call(
        kernel,
        grid=(4,),
        in_specs=[rows, rows, columns, columns],
        out_specs=pl.BlockSpec((TOK, 256), lambda i: (0, i)),
        out_shape=jax.ShapeDtypeStruct((TOK, CH), F32),
        compiler_params=pltpu.CompilerParams(vmem_limit_bytes=VMEM_LIMIT),
        cost_estimate=SMALL,
        name="back_project",
    )(keep, give, w_keep, w_give)


def on_device(grad_out, x, z, b, c, dt, rate, skip, gain, w_out):
    zi, xl, core, yi, xh = (lax.axis_index(a) for a in ("z", "xl", "c", "y", "xh"))
    scan = (x, z, b.reshape(TOK, 128), c.reshape(TOK, 128), dt, rate[None], skip[None], gain[None])

    own = own_first(grad_out, core)
    below, above = both_ways(own, own, "y")
    other = send(own, "xh", 1)
    b1, a1 = both_ways(w_out, w_out, "z")
    w_late, = tie((w_out,), b1)
    w_other = send(w_late, "xl", 1)
    below, above, other, w_other, b1, a1, late = tie((below, above, other, w_other, b1, a1, scan[6]))

    b_other = send(other, "y", 1)
    far_own = send(above, "y", -1)
    a_other = send(above, "xh", 1)
    b2, a2 = both_ways(jnp.concatenate([w_other, b1], axis=0), jnp.concatenate([a1, w_other], axis=0), "z")
    ys, normed = scan_forward(*scan[:6], late, scan[7])
    b_other, far_own, a_other, b2, a2, normed = tie((b_other, far_own, a_other, b2, a2, normed))

    far_other = send(a_other, "y", -1)
    b3, a3 = both_ways(b2, a2, "z")
    normed_other = send(normed, "c", 1)
    far_other, b3, a3, normed_other = tie((far_other, b3, a3, normed_other))
    keep, give = place_tokens(yi, xh, own, other, below, b_other, above, a_other, far_own, far_other)
    theirs = send(give, "c", 1)
    b4, a4 = both_ways(b3[:192], a3[64:], "z")
    theirs, b4, a4 = tie((theirs, b4, a4))

    def blocks(*shifts):
        return weight_blocks(zi, shifts, keep, theirs, normed, normed_other)

    half = CH // 2
    far = blocks(4)[0].astype(BF16)
    up, down = both_ways(far[:, half:], far[:, :half], "z")
    b4, a4 = tie((b4, a4), far)
    x4 = send(jnp.concatenate([b4[128:], a4[:64]], axis=0), "xl", 1)
    v = blocks(3, -3)
    w_keep = place_weights(zi, xl, w_out, w_other, b1, a1, b2, a2, b3, a3, b4, a4, x4)
    up, down, v, w_keep = tie((up, down, v, w_keep))
    w_give = send(w_keep, "c", 1)

    up = jnp.concatenate([v[0, :, :half], v[0, :, half:] + up.astype(F32)], axis=1).astype(BF16)
    down = jnp.concatenate([v[1, :, :half] + down.astype(F32), v[1, :, half:]], axis=1).astype(BF16)
    up, down = both_ways(up, down, "z")
    upstream = back_project(keep, give, w_keep, w_give)
    v = blocks(2, -2)
    up, down, v, upstream = tie((up, down, v, upstream))

    up, down = both_ways((v[0] + up.astype(F32)).astype(BF16), (v[1] + down.astype(F32)).astype(BF16), "z")
    dx, dz, db, dc, ddt, small = scan_backward(upstream, ys, *scan)
    v = blocks(1, -1)
    up, down, v, small = tie((up, down, v, small))

    up, down = both_ways((v[0] + up.astype(F32)).astype(BF16), (v[1] + down.astype(F32)).astype(BF16), "z")
    small = small + send(small, "c", 1)
    small = small + send(small, "xl", 1)
    total = blocks(0)[0]
    up, down, small, total = tie((up, down, small, total))
    total = (total + (up.astype(F32) + down.astype(F32))).reshape(2, 128, CH)
    stay = lax.dynamic_index_in_dim(total, xl, 0, keepdims=False)
    leave = lax.dynamic_index_in_dim(total, 1 - xl, 0, keepdims=False)
    small, leave = tie((small, leave))
    arrived = send(leave, "xl", 1)
    for mask in (1, 2, 4):
        small = small + swap(small, "z", mask)
    arrived, = tie((arrived,), small)
    grad_weight = stay + arrived
    return (dx, dz, db[:, None], dc[:, None], ddt, small[8, :HEADS], small[9, :HEADS],
            small[:8].reshape(CH), grad_weight)


def solution(mesh):
    fine = jax.sharding.Mesh(mesh.devices.reshape(tuple(AXES.values())), tuple(AXES))
    part = P(DP, TP)
    part3 = P(DP, TP, None)
    head = P(TP)
    return jax.shard_map(
        on_device,
        mesh=fine,
        in_specs=(P(DP + TP, None), part, part, part3, part3, part, head, head, head, part),
        out_specs=(part, part, part3, part3, part, head, head, head, part),
        check_vma=False,
    )
```

```python
import jax
import jax.numpy as jnp
from jax import lax
from jax.experimental import pallas as pl
from jax.experimental.pallas import tpu as pltpu
from jax.sharding import PartitionSpec as P

F32, BF16 = jnp.float32, jnp.bfloat16
HEADS = 16
SPAN = 256
TOK = 512
CH = 1024
HALF = 128
LOG2E = 1.4426950408889634
BIG = 126.0
VMEM_LIMIT = 48 * 1024 * 1024
SMALL = pl.CostEstimate(flops=1000, bytes_accessed=1000, transcendentals=0)


def dot(a, b):
    return jnp.dot(a, b, preferred_element_type=F32)


def dot_nt(a, b):
    return lax.dot_general(a, b, (((1,), (1,)), ((), ())), preferred_element_type=F32)


def split2(v):
    hi = v.astype(BF16)
    return hi, (v - hi.astype(F32)).astype(BF16)


def dot3(a, b, fn):
    ah, al = split2(a)
    bh, bl = split2(b)
    return fn(ah, bh) + (fn(ah, bl) + fn(al, bh))


def spread_matrix(width):
    row = lax.broadcasted_iota(jnp.int32, (128, HEADS * width), 0)
    col = lax.broadcasted_iota(jnp.int32, (128, HEADS * width), 1)
    return jnp.where((row < 48) & ((row & 15) == col // width), 1.0, 0.0).astype(BF16)


def parts3(v):
    lane = lax.broadcasted_iota(jnp.int32, v.shape, 1)
    v = jnp.where(lane < HEADS, v, 0.0)
    one = v.astype(BF16).astype(F32)
    rest = v - one
    two = rest.astype(BF16).astype(F32)
    three = rest - two
    return (one + pltpu.roll(two, 16, 1) + pltpu.roll(three, 32, 1)).astype(BF16)


def cumulate(tri, v):
    one = v.astype(BF16)
    rest = v - one.astype(F32)
    two = rest.astype(BF16)
    three = (rest - two.astype(F32)).astype(BF16)
    return dot(tri, one) + (dot(tri, two) + dot(tri, three))


def triangle(n, lower):
    row = lax.broadcasted_iota(jnp.int32, (n, n), 0)
    col = lax.broadcasted_iota(jnp.int32, (n, n), 1)
    return jnp.where(row >= col if lower else row <= col, 1.0, 0.0).astype(BF16)


def prepare(dt_ref, rate_ref, pad_ref, ratepad_ref):
    pad_ref[...] = jnp.ones((TOK, 128), F32)
    pad_ref[:, :HEADS] = dt_ref[...]
    ratepad_ref[...] = jnp.zeros((8, 128), F32)
    ratepad_ref[0:1, :HEADS] = rate_ref[...]
    rate = -jnp.exp(ratepad_ref[0:1, :])
    tri = triangle(SPAN, True)
    cums, rs = [], []
    for k in range(2):
        dt = pad_ref[k * SPAN:(k + 1) * SPAN, :]
        cum = cumulate(tri, dt * (rate * LOG2E))
        cums.append(cum)
        rs.append(jnp.log2(dt) - cum)
    return rate, cums, rs


def fwd_kernel(x_ref, z_ref, b_ref, c_ref, dt_ref, rate_ref, skip_ref, gain_ref,
               ys_ref, n_ref, pad_ref, ratepad_ref, cexp_ref, rt_ref, s_ref, coef_ref):
    rate, cums, rs = prepare(dt_ref, rate_ref, pad_ref, ratepad_ref)
    wide = spread_matrix(HALF)
    narrow = spread_matrix(64)
    row = lax.broadcasted_iota(jnp.int32, (SPAN, SPAN), 0)
    col = lax.broadcasted_iota(jnp.int32, (SPAN, SPAN), 1)
    ratepad_ref[0:1, :HEADS] = skip_ref[...]
    skip = ratepad_ref[0:1, :]
    for k in range(2):
        rows = slice(k * SPAN, (k + 1) * SPAN)
        cexp_ref[rows, :] = dot(parts3(cums[k]), wide)
        rt_ref[k] = rs[k].T
        bk, ck = b_ref[rows, :], c_ref[rows, :]
        s_ref[k] = jnp.where(row > col, dot_nt(ck, bk), 0.0)
        diag = jnp.sum(bk.astype(F32) * ck.astype(F32), axis=1, keepdims=True)
        coef_ref[rows, :] = dot(parts3(diag * pad_ref[rows, :] + skip), narrow)
    lane = lax.broadcasted_iota(jnp.int32, (SPAN, 128), 1)

    def pair(hp, _):
        cols = pl.ds(pl.multiple_of(hp * 128, 128), 128)
        for k in range(2):
            rows = slice(k * SPAN, (k + 1) * SPAN)
            xp = x_ref[rows, cols]
            tops, bots = [], []
            for half in range(2):
                h = hp * 2 + half
                rrow = rt_ref[k, pl.ds(h, 1), :]
                hcols = pl.ds(pl.multiple_of(h * 128, 128), 128)
                top = cexp_ref[k * SPAN:k * SPAN + HALF, hcols]
                bot = cexp_ref[k * SPAN + HALF:(k + 1) * SPAN, hcols]
                wt = s_ref[k, :HALF, :HALF] * jnp.exp2(jnp.minimum(top + rrow[:, :HALF], BIG))
                wb = s_ref[k, HALF:, :] * jnp.exp2(
                    jnp.minimum(jnp.concatenate([bot, bot], axis=1) + rrow, BIG))
                tops += split2(wt)
                bots += split2(wb)
            yt = dot(jnp.concatenate(tops, axis=0), xp[:HALF])
            yb = dot(jnp.concatenate(bots, axis=0), xp)
            ys = [jnp.concatenate([v[256 * h:256 * h + 128] + v[256 * h + 128:256 * h + 256] for v in (yt, yb)], axis=0)
                  for h in range(2)]
            ys_ref[rows, cols] = jnp.where(lane < 64, ys[0], ys[1])
        return 0

    lax.fori_loop(0, 8, pair, 0)

    s10 = dot_nt(c_ref[SPAN:, :], b_ref[:SPAN, :])
    qdt = parts3(jnp.exp2(cums[0][SPAN - 1:SPAN, :] + rs[0]))
    p = parts3(jnp.exp2(cums[1]))
    for j in range(4):
        cols = slice(j * 256, (j + 1) * 256)
        xq = dot(qdt, narrow[:, cols]) * x_ref[:SPAN, cols].astype(F32)
        ys_ref[SPAN:, cols] += dot(p, narrow[:, cols]) * dot3(s10, xq, dot)

    gain = gain_ref[...]

    def norm(i, _):
        rows = pl.ds(pl.multiple_of(i * 32, 32), 32)
        z = z_ref[rows, :].astype(F32)
        y = ys_ref[rows, :] + coef_ref[rows, :] * x_ref[rows, :].astype(F32)
        gated = y * (z / (1.0 + jnp.exp(-z)))
        inv = lax.rsqrt(jnp.mean(gated * gated, axis=1, keepdims=True) + 1e-05)
        n_ref[rows, :] = (gated * inv * gain).astype(BF16)
        return 0

    lax.fori_loop(0, TOK // 32, norm, 0)


def bwd_kernel(u_ref, ys_ref, x_ref, z_ref, b_ref, c_ref, dt_ref, rate_ref, skip_ref, gain_ref,
               dx_ref, dz_ref, db_ref, dc_ref, ddt_ref, small_ref,
               pad_ref, ratepad_ref, rexp_ref, ct_ref, s_ref, coef_ref, dy_ref, dxs_ref, ds_ref, dg_ref):
    rate, cums, rs = prepare(dt_ref, rate_ref, pad_ref, ratepad_ref)
    wide = spread_matrix(HALF)
    narrow = spread_matrix(64)
    row = lax.broadcasted_iota(jnp.int32, (SPAN, SPAN), 0)
    col = lax.broadcasted_iota(jnp.int32, (SPAN, SPAN), 1)
    ratepad_ref[0:1, :HEADS] = skip_ref[...]
    skip = ratepad_ref[0:1, :]
    diags = []
    for k in range(2):
        rows = slice(k * SPAN, (k + 1) * SPAN)
        rexp_ref[rows, :] = dot(parts3(rs[k]), wide)
        ct_ref[k] = cums[k].T
        bk, ck = b_ref[rows, :], c_ref[rows, :]
        s_ref[k] = jnp.where(row < col, dot_nt(bk, ck), 0.0)
        diag = jnp.sum(bk.astype(F32) * ck.astype(F32), axis=1, keepdims=True)
        diags.append(diag)
        coef_ref[rows, :] = dot(parts3(diag * pad_ref[rows, :] + skip), narrow)

    gain = gain_ref[...]
    dg_ref[...] = jnp.zeros((8, CH), F32)

    def gate(i, _):
        rows = pl.ds(pl.multiple_of(i * 32, 32), 32)
        z = z_ref[rows, :].astype(F32)
        y = ys_ref[rows, :] + coef_ref[rows, :] * x_ref[rows, :].astype(F32)
        sig = 1.0 / (1.0 + jnp.exp(-z))
        sz = z * sig
        gated = y * sz
        inv = lax.rsqrt(jnp.mean(gated * gated, axis=1, keepdims=True) + 1e-05)
        unit = gated * inv
        u = u_ref[rows, :]
        ug = u * unit
        dg_ref[...] += (ug[0:8] + ug[8:16]) + (ug[16:24] + ug[24:32])
        v = u * gain
        dgated = inv * (v - unit * jnp.mean(v * unit, axis=1, keepdims=True))
        dy_ref[rows, :] = dgated * sz
        dz_ref[rows, :] = (dgated * y * (sig * (1.0 + z * (1.0 - sig)))).astype(BF16)
        return 0

    lax.fori_loop(0, TOK // 32, gate, 0)

    ds_ref[...] = jnp.zeros((2, SPAN, SPAN), F32)
    lane = lax.broadcasted_iota(jnp.int32, (SPAN, 128), 1)

    def pair(hp, _):
        cols = pl.ds(pl.multiple_of(hp * 128, 128), 128)
        for k in range(2):
            rows = slice(k * SPAN, (k + 1) * SPAN)
            xp = x_ref[rows, cols].astype(F32)
            dh, dl = split2(dy_ref[rows, cols])
            dhl = jnp.concatenate([dh, dl], axis=1)
            xx = []
            for half in range(2):
                xm = jnp.where((lane < 64) if half == 0 else (lane >= 64), xp, 0.0).astype(BF16)
                xx.append(jnp.concatenate([xm, xm], axis=1))
            gts = dot_nt(jnp.concatenate([v[:HALF] for v in xx], axis=0), dhl)
            gbs = dot_nt(jnp.concatenate([v[HALF:] for v in xx], axis=0), dhl[HALF:])
            ths, tls, bhs, bls = [], [], [], []
            dst, dsb = ds_ref[k, :HALF, :], ds_ref[k, HALF:, HALF:]
            for half in range(2):
                h = hp * 2 + half
                part = slice(half * HALF, (half + 1) * HALF)
                crow = ct_ref[k, pl.ds(h, 1), :]
                hcols = pl.ds(pl.multiple_of(h * 128, 128), 128)
                top = rexp_ref[k * SPAN:k * SPAN + HALF, hcols]
                bot = rexp_ref[k * SPAN + HALF:(k + 1) * SPAN, hcols]
                et = jnp.exp2(jnp.minimum(jnp.concatenate([top, top], axis=1) + crow, BIG))
                eb = jnp.exp2(jnp.minimum(bot + crow[:, HALF:], BIG))
                dst = dst + et * gts[part]
                dsb = dsb + eb * gbs[part]
                hi, lo = split2(s_ref[k, :HALF, :] * et)
                ths.append(hi)
                tls.append(lo)
                hi, lo = split2(s_ref[k, HALF:, HALF:] * eb)
                bhs.append(hi)
                bls.append(lo)
            ds_ref[k, :HALF, :] = dst
            ds_ref[k, HALF:, HALF:] = dsb
            ot = dot(jnp.concatenate(ths, axis=0), dhl)
            ob = dot(jnp.concatenate(bhs, axis=0), dhl[HALF:])
            ot = (ot[:, :128] + ot[:, 128:]) + dot(jnp.concatenate(tls, axis=0), dh)
            ob = (ob[:, :128] + ob[:, 128:]) + dot(jnp.concatenate(bls, axis=0), dh[HALF:])
            outs = [jnp.concatenate([v[h * HALF:(h + 1) * HALF] for v in (ot, ob)], axis=0) for h in range(2)]
            dxs_ref[rows, cols] = jnp.where(lane < 64, outs[0], outs[1])
        return 0

    lax.fori_loop(0, 8, pair, 0)

    st = dot_nt(b_ref[:SPAN, :], c_ref[SPAN:, :])
    qdt = parts3(jnp.exp2(cums[0][SPAN - 1:SPAN, :] + rs[0]))
    p = parts3(jnp.exp2(cums[1]))
    dst = jnp.zeros((SPAN, SPAN), F32)
    for j in range(4):
        cols = slice(j * 256, (j + 1) * 256)
        qx = dot(qdt, narrow[:, cols])
        xq = qx * x_ref[:SPAN, cols].astype(F32)
        pdy = dot(p, narrow[:, cols]) * dy_ref[SPAN:, cols]
        dxs_ref[:SPAN, cols] += qx * dot3(st, pdy, dot)
        dst = dst + dot3(xq, pdy, dot_nt)

    seg_row = lax.broadcasted_iota(jnp.int32, (CH, 128), 0)
    seg_col = lax.broadcasted_iota(jnp.int32, (CH, 128), 1)
    seg = jnp.where(seg_row // 64 == seg_col, 1.0, 0.0).astype(BF16)

    def heads_sum(v):
        hi, lo = split2(v)
        return dot(hi, seg) + dot(lo, seg)

    tri = triangle(SPAN, False)
    later = jnp.zeros((1, 128), F32)
    rate_sum = jnp.zeros((1, 128), F32)
    skip_sum = jnp.zeros((1, 128), F32)
    for k in (1, 0):
        rows = slice(k * SPAN, (k + 1) * SPAN)
        xf = x_ref[rows, :].astype(F32)
        dy = dy_ref[rows, :]
        dxs = dxs_ref[rows, :]
        kx = heads_sum(dy * xf)
        r = heads_sum(dy * ys_ref[rows, :])
        q = heads_sum(xf * dxs)
        suffix = cumulate(tri, r - q) + later
        later = suffix[0:1, :]
        dt = pad_ref[rows, :]
        ddt = q / dt + kx * diags[k] + rate * suffix
        ddt_ref[rows, :] = ddt[:, :HEADS]
        rate_sum = rate_sum + rate * jnp.sum(dt * suffix, axis=0, keepdims=True)
        skip_sum = skip_sum + jnp.sum(kx, axis=0, keepdims=True)
        sd = jnp.sum(dt * kx, axis=1, keepdims=True)
        dsk = jnp.where(row < col, ds_ref[k], 0.0)
        bk, ck = b_ref[rows, :], c_ref[rows, :]
        sh, sl = split2(dsk)
        db = dot(sh, ck) + dot(sl, ck) + sd * ck.astype(F32)
        sh, sl = split2(dsk.T)
        dc = dot(sh, bk) + dot(sl, bk) + sd * bk.astype(F32)
        if k == 0:
            oh, ol = split2(dst)
            db = db + dot(oh, c_ref[SPAN:, :]) + dot(ol, c_ref[SPAN:, :])
        else:
            oh, ol = split2(dst.T)
            dc = dc + dot(oh, b_ref[:SPAN, :]) + dot(ol, b_ref[:SPAN, :])
        db_ref[rows, :] = db.astype(BF16)
        dc_ref[rows, :] = dc.astype(BF16)
        dx_ref[rows, :] = (dxs + coef_ref[rows, :] * dy).astype(BF16)

    dg = jnp.sum(dg_ref[...], axis=0, keepdims=True)
    for j in range(8):
        small_ref[j:j + 1, :] = dg[:, j * 128:(j + 1) * 128]
    small_ref[8:9, :] = rate_sum
    small_ref[9:10, :] = skip_sum
    small_ref[10:16, :] = jnp.zeros((6, 128), F32)


def scan_forward(x, z, b, c, dt, rate, skip, gain):
    return pl.pallas_call(
        fwd_kernel,
        out_shape=(jax.ShapeDtypeStruct((TOK, CH), F32), jax.ShapeDtypeStruct((TOK, CH), BF16)),
        scratch_shapes=[
            pltpu.VMEM((TOK, 128), F32),
            pltpu.VMEM((8, 128), F32),
            pltpu.VMEM((TOK, HEADS * HALF), F32),
            pltpu.VMEM((2, 128, SPAN), F32),
            pltpu.VMEM((2, SPAN, SPAN), F32),
            pltpu.VMEM((TOK, CH), F32),
        ],
        compiler_params=pltpu.CompilerParams(vmem_limit_bytes=VMEM_LIMIT),
        cost_estimate=SMALL,
        name="scan_forward",
    )(x, z, b, c, dt, rate, skip, gain)


def scan_backward(u, ys, x, z, b, c, dt, rate, skip, gain):
    return pl.pallas_call(
        bwd_kernel,
        out_shape=(
            jax.ShapeDtypeStruct((TOK, CH), BF16),
            jax.ShapeDtypeStruct((TOK, CH), BF16),
            jax.ShapeDtypeStruct((TOK, 128), BF16),
            jax.ShapeDtypeStruct((TOK, 128), BF16),
            jax.ShapeDtypeStruct((TOK, HEADS), F32),
            jax.ShapeDtypeStruct((16, 128), F32),
        ),
        scratch_shapes=[
            pltpu.VMEM((TOK, 128), F32),
            pltpu.VMEM((8, 128), F32),
            pltpu.VMEM((TOK, HEADS * HALF), F32),
            pltpu.VMEM((2, 128, SPAN), F32),
            pltpu.VMEM((2, SPAN, SPAN), F32),
            pltpu.VMEM((TOK, CH), F32),
            pltpu.VMEM((TOK, CH), F32),
            pltpu.VMEM((TOK, CH), F32),
            pltpu.VMEM((2, SPAN, SPAN), F32),
            pltpu.VMEM((8, CH), F32),
        ],
        compiler_params=pltpu.CompilerParams(vmem_limit_bytes=VMEM_LIMIT),
        cost_estimate=SMALL,
        name="scan_backward",
    )(u, ys, x, z, b, c, dt, rate, skip, gain)


AXES = {"z": 8, "xl": 2, "c": 2, "y": 4, "xh": 2}
DP = ("z", "xl", "c")
TP = ("y", "xh")


def send(v, axis, shift):
    n = AXES[axis]
    return lax.ppermute(v, axis, [(i, (i + shift) % n) for i in range(n)])


def swap(v, axis, mask):
    return lax.ppermute(v, axis, [(i, i ^ mask) for i in range(AXES[axis])])


def both_ways(up, down, axis):
    return send(up, axis, 1), send(down, axis, -1)


def tie(values, *first):
    return lax.optimization_barrier((tuple(values),) + tuple(first))[0]


def shuffle(name, shapes, plan, scalars, *arrays):
    count = len(plan([0] * len(scalars)))

    def kernel(s_ref, *refs):
        src, dst, sem = refs[:len(arrays)], refs[len(arrays):-1], refs[-1]
        copies = [
            pltpu.make_async_copy(src[i].at[a], dst[o].at[b], sem.at[k])
            for k, (i, a, o, b) in enumerate(plan([s_ref[j] for j in range(len(scalars))]))
        ]
        for copy in copies:
            copy.start()
        for copy in copies:
            copy.wait()

    return pl.pallas_call(
        kernel,
        out_shape=tuple(jax.ShapeDtypeStruct(s, BF16) for s in shapes),
        in_specs=[pl.BlockSpec(memory_space=pltpu.SMEM)] + [pl.BlockSpec(memory_space=pl.ANY)] * len(arrays),
        out_specs=tuple(pl.BlockSpec(memory_space=pltpu.VMEM) for _ in shapes),
        scratch_shapes=[pltpu.SemaphoreType.DMA((count,))],
        cost_estimate=SMALL,
        name=name,
    )(jnp.stack([s.astype(jnp.int32) for s in scalars]), *arrays)


def own_first(rows, core):
    def kernel(core_ref, in_ref, out_ref):
        for j in range(16):
            even = in_ref[:, 256 * j:256 * j + 128]
            odd = in_ref[:, 256 * j + 128:256 * j + 256]
            first = core_ref[0] == 0
            out_ref[:, 128 * j:128 * j + 128] = jnp.where(first, even, odd)
            out_ref[:, 2048 + 128 * j:2048 + 128 * j + 128] = jnp.where(first, odd, even)

    return pl.pallas_call(
        kernel,
        out_shape=jax.ShapeDtypeStruct(rows.shape, rows.dtype),
        in_specs=[pl.BlockSpec(memory_space=pltpu.SMEM), pl.BlockSpec(memory_space=pltpu.VMEM)],
        out_specs=pl.BlockSpec(memory_space=pltpu.VMEM),
        cost_estimate=SMALL,
        name="own_first",
    )(core.astype(jnp.int32).reshape(1), rows)


def at_rows(start, size):
    return (pl.ds(pl.multiple_of(start, 32), size), slice(None)) if not isinstance(start, int) else (slice(start, start + size), slice(None))


def place_tokens(yi, xh, first, *pieces):
    parts = ((0, 64, 0, 0, 0), (1, 64, 0, 1, 0), (2, 64, 3, 0, 0), (3, 64, 3, 1, 0), (4, 64, 1, 0, 0),
             (5, 64, 1, 1, 0), (6, 64, 2, 0, 0), (7, 32, 2, 1, 0), (8, 32, 2, 1, 32))

    def plan(s):
        moves = []
        for piece, size, turn, other, offset in parts:
            start = ((s[0] + turn) % 4) * 128 + (1 - s[1] if other else s[1]) * 64 + offset
            moves.append((piece, (slice(None), slice(first, first + 2048)), 0, at_rows(start, size)))
        return moves

    return shuffle("place_tokens", [(TOK, 2048)], plan, (yi, xh), *pieces)[0]


def weight_blocks(zi, shifts, keep, theirs, normed, normed_other):
    def kernel(at_ref, a_ref, b_ref, n_ref, m_ref, out_ref):
        def term(r, n):
            return lax.dot_general(r[...], n[...], (((0,), (0,)), ((), ())), preferred_element_type=F32)

        out_ref[0] = term(a_ref, n_ref) + term(b_ref, m_ref)

    columns = pl.BlockSpec((TOK, 256), lambda i, at: (0, at[i]))
    whole = pl.BlockSpec((TOK, CH), lambda i, at: (0, 0))
    return pl.pallas_call(
        kernel,
        grid_spec=pltpu.PrefetchScalarGridSpec(
            num_scalar_prefetch=1,
            grid=(len(shifts),),
            in_specs=[columns, columns, whole, whole],
            out_specs=pl.BlockSpec((1, 256, CH), lambda i, at: (i, 0, 0)),
        ),
        out_shape=jax.ShapeDtypeStruct((len(shifts), 256, CH), F32),
        compiler_params=pltpu.CompilerParams(vmem_limit_bytes=VMEM_LIMIT),
        cost_estimate=SMALL,
        name="weight_blocks",
    )(jnp.stack([(zi + k + 8) % 8 for k in shifts]).astype(jnp.int32), keep, theirs, normed, normed_other)


def back_project(core, keep, give, w):
    def kernel(core_ref, a_ref, b_ref, v_ref, w_ref, out_ref):
        out_ref[...] = dot(a_ref[...], v_ref[...].reshape(2048, 256)) + dot(b_ref[...], w_ref[...].reshape(2048, 256))

    rows = pl.BlockSpec((TOK, 2048), lambda i, core: (0, 0))
    return pl.pallas_call(
        kernel,
        grid_spec=pltpu.PrefetchScalarGridSpec(
            num_scalar_prefetch=1,
            grid=(4,),
            in_specs=[
                rows,
                rows,
                pl.BlockSpec((16, None, 128, 256), lambda i, core: (0, core[0], 0, i)),
                pl.BlockSpec((16, None, 128, 256), lambda i, core: (0, 1 - core[0], 0, i)),
            ],
            out_specs=pl.BlockSpec((TOK, 256), lambda i, core: (0, i)),
        ),
        out_shape=jax.ShapeDtypeStruct((TOK, CH), F32),
        compiler_params=pltpu.CompilerParams(vmem_limit_bytes=VMEM_LIMIT),
        cost_estimate=SMALL,
        name="back_project",
    )(core.astype(jnp.int32).reshape(1), keep, give, w, w)


def on_device(grad_out, x, z, b, c, dt, rate, skip, gain, w_out):
    zi, xl, core, yi, xh = (lax.axis_index(a) for a in ("z", "xl", "c", "y", "xh"))
    scan = (x, z, b.reshape(TOK, 128), c.reshape(TOK, 128), dt, rate[None], skip[None], gain[None])

    w = lax.all_gather(w_out, DP, axis=0, tiled=True).reshape(16, 2, 128, CH)

    own = own_first(grad_out, core)
    below, above = both_ways(own, own, "y")
    other = send(own, "xh", 1)
    below, above, other, late = tie((below, above, other, scan[6]))

    b_other = send(other, "y", 1)
    far_own = send(above, "y", -1)
    a_other = send(above, "xh", 1)
    ys, normed = scan_forward(*scan[:6], late, scan[7])
    b_other, far_own, a_other, normed = tie((b_other, far_own, a_other, normed))

    far_b, far_a = both_ways(b_other[:32], a_other[32:], "y")
    normed_other = send(normed, "c", 1)
    far_b, far_a, normed_other = tie((far_b, far_a, normed_other))
    pieces = (own, other, below, b_other, above, a_other, far_own, far_b, far_a)
    give = place_tokens(yi, xh, 2048, *pieces)
    theirs = send(give, "c", 1)
    keep = place_tokens(yi, xh, 0, *tie(pieces, give))
    theirs, keep = tie((theirs, keep))

    def blocks(*shifts):
        return weight_blocks(zi, shifts, keep, theirs, normed, normed_other)

    half = CH // 2
    far = blocks(4)[0].astype(BF16)
    up, down = both_ways(far[:, half:], far[:, :half], "z")
    v = blocks(3, -3)
    up, down, v = tie((up, down, v))

    up = jnp.concatenate([v[0, :, :half], v[0, :, half:] + up.astype(F32)], axis=1).astype(BF16)
    down = jnp.concatenate([v[1, :, :half] + down.astype(F32), v[1, :, half:]], axis=1).astype(BF16)
    up, down = both_ways(up, down, "z")
    upstream = back_project(core, keep, give, w)
    v = blocks(2, -2)
    up, down, v, upstream = tie((up, down, v, upstream))

    up, down = both_ways((v[0] + up.astype(F32)).astype(BF16), (v[1] + down.astype(F32)).astype(BF16), "z")
    dx, dz, db, dc, ddt, small = scan_backward(upstream, ys, *scan)
    v = blocks(1, -1)
    up, down, v, small = tie((up, down, v, small))

    up, down = both_ways((v[0] + up.astype(F32)).astype(BF16), (v[1] + down.astype(F32)).astype(BF16), "z")
    small = small + send(small, "c", 1)
    small = small + send(small, "xl", 1)
    total = blocks(0)[0]
    up, down, small, total = tie((up, down, small, total))
    total = (total + (up.astype(F32) + down.astype(F32))).reshape(2, 128, CH)
    stay = lax.dynamic_index_in_dim(total, xl, 0, keepdims=False)
    leave = lax.dynamic_index_in_dim(total, 1 - xl, 0, keepdims=False)
    small, leave = tie((small, leave))
    arrived = send(leave, "xl", 1)
    for mask in (1, 2, 4):
        small = small + swap(small, "z", mask)
    arrived, = tie((arrived,), small)
    grad_weight = stay + arrived
    return (dx, dz, db[:, None], dc[:, None], ddt, small[8, :HEADS], small[9, :HEADS],
            small[:8].reshape(CH), grad_weight)


def solution(mesh):
    fine = jax.sharding.Mesh(mesh.devices.reshape(tuple(AXES.values())), tuple(AXES))
    part = P(DP, TP)
    part3 = P(DP, TP, None)
    head = P(TP)
    return jax.shard_map(
        on_device,
        mesh=fine,
        in_specs=(P(DP + TP, None), part, part, part3, part3, part, head, head, head, part),
        out_specs=(part, part, part3, part3, part, head, head, head, part),
        check_vma=False,
    )
```

```python
import jax
import jax.numpy as jnp
from jax import lax
from jax.experimental import pallas as pl
from jax.experimental.pallas import tpu as pltpu
from jax.sharding import PartitionSpec as P

F32, BF16 = jnp.float32, jnp.bfloat16
HEADS = 16
SPAN = 256
TOK = 512
CH = 1024
HALF = 128
LOG2E = 1.4426950408889634
BIG = 126.0
VMEM_LIMIT = 48 * 1024 * 1024
SMALL = pl.CostEstimate(flops=1000, bytes_accessed=1000, transcendentals=0)


def dot(a, b):
    return jnp.dot(a, b, preferred_element_type=F32)


def dot_nt(a, b):
    return lax.dot_general(a, b, (((1,), (1,)), ((), ())), preferred_element_type=F32)


def split2(v):
    hi = v.astype(BF16)
    return hi, (v - hi.astype(F32)).astype(BF16)


def dot3(a, b, fn):
    ah, al = split2(a)
    bh, bl = split2(b)
    return fn(ah, bh) + (fn(ah, bl) + fn(al, bh))


def spread_matrix(width):
    row = lax.broadcasted_iota(jnp.int32, (128, HEADS * width), 0)
    col = lax.broadcasted_iota(jnp.int32, (128, HEADS * width), 1)
    return jnp.where((row < 48) & ((row & 15) == col // width), 1.0, 0.0).astype(BF16)


def parts3(v):
    lane = lax.broadcasted_iota(jnp.int32, v.shape, 1)
    v = jnp.where(lane < HEADS, v, 0.0)
    one = v.astype(BF16).astype(F32)
    rest = v - one
    two = rest.astype(BF16).astype(F32)
    three = rest - two
    return (one + pltpu.roll(two, 16, 1) + pltpu.roll(three, 32, 1)).astype(BF16)


def cumulate(tri, v):
    one = v.astype(BF16)
    rest = v - one.astype(F32)
    two = rest.astype(BF16)
    three = (rest - two.astype(F32)).astype(BF16)
    return dot(tri, one) + (dot(tri, two) + dot(tri, three))


def triangle(n, lower):
    row = lax.broadcasted_iota(jnp.int32, (n, n), 0)
    col = lax.broadcasted_iota(jnp.int32, (n, n), 1)
    return jnp.where(row >= col if lower else row <= col, 1.0, 0.0).astype(BF16)


def prepare(dt_ref, rate_ref, pad_ref, ratepad_ref):
    pad_ref[...] = jnp.ones((TOK, 128), F32)
    pad_ref[:, :HEADS] = dt_ref[...]
    ratepad_ref[...] = jnp.zeros((8, 128), F32)
    ratepad_ref[0:1, :HEADS] = rate_ref[...]
    rate = -jnp.exp(ratepad_ref[0:1, :])
    tri = triangle(SPAN, True)
    cums, rs = [], []
    for k in range(2):
        dt = pad_ref[k * SPAN:(k + 1) * SPAN, :]
        cum = cumulate(tri, dt * (rate * LOG2E))
        cums.append(cum)
        rs.append(jnp.log2(dt) - cum)
    return rate, cums, rs


def fwd_kernel(x_ref, z_ref, b_ref, c_ref, dt_ref, rate_ref, skip_ref, gain_ref,
               ys_ref, n_ref, pad_ref, ratepad_ref, cexp_ref, rt_ref, s_ref, coef_ref):
    rate, cums, rs = prepare(dt_ref, rate_ref, pad_ref, ratepad_ref)
    wide = spread_matrix(HALF)
    narrow = spread_matrix(64)
    row = lax.broadcasted_iota(jnp.int32, (SPAN, SPAN), 0)
    col = lax.broadcasted_iota(jnp.int32, (SPAN, SPAN), 1)
    ratepad_ref[0:1, :HEADS] = skip_ref[...]
    skip = ratepad_ref[0:1, :]
    for k in range(2):
        rows = slice(k * SPAN, (k + 1) * SPAN)
        cexp_ref[rows, :] = dot(parts3(cums[k]), wide)
        rt_ref[k] = rs[k].T
        bk, ck = b_ref[rows, :], c_ref[rows, :]
        s_ref[k] = jnp.where(row > col, dot_nt(ck, bk), 0.0)
        diag = jnp.sum(bk.astype(F32) * ck.astype(F32), axis=1, keepdims=True)
        coef_ref[rows, :] = dot(parts3(diag * pad_ref[rows, :] + skip), narrow)
    lane = lax.broadcasted_iota(jnp.int32, (SPAN, 128), 1)

    def pair(hp, _):
        cols = pl.ds(pl.multiple_of(hp * 128, 128), 128)
        for k in range(2):
            rows = slice(k * SPAN, (k + 1) * SPAN)
            xp = x_ref[rows, cols]
            tops, bots = [], []
            for half in range(2):
                h = hp * 2 + half
                rrow = rt_ref[k, pl.ds(h, 1), :]
                hcols = pl.ds(pl.multiple_of(h * 128, 128), 128)
                top = cexp_ref[k * SPAN:k * SPAN + HALF, hcols]
                bot = cexp_ref[k * SPAN + HALF:(k + 1) * SPAN, hcols]
                wt = s_ref[k, :HALF, :HALF] * jnp.exp2(jnp.minimum(top + rrow[:, :HALF], BIG))
                wb = s_ref[k, HALF:, :] * jnp.exp2(
                    jnp.minimum(jnp.concatenate([bot, bot], axis=1) + rrow, BIG))
                tops += split2(wt)
                bots += split2(wb)
            yt = dot(jnp.concatenate(tops, axis=0), xp[:HALF])
            yb = dot(jnp.concatenate(bots, axis=0), xp)
            ys = [jnp.concatenate([v[256 * h:256 * h + 128] + v[256 * h + 128:256 * h + 256] for v in (yt, yb)], axis=0)
                  for h in range(2)]
            ys_ref[rows, cols] = jnp.where(lane < 64, ys[0], ys[1])
        return 0

    lax.fori_loop(0, 8, pair, 0)

    s10 = dot_nt(c_ref[SPAN:, :], b_ref[:SPAN, :])
    qdt = parts3(jnp.exp2(cums[0][SPAN - 1:SPAN, :] + rs[0]))
    p = parts3(jnp.exp2(cums[1]))
    for j in range(4):
        cols = slice(j * 256, (j + 1) * 256)
        xq = dot(qdt, narrow[:, cols]) * x_ref[:SPAN, cols].astype(F32)
        ys_ref[SPAN:, cols] += dot(p, narrow[:, cols]) * dot3(s10, xq, dot)

    gain = gain_ref[...]

    def norm(i, _):
        rows = pl.ds(pl.multiple_of(i * 32, 32), 32)
        z = z_ref[rows, :].astype(F32)
        y = ys_ref[rows, :] + coef_ref[rows, :] * x_ref[rows, :].astype(F32)
        gated = y * (z / (1.0 + jnp.exp(-z)))
        inv = lax.rsqrt(jnp.mean(gated * gated, axis=1, keepdims=True) + 1e-05)
        n_ref[rows, :] = (gated * inv * gain).astype(BF16)
        return 0

    lax.fori_loop(0, TOK // 32, norm, 0)


def bwd_kernel(u_ref, ys_ref, x_ref, z_ref, b_ref, c_ref, dt_ref, rate_ref, skip_ref, gain_ref,
               dx_ref, dz_ref, db_ref, dc_ref, ddt_ref, small_ref,
               pad_ref, ratepad_ref, rexp_ref, ct_ref, s_ref, coef_ref, dy_ref, dxs_ref, ds_ref, dg_ref):
    rate, cums, rs = prepare(dt_ref, rate_ref, pad_ref, ratepad_ref)
    wide = spread_matrix(HALF)
    narrow = spread_matrix(64)
    row = lax.broadcasted_iota(jnp.int32, (SPAN, SPAN), 0)
    col = lax.broadcasted_iota(jnp.int32, (SPAN, SPAN), 1)
    ratepad_ref[0:1, :HEADS] = skip_ref[...]
    skip = ratepad_ref[0:1, :]
    diags = []
    for k in range(2):
        rows = slice(k * SPAN, (k + 1) * SPAN)
        rexp_ref[rows, :] = dot(parts3(rs[k]), wide)
        ct_ref[k] = cums[k].T
        bk, ck = b_ref[rows, :], c_ref[rows, :]
        s_ref[k] = jnp.where(row < col, dot_nt(bk, ck), 0.0)
        diag = jnp.sum(bk.astype(F32) * ck.astype(F32), axis=1, keepdims=True)
        diags.append(diag)
        coef_ref[rows, :] = dot(parts3(diag * pad_ref[rows, :] + skip), narrow)

    gain = gain_ref[...]
    dg_ref[...] = jnp.zeros((8, CH), F32)

    def gate(i, _):
        rows = pl.ds(pl.multiple_of(i * 32, 32), 32)
        z = z_ref[rows, :].astype(F32)
        y = ys_ref[rows, :] + coef_ref[rows, :] * x_ref[rows, :].astype(F32)
        sig = 1.0 / (1.0 + jnp.exp(-z))
        sz = z * sig
        gated = y * sz
        inv = lax.rsqrt(jnp.mean(gated * gated, axis=1, keepdims=True) + 1e-05)
        unit = gated * inv
        u = u_ref[rows, :]
        ug = u * unit
        dg_ref[...] += (ug[0:8] + ug[8:16]) + (ug[16:24] + ug[24:32])
        v = u * gain
        dgated = inv * (v - unit * jnp.mean(v * unit, axis=1, keepdims=True))
        dy_ref[rows, :] = dgated * sz
        dz_ref[rows, :] = (dgated * y * (sig * (1.0 + z * (1.0 - sig)))).astype(BF16)
        return 0

    lax.fori_loop(0, TOK // 32, gate, 0)

    ds_ref[...] = jnp.zeros((2, SPAN, SPAN), F32)
    lane = lax.broadcasted_iota(jnp.int32, (SPAN, 128), 1)

    def pair(hp, _):
        cols = pl.ds(pl.multiple_of(hp * 128, 128), 128)
        for k in range(2):
            rows = slice(k * SPAN, (k + 1) * SPAN)
            xp = x_ref[rows, cols].astype(F32)
            dh, dl = split2(dy_ref[rows, cols])
            dhl = jnp.concatenate([dh, dl], axis=1)
            xx = []
            for half in range(2):
                xm = jnp.where((lane < 64) if half == 0 else (lane >= 64), xp, 0.0).astype(BF16)
                xx.append(jnp.concatenate([xm, xm], axis=1))
            gts = dot_nt(jnp.concatenate([v[:HALF] for v in xx], axis=0), dhl)
            gbs = dot_nt(jnp.concatenate([v[HALF:] for v in xx], axis=0), dhl[HALF:])
            ths, tls, bhs, bls = [], [], [], []
            dst, dsb = ds_ref[k, :HALF, :], ds_ref[k, HALF:, HALF:]
            for half in range(2):
                h = hp * 2 + half
                part = slice(half * HALF, (half + 1) * HALF)
                crow = ct_ref[k, pl.ds(h, 1), :]
                hcols = pl.ds(pl.multiple_of(h * 128, 128), 128)
                top = rexp_ref[k * SPAN:k * SPAN + HALF, hcols]
                bot = rexp_ref[k * SPAN + HALF:(k + 1) * SPAN, hcols]
                et = jnp.exp2(jnp.minimum(jnp.concatenate([top, top], axis=1) + crow, BIG))
                eb = jnp.exp2(jnp.minimum(bot + crow[:, HALF:], BIG))
                dst = dst + et * gts[part]
                dsb = dsb + eb * gbs[part]
                hi, lo = split2(s_ref[k, :HALF, :] * et)
                ths.append(hi)
                tls.append(lo)
                hi, lo = split2(s_ref[k, HALF:, HALF:] * eb)
                bhs.append(hi)
                bls.append(lo)
            ds_ref[k, :HALF, :] = dst
            ds_ref[k, HALF:, HALF:] = dsb
            ot = dot(jnp.concatenate(ths, axis=0), dhl)
            ob = dot(jnp.concatenate(bhs, axis=0), dhl[HALF:])
            ot = (ot[:, :128] + ot[:, 128:]) + dot(jnp.concatenate(tls, axis=0), dh)
            ob = (ob[:, :128] + ob[:, 128:]) + dot(jnp.concatenate(bls, axis=0), dh[HALF:])
            outs = [jnp.concatenate([v[h * HALF:(h + 1) * HALF] for v in (ot, ob)], axis=0) for h in range(2)]
            dxs_ref[rows, cols] = jnp.where(lane < 64, outs[0], outs[1])
        return 0

    lax.fori_loop(0, 8, pair, 0)

    st = dot_nt(b_ref[:SPAN, :], c_ref[SPAN:, :])
    qdt = parts3(jnp.exp2(cums[0][SPAN - 1:SPAN, :] + rs[0]))
    p = parts3(jnp.exp2(cums[1]))
    dst = jnp.zeros((SPAN, SPAN), F32)
    for j in range(4):
        cols = slice(j * 256, (j + 1) * 256)
        qx = dot(qdt, narrow[:, cols])
        xq = qx * x_ref[:SPAN, cols].astype(F32)
        pdy = dot(p, narrow[:, cols]) * dy_ref[SPAN:, cols]
        dxs_ref[:SPAN, cols] += qx * dot3(st, pdy, dot)
        dst = dst + dot3(xq, pdy, dot_nt)

    seg_row = lax.broadcasted_iota(jnp.int32, (CH, 128), 0)
    seg_col = lax.broadcasted_iota(jnp.int32, (CH, 128), 1)
    seg = jnp.where(seg_row // 64 == seg_col, 1.0, 0.0).astype(BF16)

    def heads_sum(v):
        hi, lo = split2(v)
        return dot(hi, seg) + dot(lo, seg)

    tri = triangle(SPAN, False)
    later = jnp.zeros((1, 128), F32)
    rate_sum = jnp.zeros((1, 128), F32)
    skip_sum = jnp.zeros((1, 128), F32)
    for k in (1, 0):
        rows = slice(k * SPAN, (k + 1) * SPAN)
        xf = x_ref[rows, :].astype(F32)
        dy = dy_ref[rows, :]
        dxs = dxs_ref[rows, :]
        kx = heads_sum(dy * xf)
        r = heads_sum(dy * ys_ref[rows, :])
        q = heads_sum(xf * dxs)
        suffix = cumulate(tri, r - q) + later
        later = suffix[0:1, :]
        dt = pad_ref[rows, :]
        ddt = q / dt + kx * diags[k] + rate * suffix
        ddt_ref[rows, :] = ddt[:, :HEADS]
        rate_sum = rate_sum + rate * jnp.sum(dt * suffix, axis=0, keepdims=True)
        skip_sum = skip_sum + jnp.sum(kx, axis=0, keepdims=True)
        sd = jnp.sum(dt * kx, axis=1, keepdims=True)
        dsk = jnp.where(row < col, ds_ref[k], 0.0)
        bk, ck = b_ref[rows, :], c_ref[rows, :]
        sh, sl = split2(dsk)
        db = dot(sh, ck) + dot(sl, ck) + sd * ck.astype(F32)
        sh, sl = split2(dsk.T)
        dc = dot(sh, bk) + dot(sl, bk) + sd * bk.astype(F32)
        if k == 0:
            oh, ol = split2(dst)
            db = db + dot(oh, c_ref[SPAN:, :]) + dot(ol, c_ref[SPAN:, :])
        else:
            oh, ol = split2(dst.T)
            dc = dc + dot(oh, b_ref[:SPAN, :]) + dot(ol, b_ref[:SPAN, :])
        db_ref[rows, :] = db.astype(BF16)
        dc_ref[rows, :] = dc.astype(BF16)
        dx_ref[rows, :] = (dxs + coef_ref[rows, :] * dy).astype(BF16)

    dg = jnp.sum(dg_ref[...], axis=0, keepdims=True)
    for j in range(8):
        small_ref[j:j + 1, :] = dg[:, j * 128:(j + 1) * 128]
    small_ref[8:9, :] = rate_sum
    small_ref[9:10, :] = skip_sum
    small_ref[10:16, :] = jnp.zeros((6, 128), F32)


def scan_forward(x, z, b, c, dt, rate, skip, gain):
    return pl.pallas_call(
        fwd_kernel,
        out_shape=(jax.ShapeDtypeStruct((TOK, CH), F32), jax.ShapeDtypeStruct((TOK, CH), BF16)),
        scratch_shapes=[
            pltpu.VMEM((TOK, 128), F32),
            pltpu.VMEM((8, 128), F32),
            pltpu.VMEM((TOK, HEADS * HALF), F32),
            pltpu.VMEM((2, 128, SPAN), F32),
            pltpu.VMEM((2, SPAN, SPAN), F32),
            pltpu.VMEM((TOK, CH), F32),
        ],
        compiler_params=pltpu.CompilerParams(vmem_limit_bytes=VMEM_LIMIT),
        cost_estimate=SMALL,
        name="scan_forward",
    )(x, z, b, c, dt, rate, skip, gain)


def scan_backward(u, ys, x, z, b, c, dt, rate, skip, gain):
    return pl.pallas_call(
        bwd_kernel,
        out_shape=(
            jax.ShapeDtypeStruct((TOK, CH), BF16),
            jax.ShapeDtypeStruct((TOK, CH), BF16),
            jax.ShapeDtypeStruct((TOK, 128), BF16),
            jax.ShapeDtypeStruct((TOK, 128), BF16),
            jax.ShapeDtypeStruct((TOK, HEADS), F32),
            jax.ShapeDtypeStruct((16, 128), F32),
        ),
        scratch_shapes=[
            pltpu.VMEM((TOK, 128), F32),
            pltpu.VMEM((8, 128), F32),
            pltpu.VMEM((TOK, HEADS * HALF), F32),
            pltpu.VMEM((2, 128, SPAN), F32),
            pltpu.VMEM((2, SPAN, SPAN), F32),
            pltpu.VMEM((TOK, CH), F32),
            pltpu.VMEM((TOK, CH), F32),
            pltpu.VMEM((TOK, CH), F32),
            pltpu.VMEM((2, SPAN, SPAN), F32),
            pltpu.VMEM((8, CH), F32),
        ],
        compiler_params=pltpu.CompilerParams(vmem_limit_bytes=VMEM_LIMIT),
        cost_estimate=SMALL,
        name="scan_backward",
    )(u, ys, x, z, b, c, dt, rate, skip, gain)


AXES = {"z": 8, "xl": 2, "c": 2, "y": 4, "xh": 2}
DP = ("z", "xl", "c")
TP = ("y", "xh")


def send(v, axis, shift):
    n = AXES[axis]
    return lax.ppermute(v, axis, [(i, (i + shift) % n) for i in range(n)])


def swap(v, axis, mask):
    return lax.ppermute(v, axis, [(i, i ^ mask) for i in range(AXES[axis])])


def both_ways(up, down, axis):
    return send(up, axis, 1), send(down, axis, -1)


def tie(values, *first):
    return lax.optimization_barrier((tuple(values),) + tuple(first))[0]


def shuffle(name, shapes, plan, scalars, *arrays):
    count = len(plan([0] * len(scalars)))

    def kernel(s_ref, *refs):
        src, dst, sem = refs[:len(arrays)], refs[len(arrays):-1], refs[-1]
        copies = [
            pltpu.make_async_copy(src[i].at[a], dst[o].at[b], sem.at[k])
            for k, (i, a, o, b) in enumerate(plan([s_ref[j] for j in range(len(scalars))]))
        ]
        for copy in copies:
            copy.start()
        for copy in copies:
            copy.wait()

    return pl.pallas_call(
        kernel,
        out_shape=tuple(jax.ShapeDtypeStruct(s, BF16) for s in shapes),
        in_specs=[pl.BlockSpec(memory_space=pltpu.SMEM)] + [pl.BlockSpec(memory_space=pl.ANY)] * len(arrays),
        out_specs=tuple(pl.BlockSpec(memory_space=pltpu.VMEM) for _ in shapes),
        scratch_shapes=[pltpu.SemaphoreType.DMA((count,))],
        cost_estimate=SMALL,
        name=name,
    )(jnp.stack([s.astype(jnp.int32) for s in scalars]), *arrays)


def own_first(rows, core):
    def kernel(core_ref, in_ref, out_ref):
        for j in range(16):
            even = in_ref[:, 256 * j:256 * j + 128]
            odd = in_ref[:, 256 * j + 128:256 * j + 256]
            first = core_ref[0] == 0
            out_ref[:, 128 * j:128 * j + 128] = jnp.where(first, even, odd)
            out_ref[:, 2048 + 128 * j:2048 + 128 * j + 128] = jnp.where(first, odd, even)

    return pl.pallas_call(
        kernel,
        out_shape=jax.ShapeDtypeStruct(rows.shape, rows.dtype),
        in_specs=[pl.BlockSpec(memory_space=pltpu.SMEM), pl.BlockSpec(memory_space=pltpu.VMEM)],
        out_specs=pl.BlockSpec(memory_space=pltpu.VMEM),
        cost_estimate=SMALL,
        name="own_first",
    )(core.astype(jnp.int32).reshape(1), rows)


def at_rows(start, size):
    return (pl.ds(pl.multiple_of(start, 32), size), slice(None)) if not isinstance(start, int) else (slice(start, start + size), slice(None))


def place_tokens(yi, xh, first, *pieces):
    parts = ((0, 64, 0, 0, 0), (1, 64, 0, 1, 0), (2, 64, 3, 0, 0), (3, 64, 3, 1, 0), (4, 64, 1, 0, 0),
             (5, 64, 1, 1, 0), (6, 64, 2, 0, 0), (7, 32, 2, 1, 0), (8, 32, 2, 1, 32))

    def plan(s):
        moves = []
        for piece, size, turn, other, offset in parts:
            start = ((s[0] + turn) % 4) * 128 + (1 - s[1] if other else s[1]) * 64 + offset
            moves.append((piece, (slice(None), slice(first, first + 2048)), 0, at_rows(start, size)))
        return moves

    return shuffle("place_tokens", [(TOK, 2048)], plan, (yi, xh), *pieces)[0]


def place_weights(zi, xl, *arrays):
    parts = (
        (0, 0, 128, 0, 0, 0), (1, 0, 128, 0, 1, 0),
        (2, 0, 128, 7, 0, 0), (3, 0, 128, 1, 0, 0),
        (4, 0, 128, 7, 1, 0), (4, 128, 128, 6, 0, 0), (5, 0, 128, 2, 0, 0), (5, 128, 128, 1, 1, 0),
        (6, 0, 128, 5, 0, 0), (7, 0, 128, 3, 0, 0), (8, 0, 64, 4, 0, 0), (9, 0, 64, 4, 0, 64),
        (10, 0, 128, 6, 1, 0), (10, 128, 128, 2, 1, 0), (10, 256, 128, 5, 1, 0), (10, 384, 128, 3, 1, 0),
        (11, 0, 128, 4, 1, 0),
    )

    def plan(s):
        moves = []
        for array, first, size, turn, other, offset in parts:
            block = ((s[0] + turn) % 8) * 2 + (1 - s[1] if other else s[1])
            moves.append((array, at_rows(first, size), 0, at_rows(block * 128 + offset, size)))
        return moves

    return shuffle("place_weights", [(2048, CH)], plan, (zi, xl), *arrays)[0]


def weight_blocks(zi, shifts, keep, theirs, normed, normed_other):
    def kernel(at_ref, a_ref, b_ref, n_ref, m_ref, out_ref):
        def term(r, n):
            return lax.dot_general(r[...], n[...], (((0,), (0,)), ((), ())), preferred_element_type=F32)

        out_ref[0] = term(a_ref, n_ref) + term(b_ref, m_ref)

    columns = pl.BlockSpec((TOK, 256), lambda i, at: (0, at[i]))
    whole = pl.BlockSpec((TOK, CH), lambda i, at: (0, 0))
    return pl.pallas_call(
        kernel,
        grid_spec=pltpu.PrefetchScalarGridSpec(
            num_scalar_prefetch=1,
            grid=(len(shifts),),
            in_specs=[columns, columns, whole, whole],
            out_specs=pl.BlockSpec((1, 256, CH), lambda i, at: (i, 0, 0)),
        ),
        out_shape=jax.ShapeDtypeStruct((len(shifts), 256, CH), F32),
        compiler_params=pltpu.CompilerParams(vmem_limit_bytes=VMEM_LIMIT),
        cost_estimate=SMALL,
        name="weight_blocks",
    )(jnp.stack([(zi + k + 8) % 8 for k in shifts]).astype(jnp.int32), keep, theirs, normed, normed_other)


def back_project(keep, give, w_keep, w_give):
    def kernel(a_ref, b_ref, v_ref, w_ref, out_ref):
        out_ref[...] = dot(a_ref[...], v_ref[...]) + dot(b_ref[...], w_ref[...])

    rows = pl.BlockSpec((TOK, 2048), lambda i: (0, 0))
    columns = pl.BlockSpec((2048, 256), lambda i: (0, i))
    return pl.pallas_call(
        kernel,
        grid=(4,),
        in_specs=[rows, rows, columns, columns],
        out_specs=pl.BlockSpec((TOK, 256), lambda i: (0, i)),
        out_shape=jax.ShapeDtypeStruct((TOK, CH), F32),
        compiler_params=pltpu.CompilerParams(vmem_limit_bytes=VMEM_LIMIT),
        cost_estimate=SMALL,
        name="back_project",
    )(keep, give, w_keep, w_give)


def combine(v, up, down):
    width = up.shape[1]
    at = CH - width

    def kernel(v_ref, up_ref, down_ref, up_out, down_out):
        if at:
            up_out[:, :at] = v_ref[0, :, :at].astype(BF16)
            down_out[:, width:] = v_ref[1, :, width:].astype(BF16)
        up_out[:, at:] = (v_ref[0, :, at:] + up_ref[...].astype(F32)).astype(BF16)
        down_out[:, :width] = (v_ref[1, :, :width] + down_ref[...].astype(F32)).astype(BF16)

    part = pl.BlockSpec((64, width), lambda i: (i, 0))
    full = pl.BlockSpec((64, CH), lambda i: (i, 0))
    return pl.pallas_call(
        kernel,
        grid=(4,),
        in_specs=[pl.BlockSpec((2, 64, CH), lambda i: (0, i, 0)), part, part],
        out_specs=(full, full),
        out_shape=(jax.ShapeDtypeStruct((256, CH), BF16),) * 2,
        cost_estimate=SMALL,
        name="combine",
    )(v, up, down)


def on_device(grad_out, x, z, b, c, dt, rate, skip, gain, w_out):
    zi, xl, core, yi, xh = (lax.axis_index(a) for a in ("z", "xl", "c", "y", "xh"))
    scan = (x, z, b.reshape(TOK, 128), c.reshape(TOK, 128), dt, rate[None], skip[None], gain[None])

    own = own_first(grad_out, core)
    below, above = both_ways(own, own, "y")
    other = send(own, "xh", 1)
    b1, a1 = both_ways(w_out, w_out, "z")
    w_late, late = tie((w_out, scan[6]), b1)
    w_other = send(w_late, "xl", 1)
    ys, normed = scan_forward(*scan[:6], late, scan[7])
    below, above, other, w_other, b1, a1, normed = tie((below, above, other, w_other, b1, a1, normed))

    b_other = send(other, "y", 1)
    far_own = send(above, "y", -1)
    a_other = send(above, "xh", 1)
    b2, a2 = both_ways(jnp.concatenate([w_other, b1], axis=0), jnp.concatenate([a1, w_other], axis=0), "z")
    b_other, far_own, a_other, b2, a2, normed = tie((b_other, far_own, a_other, b2, a2, normed))

    far_b, far_a = both_ways(b_other[:32], a_other[32:], "y")
    normed_other = send(normed, "c", 1)
    b3, a3 = both_ways(b2[128:], a2[:128], "z")
    far_b, far_a, normed_other, b3, a3 = tie((far_b, far_a, normed_other, b3, a3))
    pieces = (own, other, below, b_other, above, a_other, far_own, far_b, far_a)
    give = place_tokens(yi, xh, 2048, *pieces)
    theirs = send(give, "c", 1)
    keep = place_tokens(yi, xh, 0, *tie(pieces, give))
    x3 = send(jnp.concatenate([b2[128:], a2[:128], b3, a3], axis=0), "xl", 1)
    theirs, keep = tie((theirs, keep))

    def blocks(*shifts):
        return weight_blocks(zi, shifts, keep, theirs, normed, normed_other)

    half = CH // 2
    far = blocks(4)[0].astype(BF16)
    up, down = both_ways(far[:, half:], far[:, :half], "z")
    b4, a4 = both_ways(b3[:64], a3[64:], "z")
    v = blocks(3, -3)
    up, down, v, x3, b4, a4 = tie((up, down, v, x3, b4, a4))

    up, down = both_ways(*combine(v, up, down), "z")
    x4 = send(jnp.concatenate([b4, a4], axis=0), "xl", 1)
    v = blocks(2, -2)
    w_keep = place_weights(zi, xl, w_out, w_other, b1, a1, b2, a2, b3, a3, b4, a4, x3, x4)
    up, down, v, w_keep = tie((up, down, v, w_keep))

    up, down = both_ways(*combine(v, up, down), "z")
    w_give = send(w_keep, "c", 1)
    v = blocks(1, -1)
    upstream = back_project(keep, give, w_keep, w_give)
    up, down, v, upstream = tie((up, down, v, upstream))

    up, down = both_ways(*combine(v, up, down), "z")
    dx, dz, db, dc, ddt, small = scan_backward(upstream, ys, *scan)
    total = blocks(0)[0]
    up, down, small, total = tie((up, down, small, total))
    small = small + send(small, "c", 1)
    total = (total + (up.astype(F32) + down.astype(F32))).reshape(2, 128, CH)
    stay = lax.dynamic_index_in_dim(total, xl, 0, keepdims=False)
    leave = lax.dynamic_index_in_dim(total, 1 - xl, 0, keepdims=False)
    small, leave = tie((small, leave))
    arrived = send(leave, "xl", 1)
    small = small + send(small, "xl", 1)
    for mask in (1, 2, 4):
        small = small + swap(small, "z", mask)
    arrived, = tie((arrived,), small)
    grad_weight = stay + arrived
    return (dx, dz, db[:, None], dc[:, None], ddt, small[8, :HEADS], small[9, :HEADS],
            small[:8].reshape(CH), grad_weight)


def solution(mesh):
    fine = jax.sharding.Mesh(mesh.devices.reshape(tuple(AXES.values())), tuple(AXES))
    part = P(DP, TP)
    part3 = P(DP, TP, None)
    head = P(TP)
    return jax.shard_map(
        on_device,
        mesh=fine,
        in_specs=(P(DP + TP, None), part, part, part3, part3, part, head, head, head, part),
        out_specs=(part, part, part3, part3, part, head, head, head, part),
        check_vma=False,
    )
```

```python
import jax
import jax.numpy as jnp
from jax import lax
from jax.experimental import pallas as pl
from jax.experimental.pallas import tpu as pltpu
from jax.sharding import PartitionSpec as P

F32, BF16 = jnp.float32, jnp.bfloat16
HEADS = 16
SPAN = 256
TOK = 512
CH = 1024
HALF = 128
LOG2E = 1.4426950408889634
BIG = 126.0
MIB = 1024 * 1024
SMALL = pl.CostEstimate(flops=1000, bytes_accessed=1000, transcendentals=0)


def dot(a, b):
    return jnp.dot(a, b, preferred_element_type=F32)


def dot_nt(a, b):
    return lax.dot_general(a, b, (((1,), (1,)), ((), ())), preferred_element_type=F32)


def split2(v):
    hi = v.astype(BF16)
    return hi, (v - hi.astype(F32)).astype(BF16)


def dot3(a, b, fn):
    ah, al = split2(a)
    bh, bl = split2(b)
    return fn(ah, bh) + (fn(ah, bl) + fn(al, bh))


def spread_matrix(width):
    row = lax.broadcasted_iota(jnp.int32, (128, HEADS * width), 0)
    col = lax.broadcasted_iota(jnp.int32, (128, HEADS * width), 1)
    return jnp.where((row < 48) & ((row & 15) == col // width), 1.0, 0.0).astype(BF16)


def parts3(v):
    lane = lax.broadcasted_iota(jnp.int32, v.shape, 1)
    v = jnp.where(lane < HEADS, v, 0.0)
    one = v.astype(BF16).astype(F32)
    rest = v - one
    two = rest.astype(BF16).astype(F32)
    three = rest - two
    return (one + pltpu.roll(two, 16, 1) + pltpu.roll(three, 32, 1)).astype(BF16)


def cumulate(tri, v):
    one = v.astype(BF16)
    rest = v - one.astype(F32)
    two = rest.astype(BF16)
    three = (rest - two.astype(F32)).astype(BF16)
    return dot(tri, one) + (dot(tri, two) + dot(tri, three))


def triangle(n, lower):
    row = lax.broadcasted_iota(jnp.int32, (n, n), 0)
    col = lax.broadcasted_iota(jnp.int32, (n, n), 1)
    return jnp.where(row >= col if lower else row <= col, 1.0, 0.0).astype(BF16)


def prepare(dt_ref, rate_ref, pad_ref, ratepad_ref):
    pad_ref[...] = jnp.ones((TOK, 128), F32)
    pad_ref[:, :HEADS] = dt_ref[...]
    ratepad_ref[...] = jnp.zeros((8, 128), F32)
    ratepad_ref[0:1, :HEADS] = rate_ref[...]
    rate = -jnp.exp(ratepad_ref[0:1, :])
    tri = triangle(SPAN, True)
    cums, rs = [], []
    for k in range(2):
        dt = pad_ref[k * SPAN:(k + 1) * SPAN, :]
        cum = cumulate(tri, dt * (rate * LOG2E))
        cums.append(cum)
        rs.append(jnp.log2(dt) - cum)
    return rate, cums, rs


def fwd_kernel(x_ref, z_ref, b_ref, c_ref, dt_ref, rate_ref, skip_ref, gain_ref,
               ys_ref, n_ref, pad_ref, ratepad_ref, cexp_ref, rt_ref, s_ref, coef_ref):
    rate, cums, rs = prepare(dt_ref, rate_ref, pad_ref, ratepad_ref)
    wide = spread_matrix(HALF)
    narrow = spread_matrix(64)
    row = lax.broadcasted_iota(jnp.int32, (SPAN, SPAN), 0)
    col = lax.broadcasted_iota(jnp.int32, (SPAN, SPAN), 1)
    ratepad_ref[0:1, :HEADS] = skip_ref[...]
    skip = ratepad_ref[0:1, :]
    for k in range(2):
        rows = slice(k * SPAN, (k + 1) * SPAN)
        cexp_ref[rows, :] = dot(parts3(cums[k]), wide)
        rt_ref[k] = rs[k].T
        bk, ck = b_ref[rows, :], c_ref[rows, :]
        s_ref[k] = jnp.where(row > col, dot_nt(ck, bk), 0.0)
        diag = jnp.sum(bk.astype(F32) * ck.astype(F32), axis=1, keepdims=True)
        coef_ref[rows, :] = dot(parts3(diag * pad_ref[rows, :] + skip), narrow)
    lane = lax.broadcasted_iota(jnp.int32, (SPAN, 128), 1)

    def pair(hp, _):
        cols = pl.ds(pl.multiple_of(hp * 128, 128), 128)
        for k in range(2):
            rows = slice(k * SPAN, (k + 1) * SPAN)
            xp = x_ref[rows, cols]
            tops, bots = [], []
            for half in range(2):
                h = hp * 2 + half
                rrow = rt_ref[k, pl.ds(h, 1), :]
                hcols = pl.ds(pl.multiple_of(h * 128, 128), 128)
                top = cexp_ref[k * SPAN:k * SPAN + HALF, hcols]
                bot = cexp_ref[k * SPAN + HALF:(k + 1) * SPAN, hcols]
                wt = s_ref[k, :HALF, :HALF] * jnp.exp2(jnp.minimum(top + rrow[:, :HALF], BIG))
                wb = s_ref[k, HALF:, :] * jnp.exp2(
                    jnp.minimum(jnp.concatenate([bot, bot], axis=1) + rrow, BIG))
                tops += split2(wt)
                bots += split2(wb)
            yt = dot(jnp.concatenate(tops, axis=0), xp[:HALF])
            yb = dot(jnp.concatenate(bots, axis=0), xp)
            ys = [jnp.concatenate([v[256 * h:256 * h + 128] + v[256 * h + 128:256 * h + 256] for v in (yt, yb)], axis=0)
                  for h in range(2)]
            ys_ref[rows, cols] = jnp.where(lane < 64, ys[0], ys[1])
        return 0

    lax.fori_loop(0, 8, pair, 0)

    s10 = dot_nt(c_ref[SPAN:, :], b_ref[:SPAN, :])
    qdt = parts3(jnp.exp2(cums[0][SPAN - 1:SPAN, :] + rs[0]))
    p = parts3(jnp.exp2(cums[1]))
    for j in range(4):
        cols = slice(j * 256, (j + 1) * 256)
        xq = dot(qdt, narrow[:, cols]) * x_ref[:SPAN, cols].astype(F32)
        ys_ref[SPAN:, cols] += dot(p, narrow[:, cols]) * dot3(s10, xq, dot)

    gain = gain_ref[...]

    def norm(i, _):
        rows = pl.ds(pl.multiple_of(i * 32, 32), 32)
        z = z_ref[rows, :].astype(F32)
        y = ys_ref[rows, :] + coef_ref[rows, :] * x_ref[rows, :].astype(F32)
        gated = y * (z / (1.0 + jnp.exp(-z)))
        inv = lax.rsqrt(jnp.mean(gated * gated, axis=1, keepdims=True) + 1e-05)
        n_ref[rows, :] = (gated * inv * gain).astype(BF16)
        return 0

    lax.fori_loop(0, TOK // 32, norm, 0)


def bwd_kernel(u_ref, ys_ref, x_ref, z_ref, b_ref, c_ref, dt_ref, rate_ref, skip_ref, gain_ref,
               dx_ref, dz_ref, db_ref, dc_ref, ddt_ref, small_ref,
               pad_ref, ratepad_ref, rexp_ref, ct_ref, s_ref, coef_ref, dy_ref, dxs_ref, ds_ref, dg_ref):
    rate, cums, rs = prepare(dt_ref, rate_ref, pad_ref, ratepad_ref)
    wide = spread_matrix(HALF)
    narrow = spread_matrix(64)
    row = lax.broadcasted_iota(jnp.int32, (SPAN, SPAN), 0)
    col = lax.broadcasted_iota(jnp.int32, (SPAN, SPAN), 1)
    ratepad_ref[0:1, :HEADS] = skip_ref[...]
    skip = ratepad_ref[0:1, :]
    diags = []
    for k in range(2):
        rows = slice(k * SPAN, (k + 1) * SPAN)
        rexp_ref[rows, :] = dot(parts3(rs[k]), wide)
        ct_ref[k] = cums[k].T
        bk, ck = b_ref[rows, :], c_ref[rows, :]
        s_ref[k] = jnp.where(row < col, dot_nt(bk, ck), 0.0)
        diag = jnp.sum(bk.astype(F32) * ck.astype(F32), axis=1, keepdims=True)
        diags.append(diag)
        coef_ref[rows, :] = dot(parts3(diag * pad_ref[rows, :] + skip), narrow)

    gain = gain_ref[...]
    dg_ref[...] = jnp.zeros((8, CH), F32)

    def gate(i, _):
        rows = pl.ds(pl.multiple_of(i * 32, 32), 32)
        z = z_ref[rows, :].astype(F32)
        y = ys_ref[rows, :] + coef_ref[rows, :] * x_ref[rows, :].astype(F32)
        sig = 1.0 / (1.0 + jnp.exp(-z))
        sz = z * sig
        gated = y * sz
        inv = lax.rsqrt(jnp.mean(gated * gated, axis=1, keepdims=True) + 1e-05)
        unit = gated * inv
        u = u_ref[rows, :]
        ug = u * unit
        dg_ref[...] += (ug[0:8] + ug[8:16]) + (ug[16:24] + ug[24:32])
        v = u * gain
        dgated = inv * (v - unit * jnp.mean(v * unit, axis=1, keepdims=True))
        dy_ref[rows, :] = dgated * sz
        dz_ref[rows, :] = (dgated * y * (sig * (1.0 + z * (1.0 - sig)))).astype(BF16)
        return 0

    lax.fori_loop(0, TOK // 32, gate, 0)

    ds_ref[...] = jnp.zeros((2, SPAN, SPAN), F32)
    lane = lax.broadcasted_iota(jnp.int32, (SPAN, 128), 1)

    def pair(hp, _):
        cols = pl.ds(pl.multiple_of(hp * 128, 128), 128)
        for k in range(2):
            rows = slice(k * SPAN, (k + 1) * SPAN)
            xp = x_ref[rows, cols].astype(F32)
            dh, dl = split2(dy_ref[rows, cols])
            dhl = jnp.concatenate([dh, dl], axis=1)
            xx = []
            for half in range(2):
                xm = jnp.where((lane < 64) if half == 0 else (lane >= 64), xp, 0.0).astype(BF16)
                xx.append(jnp.concatenate([xm, xm], axis=1))
            gts = dot_nt(jnp.concatenate([v[:HALF] for v in xx], axis=0), dhl)
            gbs = dot_nt(jnp.concatenate([v[HALF:] for v in xx], axis=0), dhl[HALF:])
            ths, tls, bhs, bls = [], [], [], []
            dst, dsb = ds_ref[k, :HALF, :], ds_ref[k, HALF:, HALF:]
            for half in range(2):
                h = hp * 2 + half
                part = slice(half * HALF, (half + 1) * HALF)
                crow = ct_ref[k, pl.ds(h, 1), :]
                hcols = pl.ds(pl.multiple_of(h * 128, 128), 128)
                top = rexp_ref[k * SPAN:k * SPAN + HALF, hcols]
                bot = rexp_ref[k * SPAN + HALF:(k + 1) * SPAN, hcols]
                et = jnp.exp2(jnp.minimum(jnp.concatenate([top, top], axis=1) + crow, BIG))
                eb = jnp.exp2(jnp.minimum(bot + crow[:, HALF:], BIG))
                dst = dst + et * gts[part]
                dsb = dsb + eb * gbs[part]
                hi, lo = split2(s_ref[k, :HALF, :] * et)
                ths.append(hi)
                tls.append(lo)
                hi, lo = split2(s_ref[k, HALF:, HALF:] * eb)
                bhs.append(hi)
                bls.append(lo)
            ds_ref[k, :HALF, :] = dst
            ds_ref[k, HALF:, HALF:] = dsb
            ot = dot(jnp.concatenate(ths, axis=0), dhl)
            ob = dot(jnp.concatenate(bhs, axis=0), dhl[HALF:])
            ot = (ot[:, :128] + ot[:, 128:]) + dot(jnp.concatenate(tls, axis=0), dh)
            ob = (ob[:, :128] + ob[:, 128:]) + dot(jnp.concatenate(bls, axis=0), dh[HALF:])
            outs = [jnp.concatenate([v[h * HALF:(h + 1) * HALF] for v in (ot, ob)], axis=0) for h in range(2)]
            dxs_ref[rows, cols] = jnp.where(lane < 64, outs[0], outs[1])
        return 0

    lax.fori_loop(0, 8, pair, 0)

    st = dot_nt(b_ref[:SPAN, :], c_ref[SPAN:, :])
    qdt = parts3(jnp.exp2(cums[0][SPAN - 1:SPAN, :] + rs[0]))
    p = parts3(jnp.exp2(cums[1]))
    dst = jnp.zeros((SPAN, SPAN), F32)
    for j in range(4):
        cols = slice(j * 256, (j + 1) * 256)
        qx = dot(qdt, narrow[:, cols])
        xq = qx * x_ref[:SPAN, cols].astype(F32)
        pdy = dot(p, narrow[:, cols]) * dy_ref[SPAN:, cols]
        dxs_ref[:SPAN, cols] += qx * dot3(st, pdy, dot)
        dst = dst + dot3(xq, pdy, dot_nt)

    seg_row = lax.broadcasted_iota(jnp.int32, (CH, 128), 0)
    seg_col = lax.broadcasted_iota(jnp.int32, (CH, 128), 1)
    seg = jnp.where(seg_row // 64 == seg_col, 1.0, 0.0).astype(BF16)

    def heads_sum(v):
        hi, lo = split2(v)
        return dot(hi, seg) + dot(lo, seg)

    tri = triangle(SPAN, False)
    later = jnp.zeros((1, 128), F32)
    rate_sum = jnp.zeros((1, 128), F32)
    skip_sum = jnp.zeros((1, 128), F32)
    for k in (1, 0):
        rows = slice(k * SPAN, (k + 1) * SPAN)
        xf = x_ref[rows, :].astype(F32)
        dy = dy_ref[rows, :]
        dxs = dxs_ref[rows, :]
        kx = heads_sum(dy * xf)
        r = heads_sum(dy * ys_ref[rows, :])
        q = heads_sum(xf * dxs)
        suffix = cumulate(tri, r - q) + later
        later = suffix[0:1, :]
        dt = pad_ref[rows, :]
        ddt = q / dt + kx * diags[k] + rate * suffix
        ddt_ref[rows, :] = ddt[:, :HEADS]
        rate_sum = rate_sum + rate * jnp.sum(dt * suffix, axis=0, keepdims=True)
        skip_sum = skip_sum + jnp.sum(kx, axis=0, keepdims=True)
        sd = jnp.sum(dt * kx, axis=1, keepdims=True)
        dsk = jnp.where(row < col, ds_ref[k], 0.0)
        bk, ck = b_ref[rows, :], c_ref[rows, :]
        sh, sl = split2(dsk)
        db = dot(sh, ck) + dot(sl, ck) + sd * ck.astype(F32)
        sh, sl = split2(dsk.T)
        dc = dot(sh, bk) + dot(sl, bk) + sd * bk.astype(F32)
        if k == 0:
            oh, ol = split2(dst)
            db = db + dot(oh, c_ref[SPAN:, :]) + dot(ol, c_ref[SPAN:, :])
        else:
            oh, ol = split2(dst.T)
            dc = dc + dot(oh, b_ref[:SPAN, :]) + dot(ol, b_ref[:SPAN, :])
        db_ref[rows, :] = db.astype(BF16)
        dc_ref[rows, :] = dc.astype(BF16)
        dx_ref[rows, :] = (dxs + coef_ref[rows, :] * dy).astype(BF16)

    dg = jnp.sum(dg_ref[...], axis=0, keepdims=True)
    for j in range(8):
        small_ref[j:j + 1, :] = dg[:, j * 128:(j + 1) * 128]
    small_ref[8:9, :] = rate_sum
    small_ref[9:10, :] = skip_sum
    small_ref[10:16, :] = jnp.zeros((6, 128), F32)


def scan_forward(x, z, b, c, dt, rate, skip, gain):
    return pl.pallas_call(
        fwd_kernel,
        out_shape=(jax.ShapeDtypeStruct((TOK, CH), F32), jax.ShapeDtypeStruct((TOK, CH), BF16)),
        scratch_shapes=[
            pltpu.VMEM((TOK, 128), F32),
            pltpu.VMEM((8, 128), F32),
            pltpu.VMEM((TOK, HEADS * HALF), F32),
            pltpu.VMEM((2, 128, SPAN), F32),
            pltpu.VMEM((2, SPAN, SPAN), F32),
            pltpu.VMEM((TOK, CH), F32),
        ],
        compiler_params=pltpu.CompilerParams(vmem_limit_bytes=28 * MIB),
        cost_estimate=SMALL,
        name="scan_forward",
    )(x, z, b, c, dt, rate, skip, gain)


def scan_backward(u, ys, x, z, b, c, dt, rate, skip, gain):
    return pl.pallas_call(
        bwd_kernel,
        out_shape=(
            jax.ShapeDtypeStruct((TOK, CH), BF16),
            jax.ShapeDtypeStruct((TOK, CH), BF16),
            jax.ShapeDtypeStruct((TOK, 128), BF16),
            jax.ShapeDtypeStruct((TOK, 128), BF16),
            jax.ShapeDtypeStruct((TOK, HEADS), F32),
            jax.ShapeDtypeStruct((16, 128), F32),
        ),
        scratch_shapes=[
            pltpu.VMEM((TOK, 128), F32),
            pltpu.VMEM((8, 128), F32),
            pltpu.VMEM((TOK, HEADS * HALF), F32),
            pltpu.VMEM((2, 128, SPAN), F32),
            pltpu.VMEM((2, SPAN, SPAN), F32),
            pltpu.VMEM((TOK, CH), F32),
            pltpu.VMEM((TOK, CH), F32),
            pltpu.VMEM((TOK, CH), F32),
            pltpu.VMEM((2, SPAN, SPAN), F32),
            pltpu.VMEM((8, CH), F32),
        ],
        compiler_params=pltpu.CompilerParams(vmem_limit_bytes=36 * MIB),
        cost_estimate=SMALL,
        name="scan_backward",
    )(u, ys, x, z, b, c, dt, rate, skip, gain)


AXES = {"z": 8, "xl": 2, "c": 2, "y": 4, "xh": 2}
DP = ("z", "xl", "c")
TP = ("y", "xh")


def send(v, axis, shift):
    n = AXES[axis]
    return lax.ppermute(v, axis, [(i, (i + shift) % n) for i in range(n)])


def swap(v, axis, mask):
    return lax.ppermute(v, axis, [(i, i ^ mask) for i in range(AXES[axis])])


def both_ways(up, down, axis):
    return send(up, axis, 1), send(down, axis, -1)


def tie(values, *first):
    return lax.optimization_barrier((tuple(values),) + tuple(first))[0]


def shuffle(name, shapes, plan, scalars, *arrays):
    count = len(plan([0] * len(scalars)))

    def kernel(s_ref, *refs):
        src, dst, sem = refs[:len(arrays)], refs[len(arrays):-1], refs[-1]
        copies = [
            pltpu.make_async_copy(src[i].at[a], dst[o].at[b], sem.at[k])
            for k, (i, a, o, b) in enumerate(plan([s_ref[j] for j in range(len(scalars))]))
        ]
        for copy in copies:
            copy.start()
        for copy in copies:
            copy.wait()

    return pl.pallas_call(
        kernel,
        out_shape=tuple(jax.ShapeDtypeStruct(s, BF16) for s in shapes),
        in_specs=[pl.BlockSpec(memory_space=pltpu.SMEM)] + [pl.BlockSpec(memory_space=pl.ANY)] * len(arrays),
        out_specs=tuple(pl.BlockSpec(memory_space=pltpu.VMEM) for _ in shapes),
        scratch_shapes=[pltpu.SemaphoreType.DMA((count,))],
        cost_estimate=SMALL,
        name=name,
    )(jnp.stack([s.astype(jnp.int32) for s in scalars]), *arrays)


def own_first(rows, core):
    def kernel(core_ref, in_ref, out_ref):
        for j in range(16):
            even = in_ref[:, 256 * j:256 * j + 128]
            odd = in_ref[:, 256 * j + 128:256 * j + 256]
            first = core_ref[0] == 0
            out_ref[:, 128 * j:128 * j + 128] = jnp.where(first, even, odd)
            out_ref[:, 2048 + 128 * j:2048 + 128 * j + 128] = jnp.where(first, odd, even)

    return pl.pallas_call(
        kernel,
        out_shape=jax.ShapeDtypeStruct(rows.shape, rows.dtype),
        in_specs=[pl.BlockSpec(memory_space=pltpu.SMEM), pl.BlockSpec(memory_space=pltpu.VMEM)],
        out_specs=pl.BlockSpec(memory_space=pltpu.VMEM),
        cost_estimate=SMALL,
        name="own_first",
    )(core.astype(jnp.int32).reshape(1), rows)


def at_rows(start, size):
    return (pl.ds(pl.multiple_of(start, 32), size), slice(None)) if not isinstance(start, int) else (slice(start, start + size), slice(None))


def place_tokens(yi, xh, first, *pieces):
    parts = ((0, 64, 0, 0, 0), (1, 64, 0, 1, 0), (2, 64, 3, 0, 0), (3, 64, 3, 1, 0), (4, 64, 1, 0, 0),
             (5, 64, 1, 1, 0), (6, 32, 2, 0, 0), (7, 32, 2, 0, 32), (8, 32, 2, 1, 0), (9, 32, 2, 1, 32))

    def plan(s):
        moves = []
        for piece, size, turn, other, offset in parts:
            start = ((s[0] + turn) % 4) * 128 + (1 - s[1] if other else s[1]) * 64 + offset
            moves.append((piece, (slice(None), slice(first, first + 2048)), 0, at_rows(start, size)))
        return moves

    return shuffle("place_tokens", [(TOK, 2048)], plan, (yi, xh), *pieces)[0]


def weight_blocks(zi, shifts, keep, theirs, normed, normed_other):
    def kernel(at_ref, a_ref, b_ref, n_ref, m_ref, out_ref):
        def term(r, n):
            return lax.dot_general(r[...], n[...], (((0,), (0,)), ((), ())), preferred_element_type=F32)

        out_ref[0] = term(a_ref, n_ref) + term(b_ref, m_ref)

    columns = pl.BlockSpec((TOK, 256), lambda i, at: (0, at[i]))
    whole = pl.BlockSpec((TOK, CH), lambda i, at: (0, 0))
    return pl.pallas_call(
        kernel,
        grid_spec=pltpu.PrefetchScalarGridSpec(
            num_scalar_prefetch=1,
            grid=(len(shifts),),
            in_specs=[columns, columns, whole, whole],
            out_specs=pl.BlockSpec((1, 256, CH), lambda i, at: (i, 0, 0)),
        ),
        out_shape=jax.ShapeDtypeStruct((len(shifts), 256, CH), F32),
        compiler_params=pltpu.CompilerParams(vmem_limit_bytes=16 * MIB),
        cost_estimate=SMALL,
        name="weight_blocks",
    )(jnp.stack([(zi + k + 8) % 8 for k in shifts]).astype(jnp.int32), keep, theirs, normed, normed_other)


def back_project(core, keep, give, w):
    def kernel(core_ref, a_ref, b_ref, v_ref, w_ref, out_ref):
        out_ref[...] = dot(a_ref[...], v_ref[...].reshape(2048, 256)) + dot(b_ref[...], w_ref[...].reshape(2048, 256))

    rows = pl.BlockSpec((TOK, 2048), lambda i, core: (0, 0))
    return pl.pallas_call(
        kernel,
        grid_spec=pltpu.PrefetchScalarGridSpec(
            num_scalar_prefetch=1,
            grid=(4,),
            in_specs=[
                rows,
                rows,
                pl.BlockSpec((16, None, 128, 256), lambda i, core: (0, core[0], 0, i)),
                pl.BlockSpec((16, None, 128, 256), lambda i, core: (0, 1 - core[0], 0, i)),
            ],
            out_specs=pl.BlockSpec((TOK, 256), lambda i, core: (0, i)),
        ),
        out_shape=jax.ShapeDtypeStruct((TOK, CH), F32),
        compiler_params=pltpu.CompilerParams(vmem_limit_bytes=24 * MIB),
        cost_estimate=SMALL,
        name="back_project",
    )(core.astype(jnp.int32).reshape(1), keep, give, w, w)


def on_device(grad_out, x, z, b, c, dt, rate, skip, gain, w_out):
    zi, xl, core, yi, xh = (lax.axis_index(a) for a in ("z", "xl", "c", "y", "xh"))
    scan = (x, z, b.reshape(TOK, 128), c.reshape(TOK, 128), dt, rate[None], skip[None], gain[None])

    w = lax.all_gather(w_out, DP, axis=0, tiled=True).reshape(16, 2, 128, CH)

    own = own_first(grad_out, core)
    below, above = both_ways(own, own, "y")
    other = send(own, "xh", 1)
    below, above, other, late = tie((below, above, other, scan[6]))

    b_other, a_other = both_ways(other, other, "y")
    far_b, far_a = both_ways(below[:32], above[32:], "y")
    ys, normed = scan_forward(*scan[:6], late, scan[7])
    b_other, a_other, far_b, far_a, normed = tie((b_other, a_other, far_b, far_a, normed))

    far_other = both_ways(b_other[:32], a_other[32:], "y")
    normed_other = send(normed, "c", 1)
    far_other, normed_other = tie((far_other, normed_other))
    pieces = (own, other, below, b_other, above, a_other, far_b, far_a) + far_other
    give = place_tokens(yi, xh, 2048, *pieces)
    theirs = send(give, "c", 1)
    keep = place_tokens(yi, xh, 0, *tie(pieces, give))
    theirs, keep = tie((theirs, keep))

    def blocks(*shifts):
        return weight_blocks(zi, shifts, keep, theirs, normed, normed_other)

    half = CH // 2
    far = blocks(4)[0].astype(BF16)
    up, down = both_ways(far[:, half:], far[:, :half], "z")
    v = blocks(3, -3, 2, -2)
    up, down, v = tie((up, down, v))

    up = jnp.concatenate([v[0, :, :half], v[0, :, half:] + up.astype(F32)], axis=1).astype(BF16)
    down = jnp.concatenate([v[1, :, :half] + down.astype(F32), v[1, :, half:]], axis=1).astype(BF16)
    up, down = both_ways(up, down, "z")
    last = blocks(1, -1, 0)
    upstream = back_project(core, keep, give, w)
    up, down, last, upstream = tie((up, down, last, upstream))

    up, down = both_ways((v[2] + up.astype(F32)).astype(BF16), (v[3] + down.astype(F32)).astype(BF16), "z")
    dx, dz, db, dc, ddt, small = scan_backward(upstream, ys, *scan)
    up, down, small = tie((up, down, small))

    def halves(r):
        return lax.dynamic_slice_in_dim(r, (1 - xl) * 128, 128, 0), lax.dynamic_slice_in_dim(r, xl * 128, 128, 0)

    up_leave, up_stay = halves((last[0] + up.astype(F32)).astype(BF16))
    down_leave, down_stay = halves((last[1] + down.astype(F32)).astype(BF16))
    up_leave, down_leave = both_ways(up_leave, down_leave, "z")
    up_stay, down_stay = both_ways(up_stay, down_stay, "z")
    small = small + send(small, "c", 1)
    small = small + send(small, "xl", 1)
    leave, stay = halves(last[2])
    up_leave, down_leave, small = tie((up_leave, down_leave, small))
    leave = send(leave + (up_leave.astype(F32) + down_leave.astype(F32)), "xl", 1)
    for mask in (1, 2, 4):
        small = small + swap(small, "z", mask)
    up_stay, down_stay, leave, stay = tie((up_stay, down_stay, leave, stay), small)
    grad_weight = (stay + leave) + (up_stay.astype(F32) + down_stay.astype(F32))
    return (dx, dz, db[:, None], dc[:, None], ddt, small[8, :HEADS], small[9, :HEADS],
            small[:8].reshape(CH), grad_weight)


def solution(mesh):
    fine = jax.sharding.Mesh(mesh.devices.reshape(tuple(AXES.values())), tuple(AXES))
    part = P(DP, TP)
    part3 = P(DP, TP, None)
    head = P(TP)
    return jax.shard_map(
        on_device,
        mesh=fine,
        in_specs=(P(DP + TP, None), part, part, part3, part3, part, head, head, head, part),
        out_specs=(part, part, part3, part3, part, head, head, head, part),
        check_vma=False,
    )
```

```python
import jax
import jax.numpy as jnp
from jax import lax
from jax.experimental import pallas as pl
from jax.experimental.pallas import tpu as pltpu
from jax.sharding import PartitionSpec as P

F32, BF16 = jnp.float32, jnp.bfloat16
HEADS = 16
SPAN = 256
TOK = 512
CH = 1024
HALF = 128
LOG2E = 1.4426950408889634
BIG = 126.0
VMEM_LIMIT = 48 * 1024 * 1024
SMALL = pl.CostEstimate(flops=1000, bytes_accessed=1000, transcendentals=0)


def dot(a, b):
    return jnp.dot(a, b, preferred_element_type=F32)


def dot_nt(a, b):
    return lax.dot_general(a, b, (((1,), (1,)), ((), ())), preferred_element_type=F32)


def split2(v):
    hi = v.astype(BF16)
    return hi, (v - hi.astype(F32)).astype(BF16)


def dot3(a, b, fn):
    ah, al = split2(a)
    bh, bl = split2(b)
    return fn(ah, bh) + (fn(ah, bl) + fn(al, bh))


def spread_matrix(width):
    row = lax.broadcasted_iota(jnp.int32, (128, HEADS * width), 0)
    col = lax.broadcasted_iota(jnp.int32, (128, HEADS * width), 1)
    return jnp.where((row < 48) & ((row & 15) == col // width), 1.0, 0.0).astype(BF16)


def parts3(v):
    lane = lax.broadcasted_iota(jnp.int32, v.shape, 1)
    v = jnp.where(lane < HEADS, v, 0.0)
    one = v.astype(BF16).astype(F32)
    rest = v - one
    two = rest.astype(BF16).astype(F32)
    three = rest - two
    return (one + pltpu.roll(two, 16, 1) + pltpu.roll(three, 32, 1)).astype(BF16)


def cumulate(tri, v):
    one = v.astype(BF16)
    rest = v - one.astype(F32)
    two = rest.astype(BF16)
    three = (rest - two.astype(F32)).astype(BF16)
    return dot(tri, one) + (dot(tri, two) + dot(tri, three))


def triangle(n, lower):
    row = lax.broadcasted_iota(jnp.int32, (n, n), 0)
    col = lax.broadcasted_iota(jnp.int32, (n, n), 1)
    return jnp.where(row >= col if lower else row <= col, 1.0, 0.0).astype(BF16)


def prepare(dt_ref, rate_ref, pad_ref, ratepad_ref):
    pad_ref[...] = jnp.ones((TOK, 128), F32)
    pad_ref[:, :HEADS] = dt_ref[...]
    ratepad_ref[...] = jnp.zeros((8, 128), F32)
    ratepad_ref[0:1, :HEADS] = rate_ref[...]
    rate = -jnp.exp(ratepad_ref[0:1, :])
    tri = triangle(SPAN, True)
    cums, rs = [], []
    for k in range(2):
        dt = pad_ref[k * SPAN:(k + 1) * SPAN, :]
        cum = cumulate(tri, dt * (rate * LOG2E))
        cums.append(cum)
        rs.append(jnp.log2(dt) - cum)
    return rate, cums, rs


def fwd_kernel(x_ref, z_ref, b_ref, c_ref, dt_ref, rate_ref, skip_ref, gain_ref,
               ys_ref, n_ref, pad_ref, ratepad_ref, cexp_ref, rt_ref, s_ref, coef_ref):
    rate, cums, rs = prepare(dt_ref, rate_ref, pad_ref, ratepad_ref)
    wide = spread_matrix(HALF)
    narrow = spread_matrix(64)
    row = lax.broadcasted_iota(jnp.int32, (SPAN, SPAN), 0)
    col = lax.broadcasted_iota(jnp.int32, (SPAN, SPAN), 1)
    ratepad_ref[0:1, :HEADS] = skip_ref[...]
    skip = ratepad_ref[0:1, :]
    for k in range(2):
        rows = slice(k * SPAN, (k + 1) * SPAN)
        cexp_ref[rows, :] = dot(parts3(cums[k]), wide)
        rt_ref[k] = rs[k].T
        bk, ck = b_ref[rows, :], c_ref[rows, :]
        s_ref[k] = jnp.where(row > col, dot_nt(ck, bk), 0.0)
        diag = jnp.sum(bk.astype(F32) * ck.astype(F32), axis=1, keepdims=True)
        coef_ref[rows, :] = dot(parts3(diag * pad_ref[rows, :] + skip), narrow)
    lane = lax.broadcasted_iota(jnp.int32, (SPAN, 128), 1)

    def pair(hp, _):
        cols = pl.ds(pl.multiple_of(hp * 128, 128), 128)
        for k in range(2):
            rows = slice(k * SPAN, (k + 1) * SPAN)
            xp = x_ref[rows, cols]
            tops, bots = [], []
            for half in range(2):
                h = hp * 2 + half
                rrow = rt_ref[k, pl.ds(h, 1), :]
                hcols = pl.ds(pl.multiple_of(h * 128, 128), 128)
                top = cexp_ref[k * SPAN:k * SPAN + HALF, hcols]
                bot = cexp_ref[k * SPAN + HALF:(k + 1) * SPAN, hcols]
                wt = s_ref[k, :HALF, :HALF] * jnp.exp2(jnp.minimum(top + rrow[:, :HALF], BIG))
                wb = s_ref[k, HALF:, :] * jnp.exp2(
                    jnp.minimum(jnp.concatenate([bot, bot], axis=1) + rrow, BIG))
                tops += split2(wt)
                bots += split2(wb)
            yt = dot(jnp.concatenate(tops, axis=0), xp[:HALF])
            yb = dot(jnp.concatenate(bots, axis=0), xp)
            ys = [jnp.concatenate([v[256 * h:256 * h + 128] + v[256 * h + 128:256 * h + 256] for v in (yt, yb)], axis=0)
                  for h in range(2)]
            ys_ref[rows, cols] = jnp.where(lane < 64, ys[0], ys[1])
        return 0

    lax.fori_loop(0, 8, pair, 0)

    s10 = dot_nt(c_ref[SPAN:, :], b_ref[:SPAN, :])
    qdt = parts3(jnp.exp2(cums[0][SPAN - 1:SPAN, :] + rs[0]))
    p = parts3(jnp.exp2(cums[1]))
    for j in range(4):
        cols = slice(j * 256, (j + 1) * 256)
        xq = dot(qdt, narrow[:, cols]) * x_ref[:SPAN, cols].astype(F32)
        ys_ref[SPAN:, cols] += dot(p, narrow[:, cols]) * dot3(s10, xq, dot)

    gain = gain_ref[...]

    def norm(i, _):
        rows = pl.ds(pl.multiple_of(i * 32, 32), 32)
        z = z_ref[rows, :].astype(F32)
        y = ys_ref[rows, :] + coef_ref[rows, :] * x_ref[rows, :].astype(F32)
        gated = y * (z / (1.0 + jnp.exp(-z)))
        inv = lax.rsqrt(jnp.mean(gated * gated, axis=1, keepdims=True) + 1e-05)
        n_ref[rows, :] = (gated * inv * gain).astype(BF16)
        return 0

    lax.fori_loop(0, TOK // 32, norm, 0)


def bwd_kernel(u_ref, ys_ref, x_ref, z_ref, b_ref, c_ref, dt_ref, rate_ref, skip_ref, gain_ref,
               dx_ref, dz_ref, db_ref, dc_ref, ddt_ref, small_ref,
               pad_ref, ratepad_ref, rexp_ref, ct_ref, s_ref, coef_ref, dy_ref, dxs_ref, ds_ref, dg_ref):
    rate, cums, rs = prepare(dt_ref, rate_ref, pad_ref, ratepad_ref)
    wide = spread_matrix(HALF)
    narrow = spread_matrix(64)
    row = lax.broadcasted_iota(jnp.int32, (SPAN, SPAN), 0)
    col = lax.broadcasted_iota(jnp.int32, (SPAN, SPAN), 1)
    ratepad_ref[0:1, :HEADS] = skip_ref[...]
    skip = ratepad_ref[0:1, :]
    diags = []
    for k in range(2):
        rows = slice(k * SPAN, (k + 1) * SPAN)
        rexp_ref[rows, :] = dot(parts3(rs[k]), wide)
        ct_ref[k] = cums[k].T
        bk, ck = b_ref[rows, :], c_ref[rows, :]
        s_ref[k] = jnp.where(row < col, dot_nt(bk, ck), 0.0)
        diag = jnp.sum(bk.astype(F32) * ck.astype(F32), axis=1, keepdims=True)
        diags.append(diag)
        coef_ref[rows, :] = dot(parts3(diag * pad_ref[rows, :] + skip), narrow)

    gain = gain_ref[...]
    dg_ref[...] = jnp.zeros((8, CH), F32)

    def gate(i, _):
        rows = pl.ds(pl.multiple_of(i * 32, 32), 32)
        z = z_ref[rows, :].astype(F32)
        y = ys_ref[rows, :] + coef_ref[rows, :] * x_ref[rows, :].astype(F32)
        sig = 1.0 / (1.0 + jnp.exp(-z))
        sz = z * sig
        gated = y * sz
        inv = lax.rsqrt(jnp.mean(gated * gated, axis=1, keepdims=True) + 1e-05)
        unit = gated * inv
        u = u_ref[rows, :]
        ug = u * unit
        dg_ref[...] += (ug[0:8] + ug[8:16]) + (ug[16:24] + ug[24:32])
        v = u * gain
        dgated = inv * (v - unit * jnp.mean(v * unit, axis=1, keepdims=True))
        dy_ref[rows, :] = dgated * sz
        dz_ref[rows, :] = (dgated * y * (sig * (1.0 + z * (1.0 - sig)))).astype(BF16)
        return 0

    lax.fori_loop(0, TOK // 32, gate, 0)

    ds_ref[...] = jnp.zeros((2, SPAN, SPAN), F32)
    lane = lax.broadcasted_iota(jnp.int32, (SPAN, 128), 1)

    def pair(hp, _):
        cols = pl.ds(pl.multiple_of(hp * 128, 128), 128)
        for k in range(2):
            rows = slice(k * SPAN, (k + 1) * SPAN)
            xp = x_ref[rows, cols].astype(F32)
            dh, dl = split2(dy_ref[rows, cols])
            dhl = jnp.concatenate([dh, dl], axis=1)
            xx = []
            for half in range(2):
                xm = jnp.where((lane < 64) if half == 0 else (lane >= 64), xp, 0.0).astype(BF16)
                xx.append(jnp.concatenate([xm, xm], axis=1))
            gts = dot_nt(jnp.concatenate([v[:HALF] for v in xx], axis=0), dhl)
            gbs = dot_nt(jnp.concatenate([v[HALF:] for v in xx], axis=0), dhl[HALF:])
            ths, tls, bhs, bls = [], [], [], []
            dst, dsb = ds_ref[k, :HALF, :], ds_ref[k, HALF:, HALF:]
            for half in range(2):
                h = hp * 2 + half
                part = slice(half * HALF, (half + 1) * HALF)
                crow = ct_ref[k, pl.ds(h, 1), :]
                hcols = pl.ds(pl.multiple_of(h * 128, 128), 128)
                top = rexp_ref[k * SPAN:k * SPAN + HALF, hcols]
                bot = rexp_ref[k * SPAN + HALF:(k + 1) * SPAN, hcols]
                et = jnp.exp2(jnp.minimum(jnp.concatenate([top, top], axis=1) + crow, BIG))
                eb = jnp.exp2(jnp.minimum(bot + crow[:, HALF:], BIG))
                dst = dst + et * gts[part]
                dsb = dsb + eb * gbs[part]
                hi, lo = split2(s_ref[k, :HALF, :] * et)
                ths.append(hi)
                tls.append(lo)
                hi, lo = split2(s_ref[k, HALF:, HALF:] * eb)
                bhs.append(hi)
                bls.append(lo)
            ds_ref[k, :HALF, :] = dst
            ds_ref[k, HALF:, HALF:] = dsb
            ot = dot(jnp.concatenate(ths, axis=0), dhl)
            ob = dot(jnp.concatenate(bhs, axis=0), dhl[HALF:])
            ot = (ot[:, :128] + ot[:, 128:]) + dot(jnp.concatenate(tls, axis=0), dh)
            ob = (ob[:, :128] + ob[:, 128:]) + dot(jnp.concatenate(bls, axis=0), dh[HALF:])
            outs = [jnp.concatenate([v[h * HALF:(h + 1) * HALF] for v in (ot, ob)], axis=0) for h in range(2)]
            dxs_ref[rows, cols] = jnp.where(lane < 64, outs[0], outs[1])
        return 0

    lax.fori_loop(0, 8, pair, 0)

    st = dot_nt(b_ref[:SPAN, :], c_ref[SPAN:, :])
    qdt = parts3(jnp.exp2(cums[0][SPAN - 1:SPAN, :] + rs[0]))
    p = parts3(jnp.exp2(cums[1]))
    dst = jnp.zeros((SPAN, SPAN), F32)
    for j in range(4):
        cols = slice(j * 256, (j + 1) * 256)
        qx = dot(qdt, narrow[:, cols])
        xq = qx * x_ref[:SPAN, cols].astype(F32)
        pdy = dot(p, narrow[:, cols]) * dy_ref[SPAN:, cols]
        dxs_ref[:SPAN, cols] += qx * dot3(st, pdy, dot)
        dst = dst + dot3(xq, pdy, dot_nt)

    seg_row = lax.broadcasted_iota(jnp.int32, (CH, 128), 0)
    seg_col = lax.broadcasted_iota(jnp.int32, (CH, 128), 1)
    seg = jnp.where(seg_row // 64 == seg_col, 1.0, 0.0).astype(BF16)

    def heads_sum(v):
        hi, lo = split2(v)
        return dot(hi, seg) + dot(lo, seg)

    tri = triangle(SPAN, False)
    later = jnp.zeros((1, 128), F32)
    rate_sum = jnp.zeros((1, 128), F32)
    skip_sum = jnp.zeros((1, 128), F32)
    for k in (1, 0):
        rows = slice(k * SPAN, (k + 1) * SPAN)
        xf = x_ref[rows, :].astype(F32)
        dy = dy_ref[rows, :]
        dxs = dxs_ref[rows, :]
        kx = heads_sum(dy * xf)
        r = heads_sum(dy * ys_ref[rows, :])
        q = heads_sum(xf * dxs)
        suffix = cumulate(tri, r - q) + later
        later = suffix[0:1, :]
        dt = pad_ref[rows, :]
        ddt = q / dt + kx * diags[k] + rate * suffix
        ddt_ref[rows, :] = ddt[:, :HEADS]
        rate_sum = rate_sum + rate * jnp.sum(dt * suffix, axis=0, keepdims=True)
        skip_sum = skip_sum + jnp.sum(kx, axis=0, keepdims=True)
        sd = jnp.sum(dt * kx, axis=1, keepdims=True)
        dsk = jnp.where(row < col, ds_ref[k], 0.0)
        bk, ck = b_ref[rows, :], c_ref[rows, :]
        sh, sl = split2(dsk)
        db = dot(sh, ck) + dot(sl, ck) + sd * ck.astype(F32)
        sh, sl = split2(dsk.T)
        dc = dot(sh, bk) + dot(sl, bk) + sd * bk.astype(F32)
        if k == 0:
            oh, ol = split2(dst)
            db = db + dot(oh, c_ref[SPAN:, :]) + dot(ol, c_ref[SPAN:, :])
        else:
            oh, ol = split2(dst.T)
            dc = dc + dot(oh, b_ref[:SPAN, :]) + dot(ol, b_ref[:SPAN, :])
        db_ref[rows, :] = db.astype(BF16)
        dc_ref[rows, :] = dc.astype(BF16)
        dx_ref[rows, :] = (dxs + coef_ref[rows, :] * dy).astype(BF16)

    dg = jnp.sum(dg_ref[...], axis=0, keepdims=True)
    for j in range(8):
        small_ref[j:j + 1, :] = dg[:, j * 128:(j + 1) * 128]
    small_ref[8:9, :] = rate_sum
    small_ref[9:10, :] = skip_sum
    small_ref[10:16, :] = jnp.zeros((6, 128), F32)


def scan_forward(x, z, b, c, dt, rate, skip, gain):
    return pl.pallas_call(
        fwd_kernel,
        out_shape=(jax.ShapeDtypeStruct((TOK, CH), F32), jax.ShapeDtypeStruct((TOK, CH), BF16)),
        scratch_shapes=[
            pltpu.VMEM((TOK, 128), F32),
            pltpu.VMEM((8, 128), F32),
            pltpu.VMEM((TOK, HEADS * HALF), F32),
            pltpu.VMEM((2, 128, SPAN), F32),
            pltpu.VMEM((2, SPAN, SPAN), F32),
            pltpu.VMEM((TOK, CH), F32),
        ],
        compiler_params=pltpu.CompilerParams(vmem_limit_bytes=VMEM_LIMIT),
        cost_estimate=SMALL,
        name="scan_forward",
    )(x, z, b, c, dt, rate, skip, gain)


def scan_backward(u, ys, x, z, b, c, dt, rate, skip, gain):
    return pl.pallas_call(
        bwd_kernel,
        out_shape=(
            jax.ShapeDtypeStruct((TOK, CH), BF16),
            jax.ShapeDtypeStruct((TOK, CH), BF16),
            jax.ShapeDtypeStruct((TOK, 128), BF16),
            jax.ShapeDtypeStruct((TOK, 128), BF16),
            jax.ShapeDtypeStruct((TOK, HEADS), F32),
            jax.ShapeDtypeStruct((16, 128), F32),
        ),
        scratch_shapes=[
            pltpu.VMEM((TOK, 128), F32),
            pltpu.VMEM((8, 128), F32),
            pltpu.VMEM((TOK, HEADS * HALF), F32),
            pltpu.VMEM((2, 128, SPAN), F32),
            pltpu.VMEM((2, SPAN, SPAN), F32),
            pltpu.VMEM((TOK, CH), F32),
            pltpu.VMEM((TOK, CH), F32),
            pltpu.VMEM((TOK, CH), F32),
            pltpu.VMEM((2, SPAN, SPAN), F32),
            pltpu.VMEM((8, CH), F32),
        ],
        compiler_params=pltpu.CompilerParams(vmem_limit_bytes=VMEM_LIMIT),
        cost_estimate=SMALL,
        name="scan_backward",
    )(u, ys, x, z, b, c, dt, rate, skip, gain)


AXES = {"z": 8, "xl": 2, "c": 2, "y": 4, "xh": 2}
DP = ("z", "xl", "c")
TP = ("y", "xh")


def send(v, axis, shift):
    n = AXES[axis]
    return lax.ppermute(v, axis, [(i, (i + shift) % n) for i in range(n)])


def swap(v, axis, mask):
    return lax.ppermute(v, axis, [(i, i ^ mask) for i in range(AXES[axis])])


def both_ways(up, down, axis):
    return send(up, axis, 1), send(down, axis, -1)


def tie(values, *first):
    return lax.optimization_barrier((tuple(values),) + tuple(first))[0]


def shuffle(name, shapes, plan, scalars, *arrays):
    count = len(plan([0] * len(scalars)))

    def kernel(s_ref, *refs):
        src, dst, sem = refs[:len(arrays)], refs[len(arrays):-1], refs[-1]
        copies = [
            pltpu.make_async_copy(src[i].at[a], dst[o].at[b], sem.at[k])
            for k, (i, a, o, b) in enumerate(plan([s_ref[j] for j in range(len(scalars))]))
        ]
        for copy in copies:
            copy.start()
        for copy in copies:
            copy.wait()

    return pl.pallas_call(
        kernel,
        out_shape=tuple(jax.ShapeDtypeStruct(s, BF16) for s in shapes),
        in_specs=[pl.BlockSpec(memory_space=pltpu.SMEM)] + [pl.BlockSpec(memory_space=pl.ANY)] * len(arrays),
        out_specs=tuple(pl.BlockSpec(memory_space=pltpu.VMEM) for _ in shapes),
        scratch_shapes=[pltpu.SemaphoreType.DMA((count,))],
        cost_estimate=SMALL,
        name=name,
    )(jnp.stack([s.astype(jnp.int32) for s in scalars]), *arrays)


def own_first(rows, core):
    def kernel(core_ref, in_ref, out_ref):
        for j in range(16):
            even = in_ref[:, 256 * j:256 * j + 128]
            odd = in_ref[:, 256 * j + 128:256 * j + 256]
            first = core_ref[0] == 0
            out_ref[:, 128 * j:128 * j + 128] = jnp.where(first, even, odd)
            out_ref[:, 2048 + 128 * j:2048 + 128 * j + 128] = jnp.where(first, odd, even)

    return pl.pallas_call(
        kernel,
        out_shape=jax.ShapeDtypeStruct(rows.shape, rows.dtype),
        in_specs=[pl.BlockSpec(memory_space=pltpu.SMEM), pl.BlockSpec(memory_space=pltpu.VMEM)],
        out_specs=pl.BlockSpec(memory_space=pltpu.VMEM),
        cost_estimate=SMALL,
        name="own_first",
    )(core.astype(jnp.int32).reshape(1), rows)


def at_rows(start, size):
    return (pl.ds(pl.multiple_of(start, 32), size), slice(None)) if not isinstance(start, int) else (slice(start, start + size), slice(None))


def place_tokens(yi, xh, first, *pieces):
    parts = ((0, 64, 0, 0, 0), (1, 64, 0, 1, 0), (2, 64, 3, 0, 0), (3, 64, 3, 1, 0), (4, 64, 1, 0, 0),
             (5, 64, 1, 1, 0), (6, 32, 2, 0, 0), (7, 32, 2, 0, 32), (8, 32, 2, 1, 0), (9, 32, 2, 1, 32))

    def plan(s):
        moves = []
        for piece, size, turn, other, offset in parts:
            start = ((s[0] + turn) % 4) * 128 + (1 - s[1] if other else s[1]) * 64 + offset
            moves.append((piece, (slice(None), slice(first, first + 2048)), 0, at_rows(start, size)))
        return moves

    return shuffle("place_tokens", [(TOK, 2048)], plan, (yi, xh), *pieces)[0]


def weight_blocks(zi, shifts, keep, theirs, normed, normed_other):
    def kernel(at_ref, a_ref, b_ref, n_ref, m_ref, out_ref):
        def term(r, n):
            return lax.dot_general(r[...], n[...], (((0,), (0,)), ((), ())), preferred_element_type=F32)

        out_ref[0] = term(a_ref, n_ref) + term(b_ref, m_ref)

    columns = pl.BlockSpec((TOK, 256), lambda i, at: (0, at[i]))
    whole = pl.BlockSpec((TOK, CH), lambda i, at: (0, 0))
    return pl.pallas_call(
        kernel,
        grid_spec=pltpu.PrefetchScalarGridSpec(
            num_scalar_prefetch=1,
            grid=(len(shifts),),
            in_specs=[columns, columns, whole, whole],
            out_specs=pl.BlockSpec((1, 256, CH), lambda i, at: (i, 0, 0)),
        ),
        out_shape=jax.ShapeDtypeStruct((len(shifts), 256, CH), F32),
        compiler_params=pltpu.CompilerParams(vmem_limit_bytes=VMEM_LIMIT),
        cost_estimate=SMALL,
        name="weight_blocks",
    )(jnp.stack([(zi + k + 8) % 8 for k in shifts]).astype(jnp.int32), keep, theirs, normed, normed_other)


def ring_step(zi, shift, keep, theirs, normed, normed_other, up, down):
    width = up.shape[1]
    at = CH - width

    def kernel(at_ref, a_ref, b_ref, n_ref, m_ref, up_ref, down_ref, up_out, down_out):
        def term(r, n):
            return lax.dot_general(r[...], n[...], (((0,), (0,)), ((), ())), preferred_element_type=F32)

        total = term(a_ref, n_ref) + term(b_ref, m_ref)

        @pl.when(pl.program_id(0) == 0)
        def _():
            if at:
                up_out[:, :at] = total[:, :at].astype(BF16)
            up_out[:, at:] = (total[:, at:] + up_ref[...].astype(F32)).astype(BF16)

        @pl.when(pl.program_id(0) == 1)
        def _():
            if at:
                down_out[:, width:] = total[:, width:].astype(BF16)
            down_out[:, :width] = (total[:, :width] + down_ref[...].astype(F32)).astype(BF16)

    columns = pl.BlockSpec((TOK, 256), lambda i, at: (0, at[i]))
    whole = pl.BlockSpec((TOK, CH), lambda i, at: (0, 0))
    part = pl.BlockSpec((256, width), lambda i, at: (0, 0))
    full = pl.BlockSpec((256, CH), lambda i, at: (0, 0))
    return pl.pallas_call(
        kernel,
        grid_spec=pltpu.PrefetchScalarGridSpec(
            num_scalar_prefetch=1,
            grid=(2,),
            in_specs=[columns, columns, whole, whole, part, part],
            out_specs=(full, full),
        ),
        out_shape=(jax.ShapeDtypeStruct((256, CH), BF16),) * 2,
        compiler_params=pltpu.CompilerParams(vmem_limit_bytes=VMEM_LIMIT),
        cost_estimate=SMALL,
        name="ring_step",
    )(jnp.stack([(zi + k + 8) % 8 for k in (shift, -shift)]).astype(jnp.int32), keep, theirs, normed, normed_other, up, down)


def back_project(core, keep, give, w):
    def kernel(core_ref, a_ref, b_ref, v_ref, w_ref, out_ref):
        out_ref[...] = dot(a_ref[...], v_ref[...].reshape(2048, 256)) + dot(b_ref[...], w_ref[...].reshape(2048, 256))

    rows = pl.BlockSpec((TOK, 2048), lambda i, core: (0, 0))
    return pl.pallas_call(
        kernel,
        grid_spec=pltpu.PrefetchScalarGridSpec(
            num_scalar_prefetch=1,
            grid=(4,),
            in_specs=[
                rows,
                rows,
                pl.BlockSpec((16, None, 128, 256), lambda i, core: (0, core[0], 0, i)),
                pl.BlockSpec((16, None, 128, 256), lambda i, core: (0, 1 - core[0], 0, i)),
            ],
            out_specs=pl.BlockSpec((TOK, 256), lambda i, core: (0, i)),
        ),
        out_shape=jax.ShapeDtypeStruct((TOK, CH), F32),
        compiler_params=pltpu.CompilerParams(vmem_limit_bytes=VMEM_LIMIT),
        cost_estimate=SMALL,
        name="back_project",
    )(core.astype(jnp.int32).reshape(1), keep, give, w, w)


def on_device(grad_out, x, z, b, c, dt, rate, skip, gain, w_out):
    zi, xl, core, yi, xh = (lax.axis_index(a) for a in ("z", "xl", "c", "y", "xh"))
    scan = (x, z, b.reshape(TOK, 128), c.reshape(TOK, 128), dt, rate[None], skip[None], gain[None])

    w = lax.all_gather(w_out, DP, axis=0, tiled=True).reshape(16, 2, 128, CH)

    own = own_first(grad_out, core)
    below, above = both_ways(own, own, "y")
    other = send(own, "xh", 1)
    below, above, other, late = tie((below, above, other, scan[6]))

    b_other, a_other = both_ways(other, other, "y")
    far_b, far_a = both_ways(below[:32], above[32:], "y")
    ys, normed = scan_forward(*scan[:6], late, scan[7])
    b_other, a_other, far_b, far_a, normed = tie((b_other, a_other, far_b, far_a, normed))

    far_other = both_ways(b_other[:32], a_other[32:], "y")
    normed_other = send(normed, "c", 1)
    far_other, normed_other = tie((far_other, normed_other))
    pieces = (own, other, below, b_other, above, a_other, far_b, far_a) + far_other
    give = place_tokens(yi, xh, 2048, *pieces)
    theirs = send(give, "c", 1)
    keep = place_tokens(yi, xh, 0, *tie(pieces, give))
    theirs, keep = tie((theirs, keep))

    def blocks(*shifts):
        return weight_blocks(zi, shifts, keep, theirs, normed, normed_other)

    half = CH // 2
    far = blocks(4)[0].astype(BF16)
    up, down = both_ways(far[:, half:], far[:, :half], "z")
    upstream = back_project(core, keep, give, w)
    up, down, upstream = tie((up, down, upstream))

    up, down = both_ways(*ring_step(zi, 3, keep, theirs, normed, normed_other, up, down), "z")
    dx, dz, db, dc, ddt, small = scan_backward(upstream, ys, *scan)
    up, down, small = tie((up, down, small))

    up, down = both_ways(*ring_step(zi, 2, keep, theirs, normed, normed_other, up, down), "z")
    last = blocks(1, -1, 0)
    small = small + send(small, "c", 1)
    small = small + send(small, "xl", 1)
    small = small + swap(small, "z", 1)
    up, down, last, small = tie((up, down, last, small))

    def halves(r):
        return lax.dynamic_slice_in_dim(r, (1 - xl) * 128, 128, 0), lax.dynamic_slice_in_dim(r, xl * 128, 128, 0)

    up_leave, up_stay = halves((last[0] + up.astype(F32)).astype(BF16))
    down_leave, down_stay = halves((last[1] + down.astype(F32)).astype(BF16))
    up_leave, down_leave = both_ways(up_leave, down_leave, "z")
    up_stay, down_stay = both_ways(up_stay, down_stay, "z")
    small = small + swap(small, "z", 2)
    leave, stay = halves(last[2])
    up_leave, down_leave, small = tie((up_leave, down_leave, small))
    leave = send(leave + (up_leave.astype(F32) + down_leave.astype(F32)), "xl", 1)
    small = small + swap(small, "z", 4)
    up_stay, down_stay, leave, stay = tie((up_stay, down_stay, leave, stay), small)
    grad_weight = (stay + leave) + (up_stay.astype(F32) + down_stay.astype(F32))
    return (dx, dz, db[:, None], dc[:, None], ddt, small[8, :HEADS], small[9, :HEADS],
            small[:8].reshape(CH), grad_weight)


def solution(mesh):
    fine = jax.sharding.Mesh(mesh.devices.reshape(tuple(AXES.values())), tuple(AXES))
    part = P(DP, TP)
    part3 = P(DP, TP, None)
    head = P(TP)
    return jax.shard_map(
        on_device,
        mesh=fine,
        in_specs=(P(DP + TP, None), part, part, part3, part3, part, head, head, head, part),
        out_specs=(part, part, part3, part3, part, head, head, head, part),
        check_vma=False,
    )
```

```python
import jax
import jax.numpy as jnp
from jax import lax
from jax.experimental import pallas as pl
from jax.experimental.pallas import tpu as pltpu
from jax.sharding import PartitionSpec as P

F32, BF16 = jnp.float32, jnp.bfloat16
HEADS = 16
SPAN = 256
TOK = 512
CH = 1024
HALF = 128
LOG2E = 1.4426950408889634
BIG = 126.0
VMEM_LIMIT = 48 * 1024 * 1024
SMALL = pl.CostEstimate(flops=1000, bytes_accessed=1000, transcendentals=0)


def dot(a, b):
    return jnp.dot(a, b, preferred_element_type=F32)


def dot_nt(a, b):
    return lax.dot_general(a, b, (((1,), (1,)), ((), ())), preferred_element_type=F32)


def split2(v):
    hi = v.astype(BF16)
    return hi, (v - hi.astype(F32)).astype(BF16)


def dot3(a, b, fn):
    ah, al = split2(a)
    bh, bl = split2(b)
    return fn(ah, bh) + (fn(ah, bl) + fn(al, bh))


def spread_matrix(width):
    row = lax.broadcasted_iota(jnp.int32, (128, HEADS * width), 0)
    col = lax.broadcasted_iota(jnp.int32, (128, HEADS * width), 1)
    return jnp.where((row < 48) & ((row & 15) == col // width), 1.0, 0.0).astype(BF16)


def parts3(v):
    lane = lax.broadcasted_iota(jnp.int32, v.shape, 1)
    v = jnp.where(lane < HEADS, v, 0.0)
    one = v.astype(BF16).astype(F32)
    rest = v - one
    two = rest.astype(BF16).astype(F32)
    three = rest - two
    return (one + pltpu.roll(two, 16, 1) + pltpu.roll(three, 32, 1)).astype(BF16)


def cumulate(tri, v):
    one = v.astype(BF16)
    rest = v - one.astype(F32)
    two = rest.astype(BF16)
    three = (rest - two.astype(F32)).astype(BF16)
    return dot(tri, one) + (dot(tri, two) + dot(tri, three))


def triangle(n, lower):
    row = lax.broadcasted_iota(jnp.int32, (n, n), 0)
    col = lax.broadcasted_iota(jnp.int32, (n, n), 1)
    return jnp.where(row >= col if lower else row <= col, 1.0, 0.0).astype(BF16)


def prepare(dt_ref, rate_ref, pad_ref, ratepad_ref):
    pad_ref[...] = jnp.ones((TOK, 128), F32)
    pad_ref[:, :HEADS] = dt_ref[...]
    ratepad_ref[...] = jnp.zeros((8, 128), F32)
    ratepad_ref[0:1, :HEADS] = rate_ref[...]
    rate = -jnp.exp(ratepad_ref[0:1, :])
    tri = triangle(SPAN, True)
    cums, rs = [], []
    for k in range(2):
        dt = pad_ref[k * SPAN:(k + 1) * SPAN, :]
        cum = cumulate(tri, dt * (rate * LOG2E))
        cums.append(cum)
        rs.append(jnp.log2(dt) - cum)
    return rate, cums, rs


def fwd_kernel(x_ref, z_ref, b_ref, c_ref, dt_ref, rate_ref, skip_ref, gain_ref,
               ys_ref, n_ref, pad_ref, ratepad_ref, cexp_ref, rt_ref, s_ref, coef_ref):
    rate, cums, rs = prepare(dt_ref, rate_ref, pad_ref, ratepad_ref)
    wide = spread_matrix(HALF)
    narrow = spread_matrix(64)
    row = lax.broadcasted_iota(jnp.int32, (SPAN, SPAN), 0)
    col = lax.broadcasted_iota(jnp.int32, (SPAN, SPAN), 1)
    ratepad_ref[0:1, :HEADS] = skip_ref[...]
    skip = ratepad_ref[0:1, :]
    for k in range(2):
        rows = slice(k * SPAN, (k + 1) * SPAN)
        cexp_ref[rows, :] = dot(parts3(cums[k]), wide)
        rt_ref[k] = rs[k].T
        bk, ck = b_ref[rows, :], c_ref[rows, :]
        s_ref[k] = jnp.where(row > col, dot_nt(ck, bk), 0.0)
        diag = jnp.sum(bk.astype(F32) * ck.astype(F32), axis=1, keepdims=True)
        coef_ref[rows, :] = dot(parts3(diag * pad_ref[rows, :] + skip), narrow)
    lane = lax.broadcasted_iota(jnp.int32, (SPAN, 128), 1)

    def pair(hp, _):
        cols = pl.ds(pl.multiple_of(hp * 128, 128), 128)
        for k in range(2):
            rows = slice(k * SPAN, (k + 1) * SPAN)
            xp = x_ref[rows, cols]
            tops, bots = [], []
            for half in range(2):
                h = hp * 2 + half
                rrow = rt_ref[k, pl.ds(h, 1), :]
                hcols = pl.ds(pl.multiple_of(h * 128, 128), 128)
                top = cexp_ref[k * SPAN:k * SPAN + HALF, hcols]
                bot = cexp_ref[k * SPAN + HALF:(k + 1) * SPAN, hcols]
                wt = s_ref[k, :HALF, :HALF] * jnp.exp2(jnp.minimum(top + rrow[:, :HALF], BIG))
                wb = s_ref[k, HALF:, :] * jnp.exp2(
                    jnp.minimum(jnp.concatenate([bot, bot], axis=1) + rrow, BIG))
                tops += split2(wt)
                bots += split2(wb)
            yt = dot(jnp.concatenate(tops, axis=0), xp[:HALF])
            yb = dot(jnp.concatenate(bots, axis=0), xp)
            ys = [jnp.concatenate([v[256 * h:256 * h + 128] + v[256 * h + 128:256 * h + 256] for v in (yt, yb)], axis=0)
                  for h in range(2)]
            ys_ref[rows, cols] = jnp.where(lane < 64, ys[0], ys[1])
        return 0

    lax.fori_loop(0, 8, pair, 0)

    s10 = dot_nt(c_ref[SPAN:, :], b_ref[:SPAN, :])
    qdt = parts3(jnp.exp2(cums[0][SPAN - 1:SPAN, :] + rs[0]))
    p = parts3(jnp.exp2(cums[1]))
    for j in range(4):
        cols = slice(j * 256, (j + 1) * 256)
        xq = dot(qdt, narrow[:, cols]) * x_ref[:SPAN, cols].astype(F32)
        ys_ref[SPAN:, cols] += dot(p, narrow[:, cols]) * dot3(s10, xq, dot)

    gain = gain_ref[...]

    def norm(i, _):
        rows = pl.ds(pl.multiple_of(i * 32, 32), 32)
        z = z_ref[rows, :].astype(F32)
        y = ys_ref[rows, :] + coef_ref[rows, :] * x_ref[rows, :].astype(F32)
        gated = y * (z / (1.0 + jnp.exp(-z)))
        inv = lax.rsqrt(jnp.mean(gated * gated, axis=1, keepdims=True) + 1e-05)
        n_ref[rows, :] = (gated * inv * gain).astype(BF16)
        return 0

    lax.fori_loop(0, TOK // 32, norm, 0)


def bwd_kernel(u_ref, ys_ref, x_ref, z_ref, b_ref, c_ref, dt_ref, rate_ref, skip_ref, gain_ref,
               dx_ref, dz_ref, db_ref, dc_ref, ddt_ref, small_ref,
               pad_ref, ratepad_ref, rexp_ref, ct_ref, s_ref, coef_ref, dy_ref, dxs_ref, ds_ref, dg_ref):
    rate, cums, rs = prepare(dt_ref, rate_ref, pad_ref, ratepad_ref)
    wide = spread_matrix(HALF)
    narrow = spread_matrix(64)
    row = lax.broadcasted_iota(jnp.int32, (SPAN, SPAN), 0)
    col = lax.broadcasted_iota(jnp.int32, (SPAN, SPAN), 1)
    ratepad_ref[0:1, :HEADS] = skip_ref[...]
    skip = ratepad_ref[0:1, :]
    diags = []
    for k in range(2):
        rows = slice(k * SPAN, (k + 1) * SPAN)
        rexp_ref[rows, :] = dot(parts3(rs[k]), wide)
        ct_ref[k] = cums[k].T
        bk, ck = b_ref[rows, :], c_ref[rows, :]
        s_ref[k] = jnp.where(row < col, dot_nt(bk, ck), 0.0)
        diag = jnp.sum(bk.astype(F32) * ck.astype(F32), axis=1, keepdims=True)
        diags.append(diag)
        coef_ref[rows, :] = dot(parts3(diag * pad_ref[rows, :] + skip), narrow)

    gain = gain_ref[...]
    dg_ref[...] = jnp.zeros((8, CH), F32)

    def gate(i, _):
        rows = pl.ds(pl.multiple_of(i * 32, 32), 32)
        z = z_ref[rows, :].astype(F32)
        y = ys_ref[rows, :] + coef_ref[rows, :] * x_ref[rows, :].astype(F32)
        sig = 1.0 / (1.0 + jnp.exp(-z))
        sz = z * sig
        gated = y * sz
        inv = lax.rsqrt(jnp.mean(gated * gated, axis=1, keepdims=True) + 1e-05)
        unit = gated * inv
        u = u_ref[rows, :]
        ug = u * unit
        dg_ref[...] += (ug[0:8] + ug[8:16]) + (ug[16:24] + ug[24:32])
        v = u * gain
        dgated = inv * (v - unit * jnp.mean(v * unit, axis=1, keepdims=True))
        dy_ref[rows, :] = dgated * sz
        dz_ref[rows, :] = (dgated * y * (sig * (1.0 + z * (1.0 - sig)))).astype(BF16)
        return 0

    lax.fori_loop(0, TOK // 32, gate, 0)

    ds_ref[...] = jnp.zeros((2, SPAN, SPAN), F32)
    lane = lax.broadcasted_iota(jnp.int32, (SPAN, 128), 1)

    def pair(hp, _):
        cols = pl.ds(pl.multiple_of(hp * 128, 128), 128)
        for k in range(2):
            rows = slice(k * SPAN, (k + 1) * SPAN)
            xp = x_ref[rows, cols].astype(F32)
            dh, dl = split2(dy_ref[rows, cols])
            dhl = jnp.concatenate([dh, dl], axis=1)
            xx = []
            for half in range(2):
                xm = jnp.where((lane < 64) if half == 0 else (lane >= 64), xp, 0.0).astype(BF16)
                xx.append(jnp.concatenate([xm, xm], axis=1))
            gts = dot_nt(jnp.concatenate([v[:HALF] for v in xx], axis=0), dhl)
            gbs = dot_nt(jnp.concatenate([v[HALF:] for v in xx], axis=0), dhl[HALF:])
            ths, tls, bhs, bls = [], [], [], []
            dst, dsb = ds_ref[k, :HALF, :], ds_ref[k, HALF:, HALF:]
            for half in range(2):
                h = hp * 2 + half
                part = slice(half * HALF, (half + 1) * HALF)
                crow = ct_ref[k, pl.ds(h, 1), :]
                hcols = pl.ds(pl.multiple_of(h * 128, 128), 128)
                top = rexp_ref[k * SPAN:k * SPAN + HALF, hcols]
                bot = rexp_ref[k * SPAN + HALF:(k + 1) * SPAN, hcols]
                et = jnp.exp2(jnp.minimum(jnp.concatenate([top, top], axis=1) + crow, BIG))
                eb = jnp.exp2(jnp.minimum(bot + crow[:, HALF:], BIG))
                dst = dst + et * gts[part]
                dsb = dsb + eb * gbs[part]
                hi, lo = split2(s_ref[k, :HALF, :] * et)
                ths.append(hi)
                tls.append(lo)
                hi, lo = split2(s_ref[k, HALF:, HALF:] * eb)
                bhs.append(hi)
                bls.append(lo)
            ds_ref[k, :HALF, :] = dst
            ds_ref[k, HALF:, HALF:] = dsb
            ot = dot(jnp.concatenate(ths, axis=0), dhl)
            ob = dot(jnp.concatenate(bhs, axis=0), dhl[HALF:])
            ot = (ot[:, :128] + ot[:, 128:]) + dot(jnp.concatenate(tls, axis=0), dh)
            ob = (ob[:, :128] + ob[:, 128:]) + dot(jnp.concatenate(bls, axis=0), dh[HALF:])
            outs = [jnp.concatenate([v[h * HALF:(h + 1) * HALF] for v in (ot, ob)], axis=0) for h in range(2)]
            dxs_ref[rows, cols] = jnp.where(lane < 64, outs[0], outs[1])
        return 0

    lax.fori_loop(0, 8, pair, 0)

    st = dot_nt(b_ref[:SPAN, :], c_ref[SPAN:, :])
    qdt = parts3(jnp.exp2(cums[0][SPAN - 1:SPAN, :] + rs[0]))
    p = parts3(jnp.exp2(cums[1]))
    dst = jnp.zeros((SPAN, SPAN), F32)
    for j in range(4):
        cols = slice(j * 256, (j + 1) * 256)
        qx = dot(qdt, narrow[:, cols])
        xq = qx * x_ref[:SPAN, cols].astype(F32)
        pdy = dot(p, narrow[:, cols]) * dy_ref[SPAN:, cols]
        dxs_ref[:SPAN, cols] += qx * dot3(st, pdy, dot)
        dst = dst + dot3(xq, pdy, dot_nt)

    seg_row = lax.broadcasted_iota(jnp.int32, (CH, 128), 0)
    seg_col = lax.broadcasted_iota(jnp.int32, (CH, 128), 1)
    seg = jnp.where(seg_row // 64 == seg_col, 1.0, 0.0).astype(BF16)

    def heads_sum(v):
        hi, lo = split2(v)
        return dot(hi, seg) + dot(lo, seg)

    tri = triangle(SPAN, False)
    later = jnp.zeros((1, 128), F32)
    rate_sum = jnp.zeros((1, 128), F32)
    skip_sum = jnp.zeros((1, 128), F32)
    for k in (1, 0):
        rows = slice(k * SPAN, (k + 1) * SPAN)
        xf = x_ref[rows, :].astype(F32)
        dy = dy_ref[rows, :]
        dxs = dxs_ref[rows, :]
        kx = heads_sum(dy * xf)
        r = heads_sum(dy * ys_ref[rows, :])
        q = heads_sum(xf * dxs)
        suffix = cumulate(tri, r - q) + later
        later = suffix[0:1, :]
        dt = pad_ref[rows, :]
        ddt = q / dt + kx * diags[k] + rate * suffix
        ddt_ref[rows, :] = ddt[:, :HEADS]
        rate_sum = rate_sum + rate * jnp.sum(dt * suffix, axis=0, keepdims=True)
        skip_sum = skip_sum + jnp.sum(kx, axis=0, keepdims=True)
        sd = jnp.sum(dt * kx, axis=1, keepdims=True)
        dsk = jnp.where(row < col, ds_ref[k], 0.0)
        bk, ck = b_ref[rows, :], c_ref[rows, :]
        sh, sl = split2(dsk)
        db = dot(sh, ck) + dot(sl, ck) + sd * ck.astype(F32)
        sh, sl = split2(dsk.T)
        dc = dot(sh, bk) + dot(sl, bk) + sd * bk.astype(F32)
        if k == 0:
            oh, ol = split2(dst)
            db = db + dot(oh, c_ref[SPAN:, :]) + dot(ol, c_ref[SPAN:, :])
        else:
            oh, ol = split2(dst.T)
            dc = dc + dot(oh, b_ref[:SPAN, :]) + dot(ol, b_ref[:SPAN, :])
        db_ref[rows, :] = db.astype(BF16)
        dc_ref[rows, :] = dc.astype(BF16)
        dx_ref[rows, :] = (dxs + coef_ref[rows, :] * dy).astype(BF16)

    dg = jnp.sum(dg_ref[...], axis=0, keepdims=True)
    for j in range(8):
        small_ref[j:j + 1, :] = dg[:, j * 128:(j + 1) * 128]
    small_ref[8:9, :] = rate_sum
    small_ref[9:10, :] = skip_sum
    small_ref[10:16, :] = jnp.zeros((6, 128), F32)


def scan_forward(x, z, b, c, dt, rate, skip, gain):
    return pl.pallas_call(
        fwd_kernel,
        out_shape=(jax.ShapeDtypeStruct((TOK, CH), F32), jax.ShapeDtypeStruct((TOK, CH), BF16)),
        scratch_shapes=[
            pltpu.VMEM((TOK, 128), F32),
            pltpu.VMEM((8, 128), F32),
            pltpu.VMEM((TOK, HEADS * HALF), F32),
            pltpu.VMEM((2, 128, SPAN), F32),
            pltpu.VMEM((2, SPAN, SPAN), F32),
            pltpu.VMEM((TOK, CH), F32),
        ],
        compiler_params=pltpu.CompilerParams(vmem_limit_bytes=VMEM_LIMIT),
        cost_estimate=SMALL,
        name="scan_forward",
    )(x, z, b, c, dt, rate, skip, gain)


def scan_backward(u, ys, x, z, b, c, dt, rate, skip, gain):
    return pl.pallas_call(
        bwd_kernel,
        out_shape=(
            jax.ShapeDtypeStruct((TOK, CH), BF16),
            jax.ShapeDtypeStruct((TOK, CH), BF16),
            jax.ShapeDtypeStruct((TOK, 128), BF16),
            jax.ShapeDtypeStruct((TOK, 128), BF16),
            jax.ShapeDtypeStruct((TOK, HEADS), F32),
            jax.ShapeDtypeStruct((16, 128), F32),
        ),
        scratch_shapes=[
            pltpu.VMEM((TOK, 128), F32),
            pltpu.VMEM((8, 128), F32),
            pltpu.VMEM((TOK, HEADS * HALF), F32),
            pltpu.VMEM((2, 128, SPAN), F32),
            pltpu.VMEM((2, SPAN, SPAN), F32),
            pltpu.VMEM((TOK, CH), F32),
            pltpu.VMEM((TOK, CH), F32),
            pltpu.VMEM((TOK, CH), F32),
            pltpu.VMEM((2, SPAN, SPAN), F32),
            pltpu.VMEM((8, CH), F32),
        ],
        compiler_params=pltpu.CompilerParams(vmem_limit_bytes=VMEM_LIMIT),
        cost_estimate=SMALL,
        name="scan_backward",
    )(u, ys, x, z, b, c, dt, rate, skip, gain)


AXES = {"z": 8, "xl": 2, "c": 2, "y": 4, "xh": 2}
DP = ("z", "xl", "c")
TP = ("y", "xh")


def send(v, axis, shift):
    n = AXES[axis]
    return lax.ppermute(v, axis, [(i, (i + shift) % n) for i in range(n)])


def swap(v, axis, mask):
    return lax.ppermute(v, axis, [(i, i ^ mask) for i in range(AXES[axis])])


def both_ways(up, down, axis):
    return send(up, axis, 1), send(down, axis, -1)


def tie(values, *first):
    return lax.optimization_barrier((tuple(values),) + tuple(first))[0]


def place_tokens(yi, xh, core, *pieces):
    parts = ((0, 64, 0, 0, 0), (1, 64, 0, 1, 0), (2, 64, 3, 0, 0), (3, 64, 3, 1, 0), (4, 64, 1, 0, 0), (5, 64, 1, 1, 0),
             (6, 32, 2, 0, 0), (7, 32, 2, 0, 32), (8, 32, 2, 1, 0), (9, 32, 2, 1, 32))

    def kernel(s_ref, *refs):
        src, (keep, give, land, sem) = refs[:len(pieces)], refs[len(pieces):]
        copies = []
        for piece, size, turn, other, offset in parts:
            start = ((s_ref[0] + turn) % 4) * 128 + (1 - s_ref[1] if other else s_ref[1]) * 64 + offset
            rows = pl.ds(pl.multiple_of(start, 32), size)
            copies.append(pltpu.make_async_copy(src[piece], land.at[rows, :], sem.at[piece]))
        for copy in copies:
            copy.start()
        for copy in copies:
            copy.wait()

        def split(even, odd):
            def step(i, _):
                rows = pl.ds(pl.multiple_of(i * 64, 64), 64)
                for j in range(16):
                    even[rows, 128 * j:128 * j + 128] = land[rows, 256 * j:256 * j + 128]
                    odd[rows, 128 * j:128 * j + 128] = land[rows, 256 * j + 128:256 * j + 256]
                return 0

            lax.fori_loop(0, TOK // 64, step, 0)

        pl.when(s_ref[2] == 0)(lambda: split(keep, give))
        pl.when(s_ref[2] == 1)(lambda: split(give, keep))

    return pl.pallas_call(
        kernel,
        out_shape=(jax.ShapeDtypeStruct((TOK, 2048), BF16),) * 2,
        in_specs=[pl.BlockSpec(memory_space=pltpu.SMEM)] + [pl.BlockSpec(memory_space=pl.ANY)] * len(pieces),
        out_specs=(pl.BlockSpec(memory_space=pltpu.VMEM),) * 2,
        scratch_shapes=[pltpu.VMEM((TOK, 4096), BF16), pltpu.SemaphoreType.DMA((len(parts),))],
        compiler_params=pltpu.CompilerParams(vmem_limit_bytes=VMEM_LIMIT),
        cost_estimate=SMALL,
        name="place_tokens",
    )(jnp.stack([yi, xh, core]).astype(jnp.int32), *pieces)


def weight_blocks(zi, shifts, keep, theirs, normed, normed_other):
    def kernel(at_ref, a_ref, b_ref, n_ref, m_ref, out_ref):
        def term(r, n):
            return lax.dot_general(r[...], n[...], (((0,), (0,)), ((), ())), preferred_element_type=F32)

        out_ref[0] = term(a_ref, n_ref) + term(b_ref, m_ref)

    columns = pl.BlockSpec((TOK, 256), lambda i, at: (0, at[i]))
    whole = pl.BlockSpec((TOK, CH), lambda i, at: (0, 0))
    return pl.pallas_call(
        kernel,
        grid_spec=pltpu.PrefetchScalarGridSpec(
            num_scalar_prefetch=1,
            grid=(len(shifts),),
            in_specs=[columns, columns, whole, whole],
            out_specs=pl.BlockSpec((1, 256, CH), lambda i, at: (i, 0, 0)),
        ),
        out_shape=jax.ShapeDtypeStruct((len(shifts), 256, CH), F32),
        compiler_params=pltpu.CompilerParams(vmem_limit_bytes=VMEM_LIMIT),
        cost_estimate=SMALL,
        name="weight_blocks",
    )(jnp.stack([(zi + k + 8) % 8 for k in shifts]).astype(jnp.int32), keep, theirs, normed, normed_other)


def ring_step(zi, shift, keep, theirs, normed, normed_other, up, down):
    width = up.shape[1]
    at = CH - width

    def kernel(at_ref, a_ref, b_ref, n_ref, m_ref, up_ref, down_ref, up_out, down_out):
        def term(r, n):
            return lax.dot_general(r[...], n[...], (((0,), (0,)), ((), ())), preferred_element_type=F32)

        total = term(a_ref, n_ref) + term(b_ref, m_ref)

        @pl.when(pl.program_id(0) == 0)
        def _():
            if at:
                up_out[:, :at] = total[:, :at].astype(BF16)
            up_out[:, at:] = (total[:, at:] + up_ref[...].astype(F32)).astype(BF16)

        @pl.when(pl.program_id(0) == 1)
        def _():
            if at:
                down_out[:, width:] = total[:, width:].astype(BF16)
            down_out[:, :width] = (total[:, :width] + down_ref[...].astype(F32)).astype(BF16)

    columns = pl.BlockSpec((TOK, 256), lambda i, at: (0, at[i]))
    whole = pl.BlockSpec((TOK, CH), lambda i, at: (0, 0))
    part = pl.BlockSpec((256, width), lambda i, at: (0, 0))
    full = pl.BlockSpec((256, CH), lambda i, at: (0, 0))
    return pl.pallas_call(
        kernel,
        grid_spec=pltpu.PrefetchScalarGridSpec(
            num_scalar_prefetch=1,
            grid=(2,),
            in_specs=[columns, columns, whole, whole, part, part],
            out_specs=(full, full),
        ),
        out_shape=(jax.ShapeDtypeStruct((256, CH), BF16),) * 2,
        compiler_params=pltpu.CompilerParams(vmem_limit_bytes=VMEM_LIMIT),
        cost_estimate=SMALL,
        name="ring_step",
    )(jnp.stack([(zi + k + 8) % 8 for k in (shift, -shift)]).astype(jnp.int32), keep, theirs, normed, normed_other, up, down)


def first_step(zi, keep, theirs, normed, normed_other):
    def kernel(at_ref, a_ref, b_ref, n_ref, m_ref, up_out, down_out):
        def term(r, n):
            return lax.dot_general(r[...], n[...], (((0,), (0,)), ((), ())), preferred_element_type=F32)

        total = term(a_ref, n_ref) + term(b_ref, m_ref)
        up_out[...] = total[:, CH // 2:].astype(BF16)
        down_out[...] = total[:, :CH // 2].astype(BF16)

    columns = pl.BlockSpec((TOK, 256), lambda i, at: (0, at[0]))
    whole = pl.BlockSpec((TOK, CH), lambda i, at: (0, 0))
    part = pl.BlockSpec((256, CH // 2), lambda i, at: (0, 0))
    return pl.pallas_call(
        kernel,
        grid_spec=pltpu.PrefetchScalarGridSpec(
            num_scalar_prefetch=1, grid=(1,), in_specs=[columns, columns, whole, whole], out_specs=(part, part)),
        out_shape=(jax.ShapeDtypeStruct((256, CH // 2), BF16),) * 2,
        compiler_params=pltpu.CompilerParams(vmem_limit_bytes=VMEM_LIMIT),
        cost_estimate=SMALL,
        name="first_step",
    )(((zi + 4) % 8).astype(jnp.int32).reshape(1), keep, theirs, normed, normed_other)


def back_project(keep, give, w_keep, w_give):
    def kernel(a_ref, b_ref, v_ref, w_ref, out_ref):
        out_ref[...] = dot(a_ref[...], v_ref[...]) + dot(b_ref[...], w_ref[...])

    rows = pl.BlockSpec((TOK, 2048), lambda i: (0, 0))
    columns = pl.BlockSpec((2048, 256), lambda i: (0, i))
    return pl.pallas_call(
        kernel,
        grid=(4,),
        in_specs=[rows, rows, columns, columns],
        out_specs=pl.BlockSpec((TOK, 256), lambda i: (0, i)),
        out_shape=jax.ShapeDtypeStruct((TOK, CH), F32),
        compiler_params=pltpu.CompilerParams(vmem_limit_bytes=VMEM_LIMIT),
        cost_estimate=SMALL,
        name="back_project",
    )(keep, give, w_keep, w_give)


def on_device(grad_out, x, z, b, c, dt, rate, skip, gain, w_out):
    zi, xl, core, yi, xh = (lax.axis_index(a) for a in ("z", "xl", "c", "y", "xh"))
    scan = (x, z, b.reshape(TOK, 128), c.reshape(TOK, 128), dt, rate[None], skip[None], gain[None])

    w_keep = lax.all_gather(w_out, ("z", "xl"), axis=0, tiled=True)

    other = send(grad_out, "xh", 1)
    below, above = both_ways(grad_out, grad_out, "y")
    below, above, other, late = tie((below, above, other, scan[6]))

    b_other, a_other = both_ways(other, other, "y")
    far_b, far_a = both_ways(below[:32], above[32:], "y")
    ys, normed = scan_forward(*scan[:6], late, scan[7])
    b_other, a_other, far_b, far_a, normed = tie((b_other, a_other, far_b, far_a, normed))

    far_other = both_ways(b_other[:32], a_other[32:], "y")
    normed_other = send(normed, "c", 1)
    far_other, normed_other = tie((far_other, normed_other))
    pieces = (grad_out, other, below, b_other, above, a_other, far_b, far_a) + far_other
    keep, give = place_tokens(yi, xh, core, *pieces)
    theirs = send(give, "c", 1)
    theirs, keep = tie((theirs, keep))
    w_keep, = tie((w_keep,), theirs)
    w_give = send(w_keep, "c", 1)

    def blocks(*shifts):
        return weight_blocks(zi, shifts, keep, theirs, normed, normed_other)

    up, down = both_ways(*first_step(zi, keep, theirs, normed, normed_other), "z")
    upstream = back_project(keep, give, w_keep, w_give)
    up, down, upstream = tie((up, down, upstream))

    up, down = both_ways(*ring_step(zi, 3, keep, theirs, normed, normed_other, up, down), "z")
    dx, dz, db, dc, ddt, small = scan_backward(upstream, ys, *scan)
    up, down, small = tie((up, down, small))

    up, down = both_ways(*ring_step(zi, 2, keep, theirs, normed, normed_other, up, down), "z")
    last = blocks(1, -1, 0)
    small = small + send(small, "c", 1)
    small = small + send(small, "xl", 1)
    small = small + swap(small, "z", 1)
    up, down, last, small = tie((up, down, last, small))

    def halves(r):
        return lax.dynamic_slice_in_dim(r, (1 - xl) * 128, 128, 0), lax.dynamic_slice_in_dim(r, xl * 128, 128, 0)

    up_leave, up_stay = halves((last[0] + up.astype(F32)).astype(BF16))
    down_leave, down_stay = halves((last[1] + down.astype(F32)).astype(BF16))
    up_leave, down_leave = both_ways(up_leave, down_leave, "z")
    up_stay, down_stay = both_ways(up_stay, down_stay, "z")
    small = small + swap(small, "z", 2)
    leave, stay = halves(last[2])
    up_leave, down_leave, small = tie((up_leave, down_leave, small))
    leave = send(leave + (up_leave.astype(F32) + down_leave.astype(F32)), "xl", 1)
    small = small + swap(small, "z", 4)
    up_stay, down_stay, leave, stay = tie((up_stay, down_stay, leave, stay), small)
    grad_weight = (stay + leave) + (up_stay.astype(F32) + down_stay.astype(F32))
    return (dx, dz, db[:, None], dc[:, None], ddt, small[8, :HEADS], small[9, :HEADS],
            small[:8].reshape(CH), grad_weight)


def solution(mesh):
    fine = jax.sharding.Mesh(mesh.devices.reshape(tuple(AXES.values())), tuple(AXES))
    part = P(DP, TP)
    part3 = P(DP, TP, None)
    head = P(TP)
    return jax.shard_map(
        on_device,
        mesh=fine,
        in_specs=(P(DP + TP, None), part, part, part3, part3, part, head, head, head, part),
        out_specs=(part, part, part3, part3, part, head, head, head, part),
        check_vma=False,
    )
```

```python
import jax
import jax.numpy as jnp
from jax import lax
from jax.experimental import pallas as pl
from jax.experimental.pallas import tpu as pltpu
from jax.sharding import PartitionSpec as P

F32, BF16 = jnp.float32, jnp.bfloat16
HEADS = 16
SPAN = 256
TOK = 512
CH = 1024
HALF = 128
LOG2E = 1.4426950408889634
BIG = 126.0
VMEM_LIMIT = 48 * 1024 * 1024
SMALL = pl.CostEstimate(flops=1000, bytes_accessed=1000, transcendentals=0)


def dot(a, b):
    return jnp.dot(a, b, preferred_element_type=F32)


def dot_nt(a, b):
    return lax.dot_general(a, b, (((1,), (1,)), ((), ())), preferred_element_type=F32)


def split2(v):
    hi = v.astype(BF16)
    return hi, (v - hi.astype(F32)).astype(BF16)


def dot3(a, b, fn):
    ah, al = split2(a)
    bh, bl = split2(b)
    return fn(ah, bh) + (fn(ah, bl) + fn(al, bh))


def spread_matrix(width):
    row = lax.broadcasted_iota(jnp.int32, (128, HEADS * width), 0)
    col = lax.broadcasted_iota(jnp.int32, (128, HEADS * width), 1)
    return jnp.where((row < 48) & ((row & 15) == col // width), 1.0, 0.0).astype(BF16)


def parts3(v):
    lane = lax.broadcasted_iota(jnp.int32, v.shape, 1)
    v = jnp.where(lane < HEADS, v, 0.0)
    one = v.astype(BF16).astype(F32)
    rest = v - one
    two = rest.astype(BF16).astype(F32)
    three = rest - two
    return (one + pltpu.roll(two, 16, 1) + pltpu.roll(three, 32, 1)).astype(BF16)


def cumulate(tri, v):
    one = v.astype(BF16)
    rest = v - one.astype(F32)
    two = rest.astype(BF16)
    three = (rest - two.astype(F32)).astype(BF16)
    return dot(tri, one) + (dot(tri, two) + dot(tri, three))


def triangle(n, lower):
    row = lax.broadcasted_iota(jnp.int32, (n, n), 0)
    col = lax.broadcasted_iota(jnp.int32, (n, n), 1)
    return jnp.where(row >= col if lower else row <= col, 1.0, 0.0).astype(BF16)


def prepare(dt_ref, rate_ref, pad_ref, ratepad_ref):
    pad_ref[...] = jnp.ones((TOK, 128), F32)
    pad_ref[:, :HEADS] = dt_ref[...]
    ratepad_ref[...] = jnp.zeros((8, 128), F32)
    ratepad_ref[0:1, :HEADS] = rate_ref[...]
    rate = -jnp.exp(ratepad_ref[0:1, :])
    tri = triangle(SPAN, True)
    cums, rs = [], []
    for k in range(2):
        dt = pad_ref[k * SPAN:(k + 1) * SPAN, :]
        cum = cumulate(tri, dt * (rate * LOG2E))
        cums.append(cum)
        rs.append(jnp.log2(dt) - cum)
    return rate, cums, rs


def fwd_kernel(x_ref, z_ref, b_ref, c_ref, dt_ref, rate_ref, skip_ref, gain_ref,
               ys_ref, n_ref, pad_ref, ratepad_ref, cexp_ref, rt_ref, s_ref, coef_ref):
    rate, cums, rs = prepare(dt_ref, rate_ref, pad_ref, ratepad_ref)
    wide = spread_matrix(HALF)
    narrow = spread_matrix(64)
    row = lax.broadcasted_iota(jnp.int32, (SPAN, SPAN), 0)
    col = lax.broadcasted_iota(jnp.int32, (SPAN, SPAN), 1)
    ratepad_ref[0:1, :HEADS] = skip_ref[...]
    skip = ratepad_ref[0:1, :]
    for k in range(2):
        rows = slice(k * SPAN, (k + 1) * SPAN)
        cexp_ref[rows, :] = dot(parts3(cums[k]), wide)
        rt_ref[k] = rs[k].T
        bk, ck = b_ref[rows, :], c_ref[rows, :]
        s_ref[k] = jnp.where(row > col, dot_nt(ck, bk), 0.0)
        diag = jnp.sum(bk.astype(F32) * ck.astype(F32), axis=1, keepdims=True)
        coef_ref[rows, :] = dot(parts3(diag * pad_ref[rows, :] + skip), narrow)
    lane = lax.broadcasted_iota(jnp.int32, (SPAN, 128), 1)

    def pair(hp, _):
        cols = pl.ds(pl.multiple_of(hp * 128, 128), 128)
        for k in range(2):
            rows = slice(k * SPAN, (k + 1) * SPAN)
            xp = x_ref[rows, cols]
            tops, bots = [], []
            for half in range(2):
                h = hp * 2 + half
                rrow = rt_ref[k, pl.ds(h, 1), :]
                hcols = pl.ds(pl.multiple_of(h * 128, 128), 128)
                top = cexp_ref[k * SPAN:k * SPAN + HALF, hcols]
                bot = cexp_ref[k * SPAN + HALF:(k + 1) * SPAN, hcols]
                wt = s_ref[k, :HALF, :HALF] * jnp.exp2(jnp.minimum(top + rrow[:, :HALF], BIG))
                wb = s_ref[k, HALF:, :] * jnp.exp2(
                    jnp.minimum(jnp.concatenate([bot, bot], axis=1) + rrow, BIG))
                tops += split2(wt)
                bots += split2(wb)
            yt = dot(jnp.concatenate(tops, axis=0), xp[:HALF])
            yb = dot(jnp.concatenate(bots, axis=0), xp)
            ys = [jnp.concatenate([v[256 * h:256 * h + 128] + v[256 * h + 128:256 * h + 256] for v in (yt, yb)], axis=0)
                  for h in range(2)]
            ys_ref[rows, cols] = jnp.where(lane < 64, ys[0], ys[1])
        return 0

    lax.fori_loop(0, 8, pair, 0)

    s10 = dot_nt(c_ref[SPAN:, :], b_ref[:SPAN, :])
    qdt = parts3(jnp.exp2(cums[0][SPAN - 1:SPAN, :] + rs[0]))
    p = parts3(jnp.exp2(cums[1]))
    for j in range(4):
        cols = slice(j * 256, (j + 1) * 256)
        xq = dot(qdt, narrow[:, cols]) * x_ref[:SPAN, cols].astype(F32)
        ys_ref[SPAN:, cols] += dot(p, narrow[:, cols]) * dot3(s10, xq, dot)

    gain = gain_ref[...]

    def norm(i, _):
        rows = pl.ds(pl.multiple_of(i * 32, 32), 32)
        z = z_ref[rows, :].astype(F32)
        y = ys_ref[rows, :] + coef_ref[rows, :] * x_ref[rows, :].astype(F32)
        gated = y * (z / (1.0 + jnp.exp(-z)))
        inv = lax.rsqrt(jnp.mean(gated * gated, axis=1, keepdims=True) + 1e-05)
        n_ref[rows, :] = (gated * inv * gain).astype(BF16)
        return 0

    lax.fori_loop(0, TOK // 32, norm, 0)


def bwd_kernel(u_hbm, ys_hbm, x_hbm, z_hbm, b_ref, c_ref, dt_ref, rate_ref, skip_ref, gain_ref,
               dx_ref, dz_hbm, db_ref, dc_ref, ddt_ref, small_ref,
               pad_ref, ratepad_ref, rexp_ref, ct_ref, s_ref, coef_ref, dy_ref, dxs_ref, ds_ref, dg_ref,
               u_ref, ys_ref, x_ref, z_ref, dz_ref, sem):
    loads = [
        pltpu.make_async_copy(src, dst, sem.at[j])
        for j, (src, dst) in enumerate(((z_hbm, z_ref), (ys_hbm, ys_ref), (x_hbm, x_ref), (u_hbm, u_ref)))
    ]
    for load in loads:
        load.start()
    rate, cums, rs = prepare(dt_ref, rate_ref, pad_ref, ratepad_ref)
    wide = spread_matrix(HALF)
    narrow = spread_matrix(64)
    row = lax.broadcasted_iota(jnp.int32, (SPAN, SPAN), 0)
    col = lax.broadcasted_iota(jnp.int32, (SPAN, SPAN), 1)
    ratepad_ref[0:1, :HEADS] = skip_ref[...]
    skip = ratepad_ref[0:1, :]
    diags = []
    for k in range(2):
        rows = slice(k * SPAN, (k + 1) * SPAN)
        rexp_ref[rows, :] = dot(parts3(rs[k]), wide)
        ct_ref[k] = cums[k].T
        bk, ck = b_ref[rows, :], c_ref[rows, :]
        s_ref[k] = jnp.where(row < col, dot_nt(bk, ck), 0.0)
        diag = jnp.sum(bk.astype(F32) * ck.astype(F32), axis=1, keepdims=True)
        diags.append(diag)
        coef_ref[rows, :] = dot(parts3(diag * pad_ref[rows, :] + skip), narrow)

    gain = gain_ref[...]
    dg_ref[...] = jnp.zeros((8, CH), F32)

    def gate(i, _):
        rows = pl.ds(pl.multiple_of(i * 32, 32), 32)
        z = z_ref[rows, :].astype(F32)
        y = ys_ref[rows, :] + coef_ref[rows, :] * x_ref[rows, :].astype(F32)
        sig = 1.0 / (1.0 + jnp.exp(-z))
        sz = z * sig
        gated = y * sz
        inv = lax.rsqrt(jnp.mean(gated * gated, axis=1, keepdims=True) + 1e-05)
        unit = gated * inv
        u = u_ref[rows, :]
        ug = u * unit
        dg_ref[...] += (ug[0:8] + ug[8:16]) + (ug[16:24] + ug[24:32])
        v = u * gain
        dgated = inv * (v - unit * jnp.mean(v * unit, axis=1, keepdims=True))
        dy_ref[rows, :] = dgated * sz
        dz_ref[rows, :] = (dgated * y * (sig * (1.0 + z * (1.0 - sig)))).astype(BF16)
        return 0

    for load in loads:
        load.wait()
    lax.fori_loop(0, TOK // 32, gate, 0)
    store = pltpu.make_async_copy(dz_ref, dz_hbm, sem.at[4])
    store.start()

    ds_ref[...] = jnp.zeros((2, SPAN, SPAN), F32)
    lane = lax.broadcasted_iota(jnp.int32, (SPAN, 128), 1)

    def pair(hp, _):
        cols = pl.ds(pl.multiple_of(hp * 128, 128), 128)
        for k in range(2):
            rows = slice(k * SPAN, (k + 1) * SPAN)
            xp = x_ref[rows, cols].astype(F32)
            dh, dl = split2(dy_ref[rows, cols])
            dhl = jnp.concatenate([dh, dl], axis=1)
            xx = []
            for half in range(2):
                xm = jnp.where((lane < 64) if half == 0 else (lane >= 64), xp, 0.0).astype(BF16)
                xx.append(jnp.concatenate([xm, xm], axis=1))
            gts = dot_nt(jnp.concatenate([v[:HALF] for v in xx], axis=0), dhl)
            gbs = dot_nt(jnp.concatenate([v[HALF:] for v in xx], axis=0), dhl[HALF:])
            ths, tls, bhs, bls = [], [], [], []
            dst, dsb = ds_ref[k, :HALF, :], ds_ref[k, HALF:, HALF:]
            for half in range(2):
                h = hp * 2 + half
                part = slice(half * HALF, (half + 1) * HALF)
                crow = ct_ref[k, pl.ds(h, 1), :]
                hcols = pl.ds(pl.multiple_of(h * 128, 128), 128)
                top = rexp_ref[k * SPAN:k * SPAN + HALF, hcols]
                bot = rexp_ref[k * SPAN + HALF:(k + 1) * SPAN, hcols]
                et = jnp.exp2(jnp.minimum(jnp.concatenate([top, top], axis=1) + crow, BIG))
                eb = jnp.exp2(jnp.minimum(bot + crow[:, HALF:], BIG))
                dst = dst + et * gts[part]
                dsb = dsb + eb * gbs[part]
                hi, lo = split2(s_ref[k, :HALF, :] * et)
                ths.append(hi)
                tls.append(lo)
                hi, lo = split2(s_ref[k, HALF:, HALF:] * eb)
                bhs.append(hi)
                bls.append(lo)
            ds_ref[k, :HALF, :] = dst
            ds_ref[k, HALF:, HALF:] = dsb
            ot = dot(jnp.concatenate(ths, axis=0), dhl)
            ob = dot(jnp.concatenate(bhs, axis=0), dhl[HALF:])
            ot = (ot[:, :128] + ot[:, 128:]) + dot(jnp.concatenate(tls, axis=0), dh)
            ob = (ob[:, :128] + ob[:, 128:]) + dot(jnp.concatenate(bls, axis=0), dh[HALF:])
            outs = [jnp.concatenate([v[h * HALF:(h + 1) * HALF] for v in (ot, ob)], axis=0) for h in range(2)]
            dxs_ref[rows, cols] = jnp.where(lane < 64, outs[0], outs[1])
        return 0

    lax.fori_loop(0, 8, pair, 0)

    st = dot_nt(b_ref[:SPAN, :], c_ref[SPAN:, :])
    qdt = parts3(jnp.exp2(cums[0][SPAN - 1:SPAN, :] + rs[0]))
    p = parts3(jnp.exp2(cums[1]))
    dst = jnp.zeros((SPAN, SPAN), F32)
    for j in range(4):
        cols = slice(j * 256, (j + 1) * 256)
        qx = dot(qdt, narrow[:, cols])
        xq = qx * x_ref[:SPAN, cols].astype(F32)
        pdy = dot(p, narrow[:, cols]) * dy_ref[SPAN:, cols]
        dxs_ref[:SPAN, cols] += qx * dot3(st, pdy, dot)
        dst = dst + dot3(xq, pdy, dot_nt)

    seg_row = lax.broadcasted_iota(jnp.int32, (CH, 128), 0)
    seg_col = lax.broadcasted_iota(jnp.int32, (CH, 128), 1)
    seg = jnp.where(seg_row // 64 == seg_col, 1.0, 0.0).astype(BF16)

    def heads_sum(v):
        hi, lo = split2(v)
        return dot(hi, seg) + dot(lo, seg)

    tri = triangle(SPAN, False)
    later = jnp.zeros((1, 128), F32)
    rate_sum = jnp.zeros((1, 128), F32)
    skip_sum = jnp.zeros((1, 128), F32)
    for k in (1, 0):
        rows = slice(k * SPAN, (k + 1) * SPAN)
        xf = x_ref[rows, :].astype(F32)
        dy = dy_ref[rows, :]
        dxs = dxs_ref[rows, :]
        kx = heads_sum(dy * xf)
        r = heads_sum(dy * ys_ref[rows, :])
        q = heads_sum(xf * dxs)
        suffix = cumulate(tri, r - q) + later
        later = suffix[0:1, :]
        dt = pad_ref[rows, :]
        ddt = q / dt + kx * diags[k] + rate * suffix
        ddt_ref[rows, :] = ddt[:, :HEADS]
        rate_sum = rate_sum + rate * jnp.sum(dt * suffix, axis=0, keepdims=True)
        skip_sum = skip_sum + jnp.sum(kx, axis=0, keepdims=True)
        sd = jnp.sum(dt * kx, axis=1, keepdims=True)
        dsk = jnp.where(row < col, ds_ref[k], 0.0)
        bk, ck = b_ref[rows, :], c_ref[rows, :]
        sh, sl = split2(dsk)
        db = dot(sh, ck) + dot(sl, ck) + sd * ck.astype(F32)
        sh, sl = split2(dsk.T)
        dc = dot(sh, bk) + dot(sl, bk) + sd * bk.astype(F32)
        if k == 0:
            oh, ol = split2(dst)
            db = db + dot(oh, c_ref[SPAN:, :]) + dot(ol, c_ref[SPAN:, :])
        else:
            oh, ol = split2(dst.T)
            dc = dc + dot(oh, b_ref[:SPAN, :]) + dot(ol, b_ref[:SPAN, :])
        db_ref[rows, :] = db.astype(BF16)
        dc_ref[rows, :] = dc.astype(BF16)
        dx_ref[rows, :] = (dxs + coef_ref[rows, :] * dy).astype(BF16)

    dg = jnp.sum(dg_ref[...], axis=0, keepdims=True)
    for j in range(8):
        small_ref[j:j + 1, :] = dg[:, j * 128:(j + 1) * 128]
    small_ref[8:9, :] = rate_sum
    small_ref[9:10, :] = skip_sum
    small_ref[10:16, :] = jnp.zeros((6, 128), F32)
    store.wait()


def scan_forward(x, z, b, c, dt, rate, skip, gain):
    return pl.pallas_call(
        fwd_kernel,
        out_shape=(jax.ShapeDtypeStruct((TOK, CH), F32), jax.ShapeDtypeStruct((TOK, CH), BF16)),
        scratch_shapes=[
            pltpu.VMEM((TOK, 128), F32),
            pltpu.VMEM((8, 128), F32),
            pltpu.VMEM((TOK, HEADS * HALF), F32),
            pltpu.VMEM((2, 128, SPAN), F32),
            pltpu.VMEM((2, SPAN, SPAN), F32),
            pltpu.VMEM((TOK, CH), F32),
        ],
        compiler_params=pltpu.CompilerParams(vmem_limit_bytes=VMEM_LIMIT),
        cost_estimate=SMALL,
        name="scan_forward",
    )(x, z, b, c, dt, rate, skip, gain)


def scan_backward(u, ys, x, z, b, c, dt, rate, skip, gain):
    return pl.pallas_call(
        bwd_kernel,
        out_shape=(
            jax.ShapeDtypeStruct((TOK, CH), BF16),
            jax.ShapeDtypeStruct((TOK, CH), BF16),
            jax.ShapeDtypeStruct((TOK, 128), BF16),
            jax.ShapeDtypeStruct((TOK, 128), BF16),
            jax.ShapeDtypeStruct((TOK, HEADS), F32),
            jax.ShapeDtypeStruct((16, 128), F32),
        ),
        scratch_shapes=[
            pltpu.VMEM((TOK, 128), F32),
            pltpu.VMEM((8, 128), F32),
            pltpu.VMEM((TOK, HEADS * HALF), F32),
            pltpu.VMEM((2, 128, SPAN), F32),
            pltpu.VMEM((2, SPAN, SPAN), F32),
            pltpu.VMEM((TOK, CH), F32),
            pltpu.VMEM((TOK, CH), F32),
            pltpu.VMEM((TOK, CH), F32),
            pltpu.VMEM((2, SPAN, SPAN), F32),
            pltpu.VMEM((8, CH), F32),
            pltpu.VMEM((TOK, CH), F32),
            pltpu.VMEM((TOK, CH), F32),
            pltpu.VMEM((TOK, CH), BF16),
            pltpu.VMEM((TOK, CH), BF16),
            pltpu.VMEM((TOK, CH), BF16),
            pltpu.SemaphoreType.DMA((5,)),
        ],
        in_specs=[pl.BlockSpec(memory_space=pltpu.HBM)] * 4 + [pl.BlockSpec(memory_space=pltpu.VMEM)] * 6,
        out_specs=tuple(pl.BlockSpec(memory_space=pltpu.HBM if j == 1 else pltpu.VMEM) for j in range(6)),
        compiler_params=pltpu.CompilerParams(vmem_limit_bytes=VMEM_LIMIT),
        cost_estimate=SMALL,
        name="scan_backward",
    )(u, ys, x, z, b, c, dt, rate, skip, gain)


AXES = {"z": 8, "xl": 2, "c": 2, "y": 4, "xh": 2}
DP = ("z", "xl", "c")
TP = ("y", "xh")


def send(v, axis, shift):
    n = AXES[axis]
    return lax.ppermute(v, axis, [(i, (i + shift) % n) for i in range(n)])


def swap(v, axis, mask):
    return lax.ppermute(v, axis, [(i, i ^ mask) for i in range(AXES[axis])])


def both_ways(up, down, axis):
    return send(up, axis, 1), send(down, axis, -1)


def tie(values, *first):
    return lax.optimization_barrier((tuple(values),) + tuple(first))[0]


def shuffle(name, shapes, plan, scalars, *arrays):
    count = len(plan([0] * len(scalars)))

    def kernel(s_ref, *refs):
        src, dst, sem = refs[:len(arrays)], refs[len(arrays):-1], refs[-1]
        copies = [
            pltpu.make_async_copy(src[i].at[a], dst[o].at[b], sem.at[k])
            for k, (i, a, o, b) in enumerate(plan([s_ref[j] for j in range(len(scalars))]))
        ]
        for copy in copies:
            copy.start()
        for copy in copies:
            copy.wait()

    return pl.pallas_call(
        kernel,
        out_shape=tuple(jax.ShapeDtypeStruct(s, BF16) for s in shapes),
        in_specs=[pl.BlockSpec(memory_space=pltpu.SMEM)] + [pl.BlockSpec(memory_space=pl.ANY)] * len(arrays),
        out_specs=tuple(pl.BlockSpec(memory_space=pltpu.VMEM) for _ in shapes),
        scratch_shapes=[pltpu.SemaphoreType.DMA((count,))],
        cost_estimate=SMALL,
        name=name,
    )(jnp.stack([s.astype(jnp.int32) for s in scalars]), *arrays)


def own_first(rows, core):
    def kernel(core_ref, in_ref, out_ref):
        for j in range(16):
            even = in_ref[:, 256 * j:256 * j + 128]
            odd = in_ref[:, 256 * j + 128:256 * j + 256]
            first = core_ref[0] == 0
            out_ref[:, 128 * j:128 * j + 128] = jnp.where(first, even, odd)
            out_ref[:, 2048 + 128 * j:2048 + 128 * j + 128] = jnp.where(first, odd, even)

    return pl.pallas_call(
        kernel,
        out_shape=jax.ShapeDtypeStruct(rows.shape, rows.dtype),
        in_specs=[pl.BlockSpec(memory_space=pltpu.SMEM), pl.BlockSpec(memory_space=pltpu.VMEM)],
        out_specs=pl.BlockSpec(memory_space=pltpu.VMEM),
        cost_estimate=SMALL,
        name="own_first",
    )(core.astype(jnp.int32).reshape(1), rows)


def at_rows(start, size):
    return (pl.ds(pl.multiple_of(start, 32), size), slice(None)) if not isinstance(start, int) else (slice(start, start + size), slice(None))


def place_tokens(yi, xh, first, *pieces):
    parts = ((0, 64, 0, 0, 0), (1, 64, 0, 1, 0), (2, 64, 3, 0, 0), (3, 64, 3, 1, 0), (4, 64, 1, 0, 0),
             (5, 64, 1, 1, 0), (6, 32, 2, 0, 0), (7, 32, 2, 0, 32), (8, 32, 2, 1, 0), (9, 32, 2, 1, 32))

    def plan(s):
        moves = []
        for piece, size, turn, other, offset in parts:
            start = ((s[0] + turn) % 4) * 128 + (1 - s[1] if other else s[1]) * 64 + offset
            moves.append((piece, (slice(None), slice(first, first + 2048)), 0, at_rows(start, size)))
        return moves

    return shuffle("place_tokens", [(TOK, 2048)], plan, (yi, xh), *pieces)[0]


def weight_blocks(zi, shifts, keep, theirs, normed, normed_other):
    def kernel(at_ref, a_ref, b_ref, n_ref, m_ref, out_ref):
        def term(r, n):
            return lax.dot_general(r[...], n[...], (((0,), (0,)), ((), ())), preferred_element_type=F32)

        out_ref[0] = term(a_ref, n_ref) + term(b_ref, m_ref)

    columns = pl.BlockSpec((TOK, 256), lambda i, at: (0, at[i]))
    whole = pl.BlockSpec((TOK, CH), lambda i, at: (0, 0))
    return pl.pallas_call(
        kernel,
        grid_spec=pltpu.PrefetchScalarGridSpec(
            num_scalar_prefetch=1,
            grid=(len(shifts),),
            in_specs=[columns, columns, whole, whole],
            out_specs=pl.BlockSpec((1, 256, CH), lambda i, at: (i, 0, 0)),
        ),
        out_shape=jax.ShapeDtypeStruct((len(shifts), 256, CH), F32),
        compiler_params=pltpu.CompilerParams(vmem_limit_bytes=VMEM_LIMIT),
        cost_estimate=SMALL,
        name="weight_blocks",
    )(jnp.stack([(zi + k + 8) % 8 for k in shifts]).astype(jnp.int32), keep, theirs, normed, normed_other)


def ring_step(zi, shift, keep, theirs, normed, normed_other, up, down):
    width = up.shape[1]
    at = CH - width

    def kernel(at_ref, a_ref, b_ref, n_ref, m_ref, up_ref, down_ref, up_out, down_out):
        def term(r, n):
            return lax.dot_general(r[...], n[...], (((0,), (0,)), ((), ())), preferred_element_type=F32)

        total = term(a_ref, n_ref) + term(b_ref, m_ref)

        @pl.when(pl.program_id(0) == 0)
        def _():
            if at:
                up_out[:, :at] = total[:, :at].astype(BF16)
            up_out[:, at:] = (total[:, at:] + up_ref[...].astype(F32)).astype(BF16)

        @pl.when(pl.program_id(0) == 1)
        def _():
            if at:
                down_out[:, width:] = total[:, width:].astype(BF16)
            down_out[:, :width] = (total[:, :width] + down_ref[...].astype(F32)).astype(BF16)

    columns = pl.BlockSpec((TOK, 256), lambda i, at: (0, at[i]))
    whole = pl.BlockSpec((TOK, CH), lambda i, at: (0, 0))
    part = pl.BlockSpec((256, width), lambda i, at: (0, 0))
    full = pl.BlockSpec((256, CH), lambda i, at: (0, 0))
    return pl.pallas_call(
        kernel,
        grid_spec=pltpu.PrefetchScalarGridSpec(
            num_scalar_prefetch=1,
            grid=(2,),
            in_specs=[columns, columns, whole, whole, part, part],
            out_specs=(full, full),
        ),
        out_shape=(jax.ShapeDtypeStruct((256, CH), BF16),) * 2,
        compiler_params=pltpu.CompilerParams(vmem_limit_bytes=VMEM_LIMIT),
        cost_estimate=SMALL,
        name="ring_step",
    )(jnp.stack([(zi + k + 8) % 8 for k in (shift, -shift)]).astype(jnp.int32), keep, theirs, normed, normed_other, up, down)


def back_project(core, keep, give, w):
    def kernel(core_ref, a_ref, b_ref, v_ref, w_ref, out_ref):
        out_ref[...] = dot(a_ref[...], v_ref[...].reshape(2048, 256)) + dot(b_ref[...], w_ref[...].reshape(2048, 256))

    rows = pl.BlockSpec((TOK, 2048), lambda i, core: (0, 0))
    return pl.pallas_call(
        kernel,
        grid_spec=pltpu.PrefetchScalarGridSpec(
            num_scalar_prefetch=1,
            grid=(4,),
            in_specs=[
                rows,
                rows,
                pl.BlockSpec((16, None, 128, 256), lambda i, core: (0, core[0], 0, i)),
                pl.BlockSpec((16, None, 128, 256), lambda i, core: (0, 1 - core[0], 0, i)),
            ],
            out_specs=pl.BlockSpec((TOK, 256), lambda i, core: (0, i)),
        ),
        out_shape=jax.ShapeDtypeStruct((TOK, CH), F32),
        compiler_params=pltpu.CompilerParams(vmem_limit_bytes=VMEM_LIMIT),
        cost_estimate=SMALL,
        name="back_project",
    )(core.astype(jnp.int32).reshape(1), keep, give, w, w)


def on_device(grad_out, x, z, b, c, dt, rate, skip, gain, w_out):
    zi, xl, core, yi, xh = (lax.axis_index(a) for a in ("z", "xl", "c", "y", "xh"))
    scan = (x, z, b.reshape(TOK, 128), c.reshape(TOK, 128), dt, rate[None], skip[None], gain[None])

    w = lax.all_gather(w_out, DP, axis=0, tiled=True).reshape(16, 2, 128, CH)

    own = own_first(grad_out, core)
    below, above = both_ways(own, own, "y")
    other = send(own, "xh", 1)
    below, above, other, late = tie((below, above, other, scan[6]))

    b_other, a_other = both_ways(other, other, "y")
    far_b, far_a = both_ways(below[:32], above[32:], "y")
    ys, normed = scan_forward(*scan[:6], late, scan[7])
    b_other, a_other, far_b, far_a, normed = tie((b_other, a_other, far_b, far_a, normed))

    far_other = both_ways(b_other[:32], a_other[32:], "y")
    normed_other = send(normed, "c", 1)
    far_other, normed_other = tie((far_other, normed_other))
    pieces = (own, other, below, b_other, above, a_other, far_b, far_a) + far_other
    give = place_tokens(yi, xh, 2048, *pieces)
    theirs = send(give, "c", 1)
    keep = place_tokens(yi, xh, 0, *tie(pieces, give))
    theirs, keep = tie((theirs, keep))

    def blocks(*shifts):
        return weight_blocks(zi, shifts, keep, theirs, normed, normed_other)

    half = CH // 2
    far = blocks(4)[0].astype(BF16)
    up, down = both_ways(far[:, half:], far[:, :half], "z")
    last = blocks(1, -1, 0)
    w, = tie((w,), last)
    upstream = back_project(core, keep, give, w)
    up, down, last, upstream = tie((up, down, last, upstream))

    up, down = both_ways(*ring_step(zi, 3, keep, theirs, normed, normed_other, up, down), "z")
    dx, dz, db, dc, ddt, small = scan_backward(upstream, ys, *scan)
    up, down, small = tie((up, down, small))

    up, down = both_ways(*ring_step(zi, 2, keep, theirs, normed, normed_other, up, down), "z")
    small = small + send(small, "c", 1)
    small = small + send(small, "xl", 1)
    small = small + swap(small, "z", 1)
    up, down, small = tie((up, down, small))

    def halves(r):
        return lax.dynamic_slice_in_dim(r, (1 - xl) * 128, 128, 0), lax.dynamic_slice_in_dim(r, xl * 128, 128, 0)

    up_leave, up_stay = halves((last[0] + up.astype(F32)).astype(BF16))
    down_leave, down_stay = halves((last[1] + down.astype(F32)).astype(BF16))
    up_leave, down_leave = both_ways(up_leave, down_leave, "z")
    up_stay, down_stay = both_ways(up_stay, down_stay, "z")
    small = small + swap(small, "z", 2)
    leave, stay = halves(last[2])
    up_leave, down_leave, small = tie((up_leave, down_leave, small))
    leave = send(leave + (up_leave.astype(F32) + down_leave.astype(F32)), "xl", 1)
    small = small + swap(small, "z", 4)
    up_stay, down_stay, leave, stay = tie((up_stay, down_stay, leave, stay), small)
    grad_weight = (stay + leave) + (up_stay.astype(F32) + down_stay.astype(F32))
    return (dx, dz, db[:, None], dc[:, None], ddt, small[8, :HEADS], small[9, :HEADS],
            small[:8].reshape(CH), grad_weight)


def solution(mesh):
    fine = jax.sharding.Mesh(mesh.devices.reshape(tuple(AXES.values())), tuple(AXES))
    part = P(DP, TP)
    part3 = P(DP, TP, None)
    head = P(TP)
    return jax.shard_map(
        on_device,
        mesh=fine,
        in_specs=(P(DP + TP, None), part, part, part3, part3, part, head, head, head, part),
        out_specs=(part, part, part3, part3, part, head, head, head, part),
        check_vma=False,
    )
```

```python
import jax
import jax.numpy as jnp
from jax import lax
from jax.experimental import pallas as pl
from jax.experimental.pallas import tpu as pltpu
from jax.sharding import PartitionSpec as P

F32, BF16 = jnp.float32, jnp.bfloat16
HEADS = 16
SPAN = 256
TOK = 512
CH = 1024
HALF = 128
LOG2E = 1.4426950408889634
BIG = 126.0
VMEM_LIMIT = 48 * 1024 * 1024
SMALL = pl.CostEstimate(flops=1000, bytes_accessed=1000, transcendentals=0)


def dot(a, b):
    return jnp.dot(a, b, preferred_element_type=F32)


def dot_nt(a, b):
    return lax.dot_general(a, b, (((1,), (1,)), ((), ())), preferred_element_type=F32)


def split2(v):
    hi = v.astype(BF16)
    return hi, (v - hi.astype(F32)).astype(BF16)


def dot3(a, b, fn):
    ah, al = split2(a)
    bh, bl = split2(b)
    return fn(ah, bh) + (fn(ah, bl) + fn(al, bh))


def spread_matrix(width):
    row = lax.broadcasted_iota(jnp.int32, (128, HEADS * width), 0)
    col = lax.broadcasted_iota(jnp.int32, (128, HEADS * width), 1)
    return jnp.where((row < 48) & ((row & 15) == col // width), 1.0, 0.0).astype(BF16)


def parts3(v):
    lane = lax.broadcasted_iota(jnp.int32, v.shape, 1)
    v = jnp.where(lane < HEADS, v, 0.0)
    one = v.astype(BF16).astype(F32)
    rest = v - one
    two = rest.astype(BF16).astype(F32)
    three = rest - two
    return (one + pltpu.roll(two, 16, 1) + pltpu.roll(three, 32, 1)).astype(BF16)


def cumulate(tri, v):
    one = v.astype(BF16)
    rest = v - one.astype(F32)
    two = rest.astype(BF16)
    three = (rest - two.astype(F32)).astype(BF16)
    return dot(tri, one) + (dot(tri, two) + dot(tri, three))


def triangle(n, lower):
    row = lax.broadcasted_iota(jnp.int32, (n, n), 0)
    col = lax.broadcasted_iota(jnp.int32, (n, n), 1)
    return jnp.where(row >= col if lower else row <= col, 1.0, 0.0).astype(BF16)


def prepare(dt_ref, rate_ref, pad_ref, ratepad_ref):
    pad_ref[...] = jnp.ones((TOK, 128), F32)
    pad_ref[:, :HEADS] = dt_ref[...]
    ratepad_ref[...] = jnp.zeros((8, 128), F32)
    ratepad_ref[0:1, :HEADS] = rate_ref[...]
    rate = -jnp.exp(ratepad_ref[0:1, :])
    tri = triangle(SPAN, True)
    cums, rs = [], []
    for k in range(2):
        dt = pad_ref[k * SPAN:(k + 1) * SPAN, :]
        cum = cumulate(tri, dt * (rate * LOG2E))
        cums.append(cum)
        rs.append(jnp.log2(dt) - cum)
    return rate, cums, rs


def fwd_kernel(x_ref, z_ref, b_ref, c_ref, dt_ref, rate_ref, skip_ref, gain_ref,
               ys_ref, n_ref, pad_ref, ratepad_ref, cexp_ref, rt_ref, s_ref, coef_ref):
    rate, cums, rs = prepare(dt_ref, rate_ref, pad_ref, ratepad_ref)
    wide = spread_matrix(HALF)
    narrow = spread_matrix(64)
    row = lax.broadcasted_iota(jnp.int32, (SPAN, SPAN), 0)
    col = lax.broadcasted_iota(jnp.int32, (SPAN, SPAN), 1)
    ratepad_ref[0:1, :HEADS] = skip_ref[...]
    skip = ratepad_ref[0:1, :]
    for k in range(2):
        rows = slice(k * SPAN, (k + 1) * SPAN)
        cexp_ref[rows, :] = dot(parts3(cums[k]), wide)
        rt_ref[k] = rs[k].T
        bk, ck = b_ref[rows, :], c_ref[rows, :]
        s_ref[k] = jnp.where(row > col, dot_nt(ck, bk), 0.0)
        diag = jnp.sum(bk.astype(F32) * ck.astype(F32), axis=1, keepdims=True)
        coef_ref[rows, :] = dot(parts3(diag * pad_ref[rows, :] + skip), narrow)
    lane = lax.broadcasted_iota(jnp.int32, (SPAN, 128), 1)

    def pair(hp, _):
        cols = pl.ds(pl.multiple_of(hp * 128, 128), 128)
        for k in range(2):
            rows = slice(k * SPAN, (k + 1) * SPAN)
            xp = x_ref[rows, cols]
            tops, bots = [], []
            for half in range(2):
                h = hp * 2 + half
                rrow = rt_ref[k, pl.ds(h, 1), :]
                hcols = pl.ds(pl.multiple_of(h * 128, 128), 128)
                top = cexp_ref[k * SPAN:k * SPAN + HALF, hcols]
                bot = cexp_ref[k * SPAN + HALF:(k + 1) * SPAN, hcols]
                wt = s_ref[k, :HALF, :HALF] * jnp.exp2(jnp.minimum(top + rrow[:, :HALF], BIG))
                wb = s_ref[k, HALF:, :] * jnp.exp2(
                    jnp.minimum(jnp.concatenate([bot, bot], axis=1) + rrow, BIG))
                tops += split2(wt)
                bots += split2(wb)
            yt = dot(jnp.concatenate(tops, axis=0), xp[:HALF])
            yb = dot(jnp.concatenate(bots, axis=0), xp)
            ys = [jnp.concatenate([v[256 * h:256 * h + 128] + v[256 * h + 128:256 * h + 256] for v in (yt, yb)], axis=0)
                  for h in range(2)]
            ys_ref[rows, cols] = jnp.where(lane < 64, ys[0], ys[1])
        return 0

    lax.fori_loop(0, 8, pair, 0)

    s10 = dot_nt(c_ref[SPAN:, :], b_ref[:SPAN, :])
    qdt = parts3(jnp.exp2(cums[0][SPAN - 1:SPAN, :] + rs[0]))
    p = parts3(jnp.exp2(cums[1]))
    for j in range(4):
        cols = slice(j * 256, (j + 1) * 256)
        xq = dot(qdt, narrow[:, cols]) * x_ref[:SPAN, cols].astype(F32)
        ys_ref[SPAN:, cols] += dot(p, narrow[:, cols]) * dot3(s10, xq, dot)

    gain = gain_ref[...]

    def norm(i, _):
        rows = pl.ds(pl.multiple_of(i * 32, 32), 32)
        z = z_ref[rows, :].astype(F32)
        y = ys_ref[rows, :] + coef_ref[rows, :] * x_ref[rows, :].astype(F32)
        gated = y * (z / (1.0 + jnp.exp(-z)))
        inv = lax.rsqrt(jnp.mean(gated * gated, axis=1, keepdims=True) + 1e-05)
        n_ref[rows, :] = (gated * inv * gain).astype(BF16)
        return 0

    lax.fori_loop(0, TOK // 32, norm, 0)


def bwd_kernel(u_hbm, ys_hbm, x_hbm, z_hbm, b_ref, c_ref, dt_ref, rate_ref, skip_ref, gain_ref,
               dx_ref, dz_hbm, db_ref, dc_ref, ddt_ref, small_ref,
               pad_ref, ratepad_ref, rexp_ref, ct_ref, s_ref, coef_ref, dy_ref, dxs_ref, ds_ref, dg_ref,
               u_ref, ys_ref, x_ref, z_ref, dz_ref, sem):
    loads = [
        pltpu.make_async_copy(src, dst, sem.at[j])
        for j, (src, dst) in enumerate(((z_hbm, z_ref), (ys_hbm, ys_ref), (x_hbm, x_ref), (u_hbm, u_ref)))
    ]
    for load in loads:
        load.start()
    rate, cums, rs = prepare(dt_ref, rate_ref, pad_ref, ratepad_ref)
    wide = spread_matrix(HALF)
    narrow = spread_matrix(64)
    row = lax.broadcasted_iota(jnp.int32, (SPAN, SPAN), 0)
    col = lax.broadcasted_iota(jnp.int32, (SPAN, SPAN), 1)
    ratepad_ref[0:1, :HEADS] = skip_ref[...]
    skip = ratepad_ref[0:1, :]
    diags = []
    for k in range(2):
        rows = slice(k * SPAN, (k + 1) * SPAN)
        rexp_ref[rows, :] = dot(parts3(rs[k]), wide)
        ct_ref[k] = cums[k].T
        bk, ck = b_ref[rows, :], c_ref[rows, :]
        s_ref[k] = jnp.where(row < col, dot_nt(bk, ck), 0.0)
        diag = jnp.sum(bk.astype(F32) * ck.astype(F32), axis=1, keepdims=True)
        diags.append(diag)
        coef_ref[rows, :] = dot(parts3(diag * pad_ref[rows, :] + skip), narrow)

    gain = gain_ref[...]
    dg_ref[...] = jnp.zeros((8, CH), F32)

    def gate(i, _):
        rows = pl.ds(pl.multiple_of(i * 32, 32), 32)
        z = z_ref[rows, :].astype(F32)
        y = ys_ref[rows, :] + coef_ref[rows, :] * x_ref[rows, :].astype(F32)
        sig = 1.0 / (1.0 + jnp.exp(-z))
        sz = z * sig
        gated = y * sz
        inv = lax.rsqrt(jnp.mean(gated * gated, axis=1, keepdims=True) + 1e-05)
        unit = gated * inv
        u = u_ref[rows, :]
        ug = u * unit
        dg_ref[...] += (ug[0:8] + ug[8:16]) + (ug[16:24] + ug[24:32])
        v = u * gain
        dgated = inv * (v - unit * jnp.mean(v * unit, axis=1, keepdims=True))
        dy_ref[rows, :] = dgated * sz
        dz_ref[rows, :] = (dgated * y * (sig * (1.0 + z * (1.0 - sig)))).astype(BF16)
        return 0

    for load in loads:
        load.wait()
    lax.fori_loop(0, TOK // 32, gate, 0)
    store = pltpu.make_async_copy(dz_ref, dz_hbm, sem.at[4])
    store.start()

    ds_ref[...] = jnp.zeros((2, SPAN, SPAN), F32)
    lane = lax.broadcasted_iota(jnp.int32, (SPAN, 128), 1)

    def pair(hp, _):
        cols = pl.ds(pl.multiple_of(hp * 128, 128), 128)
        for k in range(2):
            rows = slice(k * SPAN, (k + 1) * SPAN)
            xp = x_ref[rows, cols].astype(F32)
            dh, dl = split2(dy_ref[rows, cols])
            dhl = jnp.concatenate([dh, dl], axis=1)
            xx = []
            for half in range(2):
                xm = jnp.where((lane < 64) if half == 0 else (lane >= 64), xp, 0.0).astype(BF16)
                xx.append(jnp.concatenate([xm, xm], axis=1))
            gts = dot_nt(jnp.concatenate([v[:HALF] for v in xx], axis=0), dhl)
            gbs = dot_nt(jnp.concatenate([v[HALF:] for v in xx], axis=0), dhl[HALF:])
            ths, tls, bhs, bls = [], [], [], []
            dst, dsb = ds_ref[k, :HALF, :], ds_ref[k, HALF:, HALF:]
            for half in range(2):
                h = hp * 2 + half
                part = slice(half * HALF, (half + 1) * HALF)
                crow = ct_ref[k, pl.ds(h, 1), :]
                hcols = pl.ds(pl.multiple_of(h * 128, 128), 128)
                top = rexp_ref[k * SPAN:k * SPAN + HALF, hcols]
                bot = rexp_ref[k * SPAN + HALF:(k + 1) * SPAN, hcols]
                et = jnp.exp2(jnp.minimum(jnp.concatenate([top, top], axis=1) + crow, BIG))
                eb = jnp.exp2(jnp.minimum(bot + crow[:, HALF:], BIG))
                dst = dst + et * gts[part]
                dsb = dsb + eb * gbs[part]
                hi, lo = split2(s_ref[k, :HALF, :] * et)
                ths.append(hi)
                tls.append(lo)
                hi, lo = split2(s_ref[k, HALF:, HALF:] * eb)
                bhs.append(hi)
                bls.append(lo)
            ds_ref[k, :HALF, :] = dst
            ds_ref[k, HALF:, HALF:] = dsb
            ot = dot(jnp.concatenate(ths, axis=0), dhl)
            ob = dot(jnp.concatenate(bhs, axis=0), dhl[HALF:])
            ot = (ot[:, :128] + ot[:, 128:]) + dot(jnp.concatenate(tls, axis=0), dh)
            ob = (ob[:, :128] + ob[:, 128:]) + dot(jnp.concatenate(bls, axis=0), dh[HALF:])
            outs = [jnp.concatenate([v[h * HALF:(h + 1) * HALF] for v in (ot, ob)], axis=0) for h in range(2)]
            dxs_ref[rows, cols] = jnp.where(lane < 64, outs[0], outs[1])
        return 0

    lax.fori_loop(0, 8, pair, 0)

    st = dot_nt(b_ref[:SPAN, :], c_ref[SPAN:, :])
    qdt = parts3(jnp.exp2(cums[0][SPAN - 1:SPAN, :] + rs[0]))
    p = parts3(jnp.exp2(cums[1]))
    dst = jnp.zeros((SPAN, SPAN), F32)
    for j in range(4):
        cols = slice(j * 256, (j + 1) * 256)
        qx = dot(qdt, narrow[:, cols])
        xq = qx * x_ref[:SPAN, cols].astype(F32)
        pdy = dot(p, narrow[:, cols]) * dy_ref[SPAN:, cols]
        dxs_ref[:SPAN, cols] += qx * dot3(st, pdy, dot)
        dst = dst + dot3(xq, pdy, dot_nt)

    seg_row = lax.broadcasted_iota(jnp.int32, (CH, 128), 0)
    seg_col = lax.broadcasted_iota(jnp.int32, (CH, 128), 1)
    seg = jnp.where(seg_row // 64 == seg_col, 1.0, 0.0).astype(BF16)

    def heads_sum(v):
        hi, lo = split2(v)
        return dot(hi, seg) + dot(lo, seg)

    tri = triangle(SPAN, False)
    later = jnp.zeros((1, 128), F32)
    rate_sum = jnp.zeros((1, 128), F32)
    skip_sum = jnp.zeros((1, 128), F32)
    for k in (1, 0):
        rows = slice(k * SPAN, (k + 1) * SPAN)
        xf = x_ref[rows, :].astype(F32)
        dy = dy_ref[rows, :]
        dxs = dxs_ref[rows, :]
        kx = heads_sum(dy * xf)
        r = heads_sum(dy * ys_ref[rows, :])
        q = heads_sum(xf * dxs)
        suffix = cumulate(tri, r - q) + later
        later = suffix[0:1, :]
        dt = pad_ref[rows, :]
        ddt = q / dt + kx * diags[k] + rate * suffix
        ddt_ref[rows, :] = ddt[:, :HEADS]
        rate_sum = rate_sum + rate * jnp.sum(dt * suffix, axis=0, keepdims=True)
        skip_sum = skip_sum + jnp.sum(kx, axis=0, keepdims=True)
        sd = jnp.sum(dt * kx, axis=1, keepdims=True)
        dsk = jnp.where(row < col, ds_ref[k], 0.0)
        bk, ck = b_ref[rows, :], c_ref[rows, :]
        sh, sl = split2(dsk)
        db = dot(sh, ck) + dot(sl, ck) + sd * ck.astype(F32)
        sh, sl = split2(dsk.T)
        dc = dot(sh, bk) + dot(sl, bk) + sd * bk.astype(F32)
        if k == 0:
            oh, ol = split2(dst)
            db = db + dot(oh, c_ref[SPAN:, :]) + dot(ol, c_ref[SPAN:, :])
        else:
            oh, ol = split2(dst.T)
            dc = dc + dot(oh, b_ref[:SPAN, :]) + dot(ol, b_ref[:SPAN, :])
        db_ref[rows, :] = db.astype(BF16)
        dc_ref[rows, :] = dc.astype(BF16)
        dx_ref[rows, :] = (dxs + coef_ref[rows, :] * dy).astype(BF16)

    dg = jnp.sum(dg_ref[...], axis=0, keepdims=True)
    for j in range(8):
        small_ref[j:j + 1, :] = dg[:, j * 128:(j + 1) * 128]
    small_ref[8:9, :] = rate_sum
    small_ref[9:10, :] = skip_sum
    small_ref[10:16, :] = jnp.zeros((6, 128), F32)
    store.wait()


def scan_forward(x, z, b, c, dt, rate, skip, gain):
    return pl.pallas_call(
        fwd_kernel,
        out_shape=(jax.ShapeDtypeStruct((TOK, CH), F32), jax.ShapeDtypeStruct((TOK, CH), BF16)),
        scratch_shapes=[
            pltpu.VMEM((TOK, 128), F32),
            pltpu.VMEM((8, 128), F32),
            pltpu.VMEM((TOK, HEADS * HALF), F32),
            pltpu.VMEM((2, 128, SPAN), F32),
            pltpu.VMEM((2, SPAN, SPAN), F32),
            pltpu.VMEM((TOK, CH), F32),
        ],
        compiler_params=pltpu.CompilerParams(vmem_limit_bytes=VMEM_LIMIT),
        cost_estimate=SMALL,
        name="scan_forward",
    )(x, z, b, c, dt, rate, skip, gain)


def scan_backward(u, ys, x, z, b, c, dt, rate, skip, gain):
    return pl.pallas_call(
        bwd_kernel,
        out_shape=(
            jax.ShapeDtypeStruct((TOK, CH), BF16),
            jax.ShapeDtypeStruct((TOK, CH), BF16),
            jax.ShapeDtypeStruct((TOK, 128), BF16),
            jax.ShapeDtypeStruct((TOK, 128), BF16),
            jax.ShapeDtypeStruct((TOK, HEADS), F32),
            jax.ShapeDtypeStruct((16, 128), F32),
        ),
        scratch_shapes=[
            pltpu.VMEM((TOK, 128), F32),
            pltpu.VMEM((8, 128), F32),
            pltpu.VMEM((TOK, HEADS * HALF), F32),
            pltpu.VMEM((2, 128, SPAN), F32),
            pltpu.VMEM((2, SPAN, SPAN), F32),
            pltpu.VMEM((TOK, CH), F32),
            pltpu.VMEM((TOK, CH), F32),
            pltpu.VMEM((TOK, CH), F32),
            pltpu.VMEM((2, SPAN, SPAN), F32),
            pltpu.VMEM((8, CH), F32),
            pltpu.VMEM((TOK, CH), F32),
            pltpu.VMEM((TOK, CH), F32),
            pltpu.VMEM((TOK, CH), BF16),
            pltpu.VMEM((TOK, CH), BF16),
            pltpu.VMEM((TOK, CH), BF16),
            pltpu.SemaphoreType.DMA((5,)),
        ],
        in_specs=[pl.BlockSpec(memory_space=pltpu.HBM)] * 4 + [pl.BlockSpec(memory_space=pltpu.VMEM)] * 6,
        out_specs=tuple(pl.BlockSpec(memory_space=pltpu.HBM if j == 1 else pltpu.VMEM) for j in range(6)),
        compiler_params=pltpu.CompilerParams(vmem_limit_bytes=VMEM_LIMIT),
        cost_estimate=SMALL,
        name="scan_backward",
    )(u, ys, x, z, b, c, dt, rate, skip, gain)


AXES = {"z": 8, "xl": 2, "c": 2, "y": 4, "xh": 2}
DP = ("z", "xl", "c")
TP = ("y", "xh")


def send(v, axis, shift):
    n = AXES[axis]
    return lax.ppermute(v, axis, [(i, (i + shift) % n) for i in range(n)])


def swap(v, axis, mask):
    return lax.ppermute(v, axis, [(i, i ^ mask) for i in range(AXES[axis])])


def both_ways(up, down, axis):
    return send(up, axis, 1), send(down, axis, -1)


def tie(values, *first):
    return lax.optimization_barrier((tuple(values),) + tuple(first))[0]


def shuffle(name, shapes, plan, scalars, *arrays):
    count = len(plan([0] * len(scalars)))

    def kernel(s_ref, *refs):
        src, dst, sem = refs[:len(arrays)], refs[len(arrays):-1], refs[-1]
        copies = [
            pltpu.make_async_copy(src[i].at[a], dst[o].at[b], sem.at[k])
            for k, (i, a, o, b) in enumerate(plan([s_ref[j] for j in range(len(scalars))]))
        ]
        for copy in copies:
            copy.start()
        for copy in copies:
            copy.wait()

    return pl.pallas_call(
        kernel,
        out_shape=tuple(jax.ShapeDtypeStruct(s, BF16) for s in shapes),
        in_specs=[pl.BlockSpec(memory_space=pltpu.SMEM)] + [pl.BlockSpec(memory_space=pl.ANY)] * len(arrays),
        out_specs=tuple(pl.BlockSpec(memory_space=pltpu.VMEM) for _ in shapes),
        scratch_shapes=[pltpu.SemaphoreType.DMA((count,))],
        cost_estimate=SMALL,
        name=name,
    )(jnp.stack([s.astype(jnp.int32) for s in scalars]), *arrays)


def own_first(rows, core):
    def kernel(core_ref, in_ref, out_ref):
        for j in range(16):
            even = in_ref[:, 256 * j:256 * j + 128]
            odd = in_ref[:, 256 * j + 128:256 * j + 256]
            first = core_ref[0] == 0
            out_ref[:, 128 * j:128 * j + 128] = jnp.where(first, even, odd)
            out_ref[:, 2048 + 128 * j:2048 + 128 * j + 128] = jnp.where(first, odd, even)

    return pl.pallas_call(
        kernel,
        out_shape=jax.ShapeDtypeStruct(rows.shape, rows.dtype),
        in_specs=[pl.BlockSpec(memory_space=pltpu.SMEM), pl.BlockSpec(memory_space=pltpu.VMEM)],
        out_specs=pl.BlockSpec(memory_space=pltpu.VMEM),
        cost_estimate=SMALL,
        name="own_first",
    )(core.astype(jnp.int32).reshape(1), rows)


def at_rows(start, size):
    return (pl.ds(pl.multiple_of(start, 32), size), slice(None)) if not isinstance(start, int) else (slice(start, start + size), slice(None))


def place_tokens(yi, xh, first, *pieces):
    parts = ((0, 64, 0, 0, 0), (1, 64, 0, 1, 0), (2, 64, 3, 0, 0), (3, 64, 3, 1, 0), (4, 64, 1, 0, 0),
             (5, 64, 1, 1, 0), (6, 32, 2, 0, 0), (7, 32, 2, 0, 32), (8, 32, 2, 1, 0), (9, 32, 2, 1, 32))

    def plan(s):
        moves = []
        for piece, size, turn, other, offset in parts:
            start = ((s[0] + turn) % 4) * 128 + (1 - s[1] if other else s[1]) * 64 + offset
            moves.append((piece, (slice(None), slice(first, first + 2048)), 0, at_rows(start, size)))
        return moves

    return shuffle("place_tokens", [(TOK, 2048)], plan, (yi, xh), *pieces)[0]


def weight_blocks(zi, shifts, keep, theirs, normed, normed_other):
    def kernel(at_ref, a_ref, b_ref, n_ref, m_ref, out_ref):
        def term(r, n):
            return lax.dot_general(r[...], n[...], (((0,), (0,)), ((), ())), preferred_element_type=F32)

        out_ref[0] = term(a_ref, n_ref) + term(b_ref, m_ref)

    columns = pl.BlockSpec((TOK, 256), lambda i, at: (0, at[i]))
    whole = pl.BlockSpec((TOK, CH), lambda i, at: (0, 0))
    return pl.pallas_call(
        kernel,
        grid_spec=pltpu.PrefetchScalarGridSpec(
            num_scalar_prefetch=1,
            grid=(len(shifts),),
            in_specs=[columns, columns, whole, whole],
            out_specs=pl.BlockSpec((1, 256, CH), lambda i, at: (i, 0, 0)),
        ),
        out_shape=jax.ShapeDtypeStruct((len(shifts), 256, CH), F32),
        compiler_params=pltpu.CompilerParams(vmem_limit_bytes=VMEM_LIMIT),
        cost_estimate=SMALL,
        name="weight_blocks",
    )(jnp.stack([(zi + k + 8) % 8 for k in shifts]).astype(jnp.int32), keep, theirs, normed, normed_other)


def ring_step(zi, shift, keep, theirs, normed, normed_other, up, down):
    width = up.shape[1]
    at = CH - width

    def kernel(at_ref, a_ref, b_ref, n_ref, m_ref, up_ref, down_ref, up_out, down_out):
        def term(r, n):
            return lax.dot_general(r[...], n[...], (((0,), (0,)), ((), ())), preferred_element_type=F32)

        total = term(a_ref, n_ref) + term(b_ref, m_ref)

        @pl.when(pl.program_id(0) == 0)
        def _():
            if at:
                up_out[:, :at] = total[:, :at].astype(BF16)
            up_out[:, at:] = (total[:, at:] + up_ref[...].astype(F32)).astype(BF16)

        @pl.when(pl.program_id(0) == 1)
        def _():
            if at:
                down_out[:, width:] = total[:, width:].astype(BF16)
            down_out[:, :width] = (total[:, :width] + down_ref[...].astype(F32)).astype(BF16)

    columns = pl.BlockSpec((TOK, 256), lambda i, at: (0, at[i]))
    whole = pl.BlockSpec((TOK, CH), lambda i, at: (0, 0))
    part = pl.BlockSpec((256, width), lambda i, at: (0, 0))
    full = pl.BlockSpec((256, CH), lambda i, at: (0, 0))
    return pl.pallas_call(
        kernel,
        grid_spec=pltpu.PrefetchScalarGridSpec(
            num_scalar_prefetch=1,
            grid=(2,),
            in_specs=[columns, columns, whole, whole, part, part],
            out_specs=(full, full),
        ),
        out_shape=(jax.ShapeDtypeStruct((256, CH), BF16),) * 2,
        compiler_params=pltpu.CompilerParams(vmem_limit_bytes=VMEM_LIMIT),
        cost_estimate=SMALL,
        name="ring_step",
    )(jnp.stack([(zi + k + 8) % 8 for k in (shift, -shift)]).astype(jnp.int32), keep, theirs, normed, normed_other, up, down)


def back_project(core, keep, give, w):
    def kernel(core_ref, a_ref, b_ref, v_ref, w_ref, out_ref):
        out_ref[...] = dot(a_ref[...], v_ref[...].reshape(2048, 256)) + dot(b_ref[...], w_ref[...].reshape(2048, 256))

    rows = pl.BlockSpec((TOK, 2048), lambda i, core: (0, 0))
    return pl.pallas_call(
        kernel,
        grid_spec=pltpu.PrefetchScalarGridSpec(
            num_scalar_prefetch=1,
            grid=(4,),
            in_specs=[
                rows,
                rows,
                pl.BlockSpec((16, None, 128, 256), lambda i, core: (0, core[0], 0, i)),
                pl.BlockSpec((16, None, 128, 256), lambda i, core: (0, 1 - core[0], 0, i)),
            ],
            out_specs=pl.BlockSpec((TOK, 256), lambda i, core: (0, i)),
        ),
        out_shape=jax.ShapeDtypeStruct((TOK, CH), F32),
        compiler_params=pltpu.CompilerParams(vmem_limit_bytes=VMEM_LIMIT),
        cost_estimate=SMALL,
        name="back_project",
    )(core.astype(jnp.int32).reshape(1), keep, give, w, w)


def on_device(grad_out, x, z, b, c, dt, rate, skip, gain, w_out):
    zi, xl, core, yi, xh = (lax.axis_index(a) for a in ("z", "xl", "c", "y", "xh"))
    scan = (x, z, b.reshape(TOK, 128), c.reshape(TOK, 128), dt, rate[None], skip[None], gain[None])

    w = lax.all_gather(w_out, DP, axis=0, tiled=True).reshape(16, 2, 128, CH)

    own = own_first(grad_out, core)
    below, above = both_ways(own, own, "y")
    other = send(own, "xh", 1)
    below, above, other, late = tie((below, above, other, scan[6]))

    b_other, a_other = both_ways(other, other, "y")
    far_b, far_a = both_ways(below[:32], above[32:], "y")
    ys, normed = scan_forward(*scan[:6], late, scan[7])
    b_other, a_other, far_b, far_a, normed = tie((b_other, a_other, far_b, far_a, normed))

    far_other = both_ways(b_other[:32], a_other[32:], "y")
    normed_other = send(normed, "c", 1)
    far_other, normed_other = tie((far_other, normed_other))
    pieces = (own, other, below, b_other, above, a_other, far_b, far_a) + far_other
    give = place_tokens(yi, xh, 2048, *pieces)
    theirs = send(give, "c", 1)
    keep = place_tokens(yi, xh, 0, *tie(pieces, give))
    theirs, keep = tie((theirs, keep))

    def blocks(*shifts):
        return weight_blocks(zi, shifts, keep, theirs, normed, normed_other)

    half = CH // 2
    far = blocks(4)[0].astype(BF16)
    up, down = both_ways(far[:, half:], far[:, :half], "z")
    mine = blocks(0)[0]
    w, = tie((w,), mine)
    upstream = back_project(core, keep, give, w)
    up, down, mine, upstream = tie((up, down, mine, upstream))

    up, down = both_ways(*ring_step(zi, 3, keep, theirs, normed, normed_other, up, down), "z")
    dx, dz, db, dc, ddt, small = scan_backward(upstream, ys, *scan)
    up, down, small = tie((up, down, small))

    up, down = both_ways(*ring_step(zi, 2, keep, theirs, normed, normed_other, up, down), "z")
    last = blocks(1, -1)
    small = small + send(small, "c", 1)
    small = small + send(small, "xl", 1)
    small = small + swap(small, "z", 1)
    up, down, last, small = tie((up, down, last, small))

    def halves(r):
        return lax.dynamic_slice_in_dim(r, (1 - xl) * 128, 128, 0), lax.dynamic_slice_in_dim(r, xl * 128, 128, 0)

    up_leave, up_stay = halves((last[0] + up.astype(F32)).astype(BF16))
    down_leave, down_stay = halves((last[1] + down.astype(F32)).astype(BF16))
    up_leave, down_leave = both_ways(up_leave, down_leave, "z")
    up_stay, down_stay = both_ways(up_stay, down_stay, "z")
    small = small + swap(small, "z", 2)
    leave, stay = halves(mine)
    up_leave, down_leave, small = tie((up_leave, down_leave, small))
    leave = send(leave + (up_leave.astype(F32) + down_leave.astype(F32)), "xl", 1)
    small = small + swap(small, "z", 4)
    up_stay, down_stay, leave, stay = tie((up_stay, down_stay, leave, stay), small)
    grad_weight = (stay + leave) + (up_stay.astype(F32) + down_stay.astype(F32))
    return (dx, dz, db[:, None], dc[:, None], ddt, small[8, :HEADS], small[9, :HEADS],
            small[:8].reshape(CH), grad_weight)


def solution(mesh):
    fine = jax.sharding.Mesh(mesh.devices.reshape(tuple(AXES.values())), tuple(AXES))
    part = P(DP, TP)
    part3 = P(DP, TP, None)
    head = P(TP)
    return jax.shard_map(
        on_device,
        mesh=fine,
        in_specs=(P(DP + TP, None), part, part, part3, part3, part, head, head, head, part),
        out_specs=(part, part, part3, part3, part, head, head, head, part),
        check_vma=False,
    )
```

```python
import jax
import jax.numpy as jnp
from jax import lax
from jax.experimental import pallas as pl
from jax.experimental.pallas import tpu as pltpu
from jax.sharding import PartitionSpec as P

F32, BF16 = jnp.float32, jnp.bfloat16
HEADS = 16
SPAN = 256
TOK = 512
CH = 1024
HALF = 128
LOG2E = 1.4426950408889634
BIG = 126.0
VMEM_LIMIT = 48 * 1024 * 1024
SMALL = pl.CostEstimate(flops=1000, bytes_accessed=1000, transcendentals=0)


def dot(a, b):
    return jnp.dot(a, b, preferred_element_type=F32)


def dot_nt(a, b):
    return lax.dot_general(a, b, (((1,), (1,)), ((), ())), preferred_element_type=F32)


def split2(v):
    hi = v.astype(BF16)
    return hi, (v - hi.astype(F32)).astype(BF16)


def dot3(a, b, fn):
    ah, al = split2(a)
    bh, bl = split2(b)
    return fn(ah, bh) + (fn(ah, bl) + fn(al, bh))


def spread_matrix(width):
    row = lax.broadcasted_iota(jnp.int32, (128, HEADS * width), 0)
    col = lax.broadcasted_iota(jnp.int32, (128, HEADS * width), 1)
    return jnp.where((row < 48) & ((row & 15) == col >> (width.bit_length() - 1)), 1.0, 0.0).astype(BF16)


def parts3(v):
    lane = lax.broadcasted_iota(jnp.int32, v.shape, 1)
    v = jnp.where(lane < HEADS, v, 0.0)
    one = v.astype(BF16).astype(F32)
    rest = v - one
    two = rest.astype(BF16).astype(F32)
    three = rest - two
    return (one + pltpu.roll(two, 16, 1) + pltpu.roll(three, 32, 1)).astype(BF16)


def cumulate(tri, v):
    one = v.astype(BF16)
    rest = v - one.astype(F32)
    two = rest.astype(BF16)
    three = (rest - two.astype(F32)).astype(BF16)
    return dot(tri, one) + (dot(tri, two) + dot(tri, three))


def triangle(n, lower):
    row = lax.broadcasted_iota(jnp.int32, (n, n), 0)
    col = lax.broadcasted_iota(jnp.int32, (n, n), 1)
    return jnp.where(row >= col if lower else row <= col, 1.0, 0.0).astype(BF16)


def prepare(dt_ref, rate_ref, pad_ref, ratepad_ref):
    pad_ref[...] = jnp.ones((TOK, 128), F32)
    pad_ref[:, :HEADS] = dt_ref[...]
    ratepad_ref[...] = jnp.zeros((8, 128), F32)
    ratepad_ref[0:1, :HEADS] = rate_ref[...]
    rate = -jnp.exp(ratepad_ref[0:1, :])
    tri = triangle(SPAN, True)
    cums, rs = [], []
    for k in range(2):
        dt = pad_ref[k * SPAN:(k + 1) * SPAN, :]
        cum = cumulate(tri, dt * (rate * LOG2E))
        cums.append(cum)
        rs.append(jnp.log2(dt) - cum)
    return rate, cums, rs


def fwd_kernel(x_ref, z_ref, b_ref, c_ref, dt_ref, rate_ref, skip_ref, gain_ref,
               ys_ref, n_ref, pad_ref, ratepad_ref, cexp_ref, rt_ref, s_ref, coef_ref):
    rate, cums, rs = prepare(dt_ref, rate_ref, pad_ref, ratepad_ref)
    wide = spread_matrix(HALF)
    narrow = spread_matrix(64)
    row = lax.broadcasted_iota(jnp.int32, (SPAN, SPAN), 0)
    col = lax.broadcasted_iota(jnp.int32, (SPAN, SPAN), 1)
    ratepad_ref[0:1, :HEADS] = skip_ref[...]
    skip = ratepad_ref[0:1, :]
    for k in range(2):
        rows = slice(k * SPAN, (k + 1) * SPAN)
        cexp_ref[rows, :] = dot(parts3(cums[k]), wide)
        rt_ref[k] = rs[k].T
        bk, ck = b_ref[rows, :], c_ref[rows, :]
        s_ref[k] = jnp.where(row > col, dot_nt(ck, bk), 0.0)
        diag = jnp.sum(bk.astype(F32) * ck.astype(F32), axis=1, keepdims=True)
        coef_ref[rows, :] = dot(parts3(diag * pad_ref[rows, :] + skip), narrow)
    lane = lax.broadcasted_iota(jnp.int32, (SPAN, 128), 1)

    def pair(hp, _):
        cols = pl.ds(pl.multiple_of(hp * 128, 128), 128)
        for k in range(2):
            rows = slice(k * SPAN, (k + 1) * SPAN)
            xp = x_ref[rows, cols]
            tops, bots = [], []
            for half in range(2):
                h = hp * 2 + half
                rrow = rt_ref[k, pl.ds(h, 1), :]
                hcols = pl.ds(pl.multiple_of(h * 128, 128), 128)
                top = cexp_ref[k * SPAN:k * SPAN + HALF, hcols]
                bot = cexp_ref[k * SPAN + HALF:(k + 1) * SPAN, hcols]
                wt = s_ref[k, :HALF, :HALF] * jnp.exp2(jnp.minimum(top + rrow[:, :HALF], BIG))
                wb = s_ref[k, HALF:, :] * jnp.exp2(
                    jnp.minimum(jnp.concatenate([bot, bot], axis=1) + rrow, BIG))
                tops += split2(wt)
                bots += split2(wb)
            yt = dot(jnp.concatenate(tops, axis=0), xp[:HALF])
            yb = dot(jnp.concatenate(bots, axis=0), xp)
            ys = [jnp.concatenate([v[256 * h:256 * h + 128] + v[256 * h + 128:256 * h + 256] for v in (yt, yb)], axis=0)
                  for h in range(2)]
            ys_ref[rows, cols] = jnp.where(lane < 64, ys[0], ys[1])
        return 0

    lax.fori_loop(0, 8, pair, 0, unroll=2)

    s10 = dot_nt(c_ref[SPAN:, :], b_ref[:SPAN, :])
    qdt = parts3(jnp.exp2(cums[0][SPAN - 1:SPAN, :] + rs[0]))
    p = parts3(jnp.exp2(cums[1]))
    for j in range(4):
        cols = slice(j * 256, (j + 1) * 256)
        xq = dot(qdt, narrow[:, cols]) * x_ref[:SPAN, cols].astype(F32)
        ys_ref[SPAN:, cols] += dot(p, narrow[:, cols]) * dot3(s10, xq, dot)

    gain = gain_ref[...]

    def norm(i, _):
        rows = pl.ds(pl.multiple_of(i * 32, 32), 32)
        z = z_ref[rows, :].astype(F32)
        y = ys_ref[rows, :] + coef_ref[rows, :] * x_ref[rows, :].astype(F32)
        gated = y * (z / (1.0 + jnp.exp(-z)))
        inv = lax.rsqrt(jnp.mean(gated * gated, axis=1, keepdims=True) + 1e-05)
        n_ref[rows, :] = (gated * inv * gain).astype(BF16)
        return 0

    lax.fori_loop(0, TOK // 32, norm, 0, unroll=2)


def bwd_kernel(u_hbm, ys_hbm, x_hbm, z_hbm, b_ref, c_ref, dt_ref, rate_ref, skip_ref, gain_ref,
               dx_ref, dz_hbm, db_ref, dc_ref, ddt_ref, small_ref,
               pad_ref, ratepad_ref, rexp_ref, ct_ref, s_ref, coef_ref, dy_ref, dxs_ref, ds_ref, dg_ref,
               u_ref, ys_ref, x_ref, z_ref, dz_ref, sem):
    loads = [
        pltpu.make_async_copy(src, dst, sem.at[j])
        for j, (src, dst) in enumerate(((z_hbm, z_ref), (ys_hbm, ys_ref), (x_hbm, x_ref), (u_hbm, u_ref)))
    ]
    for load in loads:
        load.start()
    rate, cums, rs = prepare(dt_ref, rate_ref, pad_ref, ratepad_ref)
    wide = spread_matrix(HALF)
    narrow = spread_matrix(64)
    row = lax.broadcasted_iota(jnp.int32, (SPAN, SPAN), 0)
    col = lax.broadcasted_iota(jnp.int32, (SPAN, SPAN), 1)
    ratepad_ref[0:1, :HEADS] = skip_ref[...]
    skip = ratepad_ref[0:1, :]
    diags = []
    for k in range(2):
        rows = slice(k * SPAN, (k + 1) * SPAN)
        rexp_ref[rows, :] = dot(parts3(rs[k]), wide)
        ct_ref[k] = cums[k].T
        bk, ck = b_ref[rows, :], c_ref[rows, :]
        s_ref[k] = jnp.where(row < col, dot_nt(bk, ck), 0.0)
        diag = jnp.sum(bk.astype(F32) * ck.astype(F32), axis=1, keepdims=True)
        diags.append(diag)
        coef_ref[rows, :] = dot(parts3(diag * pad_ref[rows, :] + skip), narrow)

    gain = gain_ref[...]
    dg_ref[...] = jnp.zeros((8, CH), F32)

    def gate(i, _):
        rows = pl.ds(pl.multiple_of(i * 32, 32), 32)
        z = z_ref[rows, :].astype(F32)
        y = ys_ref[rows, :] + coef_ref[rows, :] * x_ref[rows, :].astype(F32)
        sig = 1.0 / (1.0 + jnp.exp(-z))
        sz = z * sig
        gated = y * sz
        inv = lax.rsqrt(jnp.mean(gated * gated, axis=1, keepdims=True) + 1e-05)
        unit = gated * inv
        u = u_ref[rows, :]
        ug = u * unit
        dg_ref[...] += (ug[0:8] + ug[8:16]) + (ug[16:24] + ug[24:32])
        v = u * gain
        dgated = inv * (v - unit * jnp.mean(v * unit, axis=1, keepdims=True))
        dy_ref[rows, :] = dgated * sz
        dz_ref[rows, :] = (dgated * y * (sig * (1.0 + z * (1.0 - sig)))).astype(BF16)
        return 0

    for load in loads:
        load.wait()
    lax.fori_loop(0, TOK // 32, gate, 0, unroll=4)
    store = pltpu.make_async_copy(dz_ref, dz_hbm, sem.at[4])
    store.start()

    ds_ref[...] = jnp.zeros((2, SPAN, SPAN), F32)
    lane = lax.broadcasted_iota(jnp.int32, (SPAN, 128), 1)

    def pair(hp, _):
        cols = pl.ds(pl.multiple_of(hp * 128, 128), 128)
        for k in range(2):
            rows = slice(k * SPAN, (k + 1) * SPAN)
            xp = x_ref[rows, cols].astype(F32)
            dh, dl = split2(dy_ref[rows, cols])
            dhl = jnp.concatenate([dh, dl], axis=1)
            xx = []
            for half in range(2):
                xm = jnp.where((lane < 64) if half == 0 else (lane >= 64), xp, 0.0).astype(BF16)
                xx.append(jnp.concatenate([xm, xm], axis=1))
            gts = dot_nt(jnp.concatenate([v[:HALF] for v in xx], axis=0), dhl)
            gbs = dot_nt(jnp.concatenate([v[HALF:] for v in xx], axis=0), dhl[HALF:])
            ths, tls, bhs, bls = [], [], [], []
            dst, dsb = ds_ref[k, :HALF, :], ds_ref[k, HALF:, HALF:]
            for half in range(2):
                h = hp * 2 + half
                part = slice(half * HALF, (half + 1) * HALF)
                crow = ct_ref[k, pl.ds(h, 1), :]
                hcols = pl.ds(pl.multiple_of(h * 128, 128), 128)
                top = rexp_ref[k * SPAN:k * SPAN + HALF, hcols]
                bot = rexp_ref[k * SPAN + HALF:(k + 1) * SPAN, hcols]
                et = jnp.exp2(jnp.minimum(jnp.concatenate([top, top], axis=1) + crow, BIG))
                eb = jnp.exp2(jnp.minimum(bot + crow[:, HALF:], BIG))
                dst = dst + et * gts[part]
                dsb = dsb + eb * gbs[part]
                hi, lo = split2(s_ref[k, :HALF, :] * et)
                ths.append(hi)
                tls.append(lo)
                hi, lo = split2(s_ref[k, HALF:, HALF:] * eb)
                bhs.append(hi)
                bls.append(lo)
            ds_ref[k, :HALF, :] = dst
            ds_ref[k, HALF:, HALF:] = dsb
            ot = dot(jnp.concatenate(ths, axis=0), dhl)
            ob = dot(jnp.concatenate(bhs, axis=0), dhl[HALF:])
            ot = (ot[:, :128] + ot[:, 128:]) + dot(jnp.concatenate(tls, axis=0), dh)
            ob = (ob[:, :128] + ob[:, 128:]) + dot(jnp.concatenate(bls, axis=0), dh[HALF:])
            outs = [jnp.concatenate([v[h * HALF:(h + 1) * HALF] for v in (ot, ob)], axis=0) for h in range(2)]
            dxs_ref[rows, cols] = jnp.where(lane < 64, outs[0], outs[1])
        return 0

    lax.fori_loop(0, 8, pair, 0, unroll=2)

    st = dot_nt(b_ref[:SPAN, :], c_ref[SPAN:, :])
    qdt = parts3(jnp.exp2(cums[0][SPAN - 1:SPAN, :] + rs[0]))
    p = parts3(jnp.exp2(cums[1]))
    dst = jnp.zeros((SPAN, SPAN), F32)
    for j in range(4):
        cols = slice(j * 256, (j + 1) * 256)
        qx = dot(qdt, narrow[:, cols])
        xq = qx * x_ref[:SPAN, cols].astype(F32)
        pdy = dot(p, narrow[:, cols]) * dy_ref[SPAN:, cols]
        dxs_ref[:SPAN, cols] += qx * dot3(st, pdy, dot)
        dst = dst + dot3(xq, pdy, dot_nt)

    seg_row = lax.broadcasted_iota(jnp.int32, (CH, 128), 0)
    seg_col = lax.broadcasted_iota(jnp.int32, (CH, 128), 1)
    seg = jnp.where(seg_row >> 6 == seg_col, 1.0, 0.0).astype(BF16)

    def heads_sum(v):
        hi, lo = split2(v)
        return dot(hi, seg) + dot(lo, seg)

    tri = triangle(SPAN, False)
    later = jnp.zeros((1, 128), F32)
    rate_sum = jnp.zeros((1, 128), F32)
    skip_sum = jnp.zeros((1, 128), F32)
    for k in (1, 0):
        rows = slice(k * SPAN, (k + 1) * SPAN)
        xf = x_ref[rows, :].astype(F32)
        dy = dy_ref[rows, :]
        dxs = dxs_ref[rows, :]
        kx = heads_sum(dy * xf)
        r = heads_sum(dy * ys_ref[rows, :])
        q = heads_sum(xf * dxs)
        suffix = cumulate(tri, r - q) + later
        later = suffix[0:1, :]
        dt = pad_ref[rows, :]
        ddt = q / dt + kx * diags[k] + rate * suffix
        ddt_ref[rows, :] = ddt[:, :HEADS]
        rate_sum = rate_sum + rate * jnp.sum(dt * suffix, axis=0, keepdims=True)
        skip_sum = skip_sum + jnp.sum(kx, axis=0, keepdims=True)
        sd = jnp.sum(dt * kx, axis=1, keepdims=True)
        dsk = jnp.where(row < col, ds_ref[k], 0.0)
        bk, ck = b_ref[rows, :], c_ref[rows, :]
        sh, sl = split2(dsk)
        db = dot(sh, ck) + dot(sl, ck) + sd * ck.astype(F32)
        sh, sl = split2(dsk.T)
        dc = dot(sh, bk) + dot(sl, bk) + sd * bk.astype(F32)
        if k == 0:
            oh, ol = split2(dst)
            db = db + dot(oh, c_ref[SPAN:, :]) + dot(ol, c_ref[SPAN:, :])
        else:
            oh, ol = split2(dst.T)
            dc = dc + dot(oh, b_ref[:SPAN, :]) + dot(ol, b_ref[:SPAN, :])
        db_ref[rows, :] = db.astype(BF16)
        dc_ref[rows, :] = dc.astype(BF16)
        dx_ref[rows, :] = (dxs + coef_ref[rows, :] * dy).astype(BF16)

    dg = jnp.sum(dg_ref[...], axis=0, keepdims=True)
    for j in range(8):
        small_ref[j:j + 1, :] = dg[:, j * 128:(j + 1) * 128]
    small_ref[8:9, :] = rate_sum
    small_ref[9:10, :] = skip_sum
    small_ref[10:16, :] = jnp.zeros((6, 128), F32)
    store.wait()


def scan_forward(x, z, b, c, dt, rate, skip, gain):
    return pl.pallas_call(
        fwd_kernel,
        out_shape=(jax.ShapeDtypeStruct((TOK, CH), F32), jax.ShapeDtypeStruct((TOK, CH), BF16)),
        scratch_shapes=[
            pltpu.VMEM((TOK, 128), F32),
            pltpu.VMEM((8, 128), F32),
            pltpu.VMEM((TOK, HEADS * HALF), F32),
            pltpu.VMEM((2, 128, SPAN), F32),
            pltpu.VMEM((2, SPAN, SPAN), F32),
            pltpu.VMEM((TOK, CH), F32),
        ],
        compiler_params=pltpu.CompilerParams(vmem_limit_bytes=VMEM_LIMIT),
        cost_estimate=SMALL,
        name="scan_forward",
    )(x, z, b, c, dt, rate, skip, gain)


def scan_backward(u, ys, x, z, b, c, dt, rate, skip, gain):
    return pl.pallas_call(
        bwd_kernel,
        out_shape=(
            jax.ShapeDtypeStruct((TOK, CH), BF16),
            jax.ShapeDtypeStruct((TOK, CH), BF16),
            jax.ShapeDtypeStruct((TOK, 128), BF16),
            jax.ShapeDtypeStruct((TOK, 128), BF16),
            jax.ShapeDtypeStruct((TOK, HEADS), F32),
            jax.ShapeDtypeStruct((16, 128), F32),
        ),
        scratch_shapes=[
            pltpu.VMEM((TOK, 128), F32),
            pltpu.VMEM((8, 128), F32),
            pltpu.VMEM((TOK, HEADS * HALF), F32),
            pltpu.VMEM((2, 128, SPAN), F32),
            pltpu.VMEM((2, SPAN, SPAN), F32),
            pltpu.VMEM((TOK, CH), F32),
            pltpu.VMEM((TOK, CH), F32),
            pltpu.VMEM((TOK, CH), F32),
            pltpu.VMEM((2, SPAN, SPAN), F32),
            pltpu.VMEM((8, CH), F32),
            pltpu.VMEM((TOK, CH), F32),
            pltpu.VMEM((TOK, CH), F32),
            pltpu.VMEM((TOK, CH), BF16),
            pltpu.VMEM((TOK, CH), BF16),
            pltpu.VMEM((TOK, CH), BF16),
            pltpu.SemaphoreType.DMA((5,)),
        ],
        in_specs=[pl.BlockSpec(memory_space=pltpu.HBM)] * 4 + [pl.BlockSpec(memory_space=pltpu.VMEM)] * 6,
        out_specs=tuple(pl.BlockSpec(memory_space=pltpu.HBM if j == 1 else pltpu.VMEM) for j in range(6)),
        compiler_params=pltpu.CompilerParams(vmem_limit_bytes=VMEM_LIMIT),
        cost_estimate=SMALL,
        name="scan_backward",
    )(u, ys, x, z, b, c, dt, rate, skip, gain)


AXES = {"z": 8, "xl": 2, "c": 2, "y": 4, "xh": 2}
DP = ("z", "xl", "c")
TP = ("y", "xh")


def send(v, axis, shift):
    n = AXES[axis]
    return lax.ppermute(v, axis, [(i, (i + shift) % n) for i in range(n)])


def swap(v, axis, mask):
    return lax.ppermute(v, axis, [(i, i ^ mask) for i in range(AXES[axis])])


def both_ways(up, down, axis):
    return send(up, axis, 1), send(down, axis, -1)


def tie(values, *first):
    return lax.optimization_barrier((tuple(values),) + tuple(first))[0]


def shuffle(name, shapes, plan, scalars, *arrays):
    count = len(plan([0] * len(scalars)))

    def kernel(s_ref, *refs):
        src, dst, sem = refs[:len(arrays)], refs[len(arrays):-1], refs[-1]
        copies = [
            pltpu.make_async_copy(src[i].at[a], dst[o].at[b], sem.at[k])
            for k, (i, a, o, b) in enumerate(plan([s_ref[j] for j in range(len(scalars))]))
        ]
        for copy in copies:
            copy.start()
        for copy in copies:
            copy.wait()

    return pl.pallas_call(
        kernel,
        out_shape=tuple(jax.ShapeDtypeStruct(s, BF16) for s in shapes),
        in_specs=[pl.BlockSpec(memory_space=pltpu.SMEM)] + [pl.BlockSpec(memory_space=pl.ANY)] * len(arrays),
        out_specs=tuple(pl.BlockSpec(memory_space=pltpu.VMEM) for _ in shapes),
        scratch_shapes=[pltpu.SemaphoreType.DMA((count,))],
        cost_estimate=SMALL,
        name=name,
    )(jnp.stack([s.astype(jnp.int32) for s in scalars]), *arrays)


def own_first(rows, core):
    def kernel(core_ref, in_ref, out_ref):
        for j in range(16):
            even = in_ref[:, 256 * j:256 * j + 128]
            odd = in_ref[:, 256 * j + 128:256 * j + 256]
            first = core_ref[0] == 0
            out_ref[:, 128 * j:128 * j + 128] = jnp.where(first, even, odd)
            out_ref[:, 2048 + 128 * j:2048 + 128 * j + 128] = jnp.where(first, odd, even)

    return pl.pallas_call(
        kernel,
        out_shape=jax.ShapeDtypeStruct(rows.shape, rows.dtype),
        in_specs=[pl.BlockSpec(memory_space=pltpu.SMEM), pl.BlockSpec(memory_space=pltpu.VMEM)],
        out_specs=pl.BlockSpec(memory_space=pltpu.VMEM),
        cost_estimate=SMALL,
        name="own_first",
    )(core.astype(jnp.int32).reshape(1), rows)


def at_rows(start, size):
    return (pl.ds(pl.multiple_of(start, 32), size), slice(None)) if not isinstance(start, int) else (slice(start, start + size), slice(None))


def place_tokens(yi, xh, first, *pieces):
    parts = ((0, 64, 0, 0, 0), (1, 64, 0, 1, 0), (2, 64, 3, 0, 0), (3, 64, 3, 1, 0), (4, 64, 1, 0, 0),
             (5, 64, 1, 1, 0), (6, 32, 2, 0, 0), (7, 32, 2, 0, 32), (8, 32, 2, 1, 0), (9, 32, 2, 1, 32))

    def plan(s):
        moves = []
        for piece, size, turn, other, offset in parts:
            start = ((s[0] + turn) % 4) * 128 + (1 - s[1] if other else s[1]) * 64 + offset
            moves.append((piece, (slice(None), slice(first, first + 2048)), 0, at_rows(start, size)))
        return moves

    return shuffle("place_tokens", [(TOK, 2048)], plan, (yi, xh), *pieces)[0]


def weight_blocks(zi, shifts, keep, theirs, normed, normed_other):
    def kernel(at_ref, a_ref, b_ref, n_ref, m_ref, out_ref):
        def term(r, n):
            return lax.dot_general(r[...], n[...], (((0,), (0,)), ((), ())), preferred_element_type=F32)

        out_ref[0] = term(a_ref, n_ref) + term(b_ref, m_ref)

    columns = pl.BlockSpec((TOK, 256), lambda i, at: (0, at[i]))
    whole = pl.BlockSpec((TOK, CH), lambda i, at: (0, 0))
    return pl.pallas_call(
        kernel,
        grid_spec=pltpu.PrefetchScalarGridSpec(
            num_scalar_prefetch=1,
            grid=(len(shifts),),
            in_specs=[columns, columns, whole, whole],
            out_specs=pl.BlockSpec((1, 256, CH), lambda i, at: (i, 0, 0)),
        ),
        out_shape=jax.ShapeDtypeStruct((len(shifts), 256, CH), F32),
        compiler_params=pltpu.CompilerParams(vmem_limit_bytes=VMEM_LIMIT),
        cost_estimate=SMALL,
        name="weight_blocks",
    )(jnp.stack([(zi + k + 8) % 8 for k in shifts]).astype(jnp.int32), keep, theirs, normed, normed_other)


def ring_step(zi, shift, keep, theirs, normed, normed_other, up, down):
    width = up.shape[1]
    at = CH - width

    def kernel(at_ref, a_ref, b_ref, n_ref, m_ref, up_ref, down_ref, up_out, down_out):
        def term(r, n):
            return lax.dot_general(r[...], n[...], (((0,), (0,)), ((), ())), preferred_element_type=F32)

        total = term(a_ref, n_ref) + term(b_ref, m_ref)

        @pl.when(pl.program_id(0) == 0)
        def _():
            if at:
                up_out[:, :at] = total[:, :at].astype(BF16)
            up_out[:, at:] = (total[:, at:] + up_ref[...].astype(F32)).astype(BF16)

        @pl.when(pl.program_id(0) == 1)
        def _():
            if at:
                down_out[:, width:] = total[:, width:].astype(BF16)
            down_out[:, :width] = (total[:, :width] + down_ref[...].astype(F32)).astype(BF16)

    columns = pl.BlockSpec((TOK, 256), lambda i, at: (0, at[i]))
    whole = pl.BlockSpec((TOK, CH), lambda i, at: (0, 0))
    part = pl.BlockSpec((256, width), lambda i, at: (0, 0))
    full = pl.BlockSpec((256, CH), lambda i, at: (0, 0))
    return pl.pallas_call(
        kernel,
        grid_spec=pltpu.PrefetchScalarGridSpec(
            num_scalar_prefetch=1,
            grid=(2,),
            in_specs=[columns, columns, whole, whole, part, part],
            out_specs=(full, full),
        ),
        out_shape=(jax.ShapeDtypeStruct((256, CH), BF16),) * 2,
        compiler_params=pltpu.CompilerParams(vmem_limit_bytes=VMEM_LIMIT),
        cost_estimate=SMALL,
        name="ring_step",
    )(jnp.stack([(zi + k + 8) % 8 for k in (shift, -shift)]).astype(jnp.int32), keep, theirs, normed, normed_other, up, down)


def back_project(core, keep, give, w):
    def kernel(core_ref, a_ref, b_ref, v_ref, w_ref, out_ref):
        out_ref[...] = dot(a_ref[...], v_ref[...].reshape(2048, 256)) + dot(b_ref[...], w_ref[...].reshape(2048, 256))

    rows = pl.BlockSpec((TOK, 2048), lambda i, core: (0, 0))
    return pl.pallas_call(
        kernel,
        grid_spec=pltpu.PrefetchScalarGridSpec(
            num_scalar_prefetch=1,
            grid=(4,),
            in_specs=[
                rows,
                rows,
                pl.BlockSpec((16, None, 128, 256), lambda i, core: (0, core[0], 0, i)),
                pl.BlockSpec((16, None, 128, 256), lambda i, core: (0, 1 - core[0], 0, i)),
            ],
            out_specs=pl.BlockSpec((TOK, 256), lambda i, core: (0, i)),
        ),
        out_shape=jax.ShapeDtypeStruct((TOK, CH), F32),
        compiler_params=pltpu.CompilerParams(vmem_limit_bytes=VMEM_LIMIT),
        cost_estimate=SMALL,
        name="back_project",
    )(core.astype(jnp.int32).reshape(1), keep, give, w, w)


def on_device(grad_out, x, z, b, c, dt, rate, skip, gain, w_out):
    zi, xl, core, yi, xh = (lax.axis_index(a) for a in ("z", "xl", "c", "y", "xh"))
    scan = (x, z, b.reshape(TOK, 128), c.reshape(TOK, 128), dt, rate[None], skip[None], gain[None])

    w = lax.all_gather(w_out, DP, axis=0, tiled=True).reshape(16, 2, 128, CH)

    own = own_first(grad_out, core)
    below, above = both_ways(own, own, "y")
    other = send(own, "xh", 1)
    below, above, other, late = tie((below, above, other, scan[6]))

    b_other, a_other = both_ways(other, other, "y")
    far_b, far_a = both_ways(below[:32], above[32:], "y")
    ys, normed = scan_forward(*scan[:6], late, scan[7])
    b_other, a_other, far_b, far_a, normed = tie((b_other, a_other, far_b, far_a, normed))

    far_other = both_ways(b_other[:32], a_other[32:], "y")
    normed_other = send(normed, "c", 1)
    far_other, normed_other = tie((far_other, normed_other))
    pieces = (own, other, below, b_other, above, a_other, far_b, far_a) + far_other
    give = place_tokens(yi, xh, 2048, *pieces)
    theirs = send(give, "c", 1)
    keep = place_tokens(yi, xh, 0, *tie(pieces, give))
    theirs, keep = tie((theirs, keep))

    def blocks(*shifts):
        return weight_blocks(zi, shifts, keep, theirs, normed, normed_other)

    half = CH // 2
    far = blocks(4)[0].astype(BF16)
    up, down = both_ways(far[:, half:], far[:, :half], "z")
    mine = blocks(0)[0]
    w, = tie((w,), mine)
    upstream = back_project(core, keep, give, w)
    up, down, mine, upstream = tie((up, down, mine, upstream))

    up, down = both_ways(*ring_step(zi, 3, keep, theirs, normed, normed_other, up, down), "z")
    dx, dz, db, dc, ddt, small = scan_backward(upstream, ys, *scan)
    up, down, small = tie((up, down, small))

    up, down = both_ways(*ring_step(zi, 2, keep, theirs, normed, normed_other, up, down), "z")
    last = blocks(1, -1)
    small = small + send(small, "c", 1)
    small = small + send(small, "xl", 1)
    small = small + swap(small, "z", 1)
    up, down, last, small = tie((up, down, last, small))

    def halves(r):
        return lax.dynamic_slice_in_dim(r, (1 - xl) * 128, 128, 0), lax.dynamic_slice_in_dim(r, xl * 128, 128, 0)

    up_leave, up_stay = halves((last[0] + up.astype(F32)).astype(BF16))
    down_leave, down_stay = halves((last[1] + down.astype(F32)).astype(BF16))
    up_leave, down_leave = both_ways(up_leave, down_leave, "z")
    up_stay, down_stay = both_ways(up_stay, down_stay, "z")
    small = small + swap(small, "z", 2)
    leave, stay = halves(mine)
    up_leave, down_leave, small = tie((up_leave, down_leave, small))
    leave = send(leave + (up_leave.astype(F32) + down_leave.astype(F32)), "xl", 1)
    small = small + swap(small, "z", 4)
    up_stay, down_stay, leave, stay = tie((up_stay, down_stay, leave, stay), small)
    grad_weight = (stay + leave) + (up_stay.astype(F32) + down_stay.astype(F32))
    return (dx, dz, db[:, None], dc[:, None], ddt, small[8, :HEADS], small[9, :HEADS],
            small[:8].reshape(CH), grad_weight)


def solution(mesh):
    fine = jax.sharding.Mesh(mesh.devices.reshape(tuple(AXES.values())), tuple(AXES))
    part = P(DP, TP)
    part3 = P(DP, TP, None)
    head = P(TP)
    return jax.shard_map(
        on_device,
        mesh=fine,
        in_specs=(P(DP + TP, None), part, part, part3, part3, part, head, head, head, part),
        out_specs=(part, part, part3, part3, part, head, head, head, part),
        check_vma=False,
    )
```

```python
import jax
import jax.numpy as jnp
from jax import lax
from jax.experimental import pallas as pl
from jax.experimental.pallas import tpu as pltpu
from jax.sharding import PartitionSpec as P

F32, BF16 = jnp.float32, jnp.bfloat16
HEADS = 16
SPAN = 256
TOK = 512
CH = 1024
HALF = 128
LOG2E = 1.4426950408889634
BIG = 126.0
VMEM_LIMIT = 48 * 1024 * 1024
SMALL = pl.CostEstimate(flops=1000, bytes_accessed=1000, transcendentals=0)


def dot(a, b):
    return jnp.dot(a, b, preferred_element_type=F32)


def dot_nt(a, b):
    return lax.dot_general(a, b, (((1,), (1,)), ((), ())), preferred_element_type=F32)


def split2(v):
    hi = v.astype(BF16)
    return hi, (v - hi.astype(F32)).astype(BF16)


def dot3(a, b, fn):
    ah, al = split2(a)
    bh, bl = split2(b)
    return fn(ah, bh) + (fn(ah, bl) + fn(al, bh))


def spread_matrix(width):
    row = lax.broadcasted_iota(jnp.int32, (128, HEADS * width), 0)
    col = lax.broadcasted_iota(jnp.int32, (128, HEADS * width), 1)
    return jnp.where((row < 48) & ((row & 15) == col >> (width.bit_length() - 1)), 1.0, 0.0).astype(BF16)


def parts3(v):
    lane = lax.broadcasted_iota(jnp.int32, v.shape, 1)
    v = jnp.where(lane < HEADS, v, 0.0)
    one = v.astype(BF16).astype(F32)
    rest = v - one
    two = rest.astype(BF16).astype(F32)
    three = rest - two
    return (one + pltpu.roll(two, 16, 1) + pltpu.roll(three, 32, 1)).astype(BF16)


def cumulate(tri, v):
    one = v.astype(BF16)
    rest = v - one.astype(F32)
    two = rest.astype(BF16)
    three = (rest - two.astype(F32)).astype(BF16)
    return dot(tri, one) + (dot(tri, two) + dot(tri, three))


def triangle(n, lower):
    row = lax.broadcasted_iota(jnp.int32, (n, n), 0)
    col = lax.broadcasted_iota(jnp.int32, (n, n), 1)
    return jnp.where(row >= col if lower else row <= col, 1.0, 0.0).astype(BF16)


def prepare(dt_ref, rate_ref, pad_ref, ratepad_ref):
    pad_ref[...] = jnp.ones((TOK, 128), F32)
    pad_ref[:, :HEADS] = dt_ref[...]
    ratepad_ref[...] = jnp.zeros((8, 128), F32)
    ratepad_ref[0:1, :HEADS] = rate_ref[...]
    rate = -jnp.exp(ratepad_ref[0:1, :])
    tri = triangle(SPAN, True)
    cums, rs = [], []
    for k in range(2):
        dt = pad_ref[k * SPAN:(k + 1) * SPAN, :]
        cum = cumulate(tri, dt * (rate * LOG2E))
        cums.append(cum)
        rs.append(jnp.log2(dt) - cum)
    return rate, cums, rs


def fwd_kernel(x_ref, z_ref, b_ref, c_ref, dt_ref, rate_ref, skip_ref, gain_ref,
               ys_ref, n_ref, pad_ref, ratepad_ref, cexp_ref, rt_ref, s_ref, coef_ref):
    rate, cums, rs = prepare(dt_ref, rate_ref, pad_ref, ratepad_ref)
    wide = spread_matrix(HALF)
    narrow = spread_matrix(64)
    row = lax.broadcasted_iota(jnp.int32, (SPAN, SPAN), 0)
    col = lax.broadcasted_iota(jnp.int32, (SPAN, SPAN), 1)
    ratepad_ref[0:1, :HEADS] = skip_ref[...]
    skip = ratepad_ref[0:1, :]
    for k in range(2):
        rows = slice(k * SPAN, (k + 1) * SPAN)
        cexp_ref[rows, :] = dot(parts3(cums[k]), wide)
        rt_ref[k] = rs[k].T
        bk, ck = b_ref[rows, :], c_ref[rows, :]
        s_ref[k] = jnp.where(row > col, dot_nt(ck, bk), 0.0)
        diag = jnp.sum(bk.astype(F32) * ck.astype(F32), axis=1, keepdims=True)
        coef_ref[rows, :] = dot(parts3(diag * pad_ref[rows, :] + skip), narrow)
    lane = lax.broadcasted_iota(jnp.int32, (SPAN, 128), 1)

    def pair(hp, _):
        cols = pl.ds(pl.multiple_of(hp * 128, 128), 128)
        for k in range(2):
            rows = slice(k * SPAN, (k + 1) * SPAN)
            xp = x_ref[rows, cols]
            tops, bots = [], []
            for half in range(2):
                h = hp * 2 + half
                rrow = rt_ref[k, pl.ds(h, 1), :]
                hcols = pl.ds(pl.multiple_of(h * 128, 128), 128)
                top = cexp_ref[k * SPAN:k * SPAN + HALF, hcols]
                bot = cexp_ref[k * SPAN + HALF:(k + 1) * SPAN, hcols]
                wt = s_ref[k, :HALF, :HALF] * jnp.exp2(jnp.minimum(top + rrow[:, :HALF], BIG))
                wb = s_ref[k, HALF:, :] * jnp.exp2(
                    jnp.minimum(jnp.concatenate([bot, bot], axis=1) + rrow, BIG))
                tops += split2(wt)
                bots += split2(wb)
            yt = dot(jnp.concatenate(tops, axis=0), xp[:HALF])
            yb = dot(jnp.concatenate(bots, axis=0), xp)
            ys = [jnp.concatenate([v[256 * h:256 * h + 128] + v[256 * h + 128:256 * h + 256] for v in (yt, yb)], axis=0)
                  for h in range(2)]
            ys_ref[rows, cols] = jnp.where(lane < 64, ys[0], ys[1])
        return 0

    lax.fori_loop(0, 8, pair, 0, unroll=2)

    s10 = dot_nt(c_ref[SPAN:, :], b_ref[:SPAN, :])
    qdt = parts3(jnp.exp2(cums[0][SPAN - 1:SPAN, :] + rs[0]))
    p = parts3(jnp.exp2(cums[1]))
    for j in range(4):
        cols = slice(j * 256, (j + 1) * 256)
        xq = dot(qdt, narrow[:, cols]) * x_ref[:SPAN, cols].astype(F32)
        ys_ref[SPAN:, cols] += dot(p, narrow[:, cols]) * dot3(s10, xq, dot)

    gain = gain_ref[...]

    def norm(i, _):
        rows = pl.ds(pl.multiple_of(i * 32, 32), 32)
        z = z_ref[rows, :].astype(F32)
        y = ys_ref[rows, :] + coef_ref[rows, :] * x_ref[rows, :].astype(F32)
        gated = y * (z / (1.0 + jnp.exp(-z)))
        inv = lax.rsqrt(jnp.mean(gated * gated, axis=1, keepdims=True) + 1e-05)
        n_ref[rows, :] = (gated * inv * gain).astype(BF16)
        return 0

    lax.fori_loop(0, TOK // 32, norm, 0, unroll=2)


def bwd_kernel(u_hbm, ys_hbm, x_hbm, z_hbm, b_ref, c_ref, dt_ref, rate_ref, skip_ref, gain_ref,
               dx_ref, dz_hbm, db_ref, dc_ref, ddt_ref, small_ref,
               pad_ref, ratepad_ref, rexp_ref, ct_ref, s_ref, coef_ref, dy_ref, dxs_ref, ds_ref, dg_ref,
               u_ref, ys_ref, x_ref, z_ref, dz_ref, sem):
    loads = [
        pltpu.make_async_copy(src, dst, sem.at[j])
        for j, (src, dst) in enumerate(((z_hbm, z_ref), (ys_hbm, ys_ref), (x_hbm, x_ref), (u_hbm, u_ref)))
    ]
    for load in loads:
        load.start()
    rate, cums, rs = prepare(dt_ref, rate_ref, pad_ref, ratepad_ref)
    wide = spread_matrix(HALF)
    narrow = spread_matrix(64)
    row = lax.broadcasted_iota(jnp.int32, (SPAN, SPAN), 0)
    col = lax.broadcasted_iota(jnp.int32, (SPAN, SPAN), 1)
    ratepad_ref[0:1, :HEADS] = skip_ref[...]
    skip = ratepad_ref[0:1, :]
    diags = []
    for k in range(2):
        rows = slice(k * SPAN, (k + 1) * SPAN)
        rexp_ref[rows, :] = dot(parts3(rs[k]), wide)
        ct_ref[k] = cums[k].T
        bk, ck = b_ref[rows, :], c_ref[rows, :]
        s_ref[k] = jnp.where(row < col, dot_nt(bk, ck), 0.0)
        diag = jnp.sum(bk.astype(F32) * ck.astype(F32), axis=1, keepdims=True)
        diags.append(diag)
        coef_ref[rows, :] = dot(parts3(diag * pad_ref[rows, :] + skip), narrow)

    gain = gain_ref[...]
    dg_ref[...] = jnp.zeros((8, CH), F32)

    def gate(i, _):
        rows = pl.ds(pl.multiple_of(i * 32, 32), 32)
        z = z_ref[rows, :].astype(F32)
        y = ys_ref[rows, :] + coef_ref[rows, :] * x_ref[rows, :].astype(F32)
        sig = 1.0 / (1.0 + jnp.exp(-z))
        sz = z * sig
        gated = y * sz
        inv = lax.rsqrt(jnp.mean(gated * gated, axis=1, keepdims=True) + 1e-05)
        unit = gated * inv
        u = u_ref[rows, :]
        ug = u * unit
        dg_ref[...] += (ug[0:8] + ug[8:16]) + (ug[16:24] + ug[24:32])
        v = u * gain
        dgated = inv * (v - unit * jnp.mean(v * unit, axis=1, keepdims=True))
        dy_ref[rows, :] = dgated * sz
        dz_ref[rows, :] = (dgated * y * (sig * (1.0 + z * (1.0 - sig)))).astype(BF16)
        return 0

    for load in loads:
        load.wait()
    lax.fori_loop(0, TOK // 32, gate, 0, unroll=4)
    store = pltpu.make_async_copy(dz_ref, dz_hbm, sem.at[4])
    store.start()

    ds_ref[...] = jnp.zeros((2, SPAN, SPAN), F32)
    lane = lax.broadcasted_iota(jnp.int32, (SPAN, 128), 1)

    def pair(hp, _):
        cols = pl.ds(pl.multiple_of(hp * 128, 128), 128)
        for k in range(2):
            rows = slice(k * SPAN, (k + 1) * SPAN)
            xp = x_ref[rows, cols].astype(F32)
            dh, dl = split2(dy_ref[rows, cols])
            dhl = jnp.concatenate([dh, dl], axis=1)
            xx = []
            for half in range(2):
                xm = jnp.where((lane < 64) if half == 0 else (lane >= 64), xp, 0.0).astype(BF16)
                xx.append(jnp.concatenate([xm, xm], axis=1))
            gts = dot_nt(jnp.concatenate([v[:HALF] for v in xx], axis=0), dhl)
            gbs = dot_nt(jnp.concatenate([v[HALF:] for v in xx], axis=0), dhl[HALF:])
            ths, tls, bhs, bls = [], [], [], []
            dst, dsb = ds_ref[k, :HALF, :], ds_ref[k, HALF:, HALF:]
            for half in range(2):
                h = hp * 2 + half
                part = slice(half * HALF, (half + 1) * HALF)
                crow = ct_ref[k, pl.ds(h, 1), :]
                hcols = pl.ds(pl.multiple_of(h * 128, 128), 128)
                top = rexp_ref[k * SPAN:k * SPAN + HALF, hcols]
                bot = rexp_ref[k * SPAN + HALF:(k + 1) * SPAN, hcols]
                et = jnp.exp2(jnp.minimum(jnp.concatenate([top, top], axis=1) + crow, BIG))
                eb = jnp.exp2(jnp.minimum(bot + crow[:, HALF:], BIG))
                dst = dst + et * gts[part]
                dsb = dsb + eb * gbs[part]
                hi, lo = split2(s_ref[k, :HALF, :] * et)
                ths.append(hi)
                tls.append(lo)
                hi, lo = split2(s_ref[k, HALF:, HALF:] * eb)
                bhs.append(hi)
                bls.append(lo)
            ds_ref[k, :HALF, :] = dst
            ds_ref[k, HALF:, HALF:] = dsb
            ot = dot(jnp.concatenate(ths, axis=0), dhl)
            ob = dot(jnp.concatenate(bhs, axis=0), dhl[HALF:])
            ot = (ot[:, :128] + ot[:, 128:]) + dot(jnp.concatenate(tls, axis=0), dh)
            ob = (ob[:, :128] + ob[:, 128:]) + dot(jnp.concatenate(bls, axis=0), dh[HALF:])
            outs = [jnp.concatenate([v[h * HALF:(h + 1) * HALF] for v in (ot, ob)], axis=0) for h in range(2)]
            dxs_ref[rows, cols] = jnp.where(lane < 64, outs[0], outs[1])
        return 0

    lax.fori_loop(0, 8, pair, 0, unroll=2)

    st = dot_nt(b_ref[:SPAN, :], c_ref[SPAN:, :])
    qdt = parts3(jnp.exp2(cums[0][SPAN - 1:SPAN, :] + rs[0]))
    p = parts3(jnp.exp2(cums[1]))
    dst = jnp.zeros((SPAN, SPAN), F32)
    for j in range(4):
        cols = slice(j * 256, (j + 1) * 256)
        qx = dot(qdt, narrow[:, cols])
        xq = qx * x_ref[:SPAN, cols].astype(F32)
        pdy = dot(p, narrow[:, cols]) * dy_ref[SPAN:, cols]
        dxs_ref[:SPAN, cols] += qx * dot3(st, pdy, dot)
        dst = dst + dot3(xq, pdy, dot_nt)

    seg_row = lax.broadcasted_iota(jnp.int32, (CH, 128), 0)
    seg_col = lax.broadcasted_iota(jnp.int32, (CH, 128), 1)
    seg = jnp.where(seg_row >> 6 == seg_col, 1.0, 0.0).astype(BF16)

    def heads_sum(v):
        hi, lo = split2(v)
        return dot(hi, seg) + dot(lo, seg)

    tri = triangle(SPAN, False)
    later = jnp.zeros((1, 128), F32)
    rate_sum = jnp.zeros((1, 128), F32)
    skip_sum = jnp.zeros((1, 128), F32)
    for k in (1, 0):
        rows = slice(k * SPAN, (k + 1) * SPAN)
        xf = x_ref[rows, :].astype(F32)
        dy = dy_ref[rows, :]
        dxs = dxs_ref[rows, :]
        kx = heads_sum(dy * xf)
        r = heads_sum(dy * ys_ref[rows, :])
        q = heads_sum(xf * dxs)
        suffix = cumulate(tri, r - q) + later
        later = suffix[0:1, :]
        dt = pad_ref[rows, :]
        ddt = q / dt + kx * diags[k] + rate * suffix
        ddt_ref[rows, :] = ddt[:, :HEADS]
        rate_sum = rate_sum + rate * jnp.sum(dt * suffix, axis=0, keepdims=True)
        skip_sum = skip_sum + jnp.sum(kx, axis=0, keepdims=True)
        sd = jnp.sum(dt * kx, axis=1, keepdims=True)
        dsk = jnp.where(row < col, ds_ref[k], 0.0)
        bk, ck = b_ref[rows, :], c_ref[rows, :]
        sh, sl = split2(dsk)
        db = dot(sh, ck) + dot(sl, ck) + sd * ck.astype(F32)
        sh, sl = split2(dsk.T)
        dc = dot(sh, bk) + dot(sl, bk) + sd * bk.astype(F32)
        if k == 0:
            oh, ol = split2(dst)
            db = db + dot(oh, c_ref[SPAN:, :]) + dot(ol, c_ref[SPAN:, :])
        else:
            oh, ol = split2(dst.T)
            dc = dc + dot(oh, b_ref[:SPAN, :]) + dot(ol, b_ref[:SPAN, :])
        db_ref[rows, :] = db.astype(BF16)
        dc_ref[rows, :] = dc.astype(BF16)
        dx_ref[rows, :] = (dxs + coef_ref[rows, :] * dy).astype(BF16)

    dg = jnp.sum(dg_ref[...], axis=0, keepdims=True)
    for j in range(8):
        small_ref[j:j + 1, :] = dg[:, j * 128:(j + 1) * 128]
    small_ref[8:9, :] = rate_sum
    small_ref[9:10, :] = skip_sum
    small_ref[10:16, :] = jnp.zeros((6, 128), F32)
    store.wait()


def scan_forward(x, z, b, c, dt, rate, skip, gain):
    return pl.pallas_call(
        fwd_kernel,
        out_shape=(jax.ShapeDtypeStruct((TOK, CH), F32), jax.ShapeDtypeStruct((TOK, CH), BF16)),
        scratch_shapes=[
            pltpu.VMEM((TOK, 128), F32),
            pltpu.VMEM((8, 128), F32),
            pltpu.VMEM((TOK, HEADS * HALF), F32),
            pltpu.VMEM((2, 128, SPAN), F32),
            pltpu.VMEM((2, SPAN, SPAN), F32),
            pltpu.VMEM((TOK, CH), F32),
        ],
        compiler_params=pltpu.CompilerParams(vmem_limit_bytes=VMEM_LIMIT),
        cost_estimate=SMALL,
        name="scan_forward",
    )(x, z, b, c, dt, rate, skip, gain)


def scan_backward(u, ys, x, z, b, c, dt, rate, skip, gain):
    return pl.pallas_call(
        bwd_kernel,
        out_shape=(
            jax.ShapeDtypeStruct((TOK, CH), BF16),
            jax.ShapeDtypeStruct((TOK, CH), BF16),
            jax.ShapeDtypeStruct((TOK, 128), BF16),
            jax.ShapeDtypeStruct((TOK, 128), BF16),
            jax.ShapeDtypeStruct((TOK, HEADS), F32),
            jax.ShapeDtypeStruct((16, 128), F32),
        ),
        scratch_shapes=[
            pltpu.VMEM((TOK, 128), F32),
            pltpu.VMEM((8, 128), F32),
            pltpu.VMEM((TOK, HEADS * HALF), F32),
            pltpu.VMEM((2, 128, SPAN), F32),
            pltpu.VMEM((2, SPAN, SPAN), F32),
            pltpu.VMEM((TOK, CH), F32),
            pltpu.VMEM((TOK, CH), F32),
            pltpu.VMEM((TOK, CH), F32),
            pltpu.VMEM((2, SPAN, SPAN), F32),
            pltpu.VMEM((8, CH), F32),
            pltpu.VMEM((TOK, CH), F32),
            pltpu.VMEM((TOK, CH), F32),
            pltpu.VMEM((TOK, CH), BF16),
            pltpu.VMEM((TOK, CH), BF16),
            pltpu.VMEM((TOK, CH), BF16),
            pltpu.SemaphoreType.DMA((5,)),
        ],
        in_specs=[pl.BlockSpec(memory_space=pltpu.HBM)] * 4 + [pl.BlockSpec(memory_space=pltpu.VMEM)] * 6,
        out_specs=tuple(pl.BlockSpec(memory_space=pltpu.HBM if j == 1 else pltpu.VMEM) for j in range(6)),
        compiler_params=pltpu.CompilerParams(vmem_limit_bytes=VMEM_LIMIT),
        cost_estimate=SMALL,
        name="scan_backward",
    )(u, ys, x, z, b, c, dt, rate, skip, gain)


AXES = {"z": 8, "xl": 2, "c": 2, "y": 4, "xh": 2}
DP = ("z", "xl", "c")
TP = ("y", "xh")


def send(v, axis, shift):
    n = AXES[axis]
    return lax.ppermute(v, axis, [(i, (i + shift) % n) for i in range(n)])


def swap(v, axis, mask):
    return lax.ppermute(v, axis, [(i, i ^ mask) for i in range(AXES[axis])])


def both_ways(up, down, axis):
    return send(up, axis, 1), send(down, axis, -1)


def tie(values, *first):
    return lax.optimization_barrier((tuple(values),) + tuple(first))[0]


def shuffle(name, shapes, plan, scalars, *arrays):
    count = len(plan([0] * len(scalars)))

    def kernel(s_ref, *refs):
        src, dst, sem = refs[:len(arrays)], refs[len(arrays):-1], refs[-1]
        copies = [
            pltpu.make_async_copy(src[i].at[a], dst[o].at[b], sem.at[k])
            for k, (i, a, o, b) in enumerate(plan([s_ref[j] for j in range(len(scalars))]))
        ]
        for copy in copies:
            copy.start()
        for copy in copies:
            copy.wait()

    return pl.pallas_call(
        kernel,
        out_shape=tuple(jax.ShapeDtypeStruct(s, BF16) for s in shapes),
        in_specs=[pl.BlockSpec(memory_space=pltpu.SMEM)] + [pl.BlockSpec(memory_space=pl.ANY)] * len(arrays),
        out_specs=tuple(pl.BlockSpec(memory_space=pltpu.VMEM) for _ in shapes),
        scratch_shapes=[pltpu.SemaphoreType.DMA((count,))],
        cost_estimate=SMALL,
        name=name,
    )(jnp.stack([s.astype(jnp.int32) for s in scalars]), *arrays)


def own_first(rows, core):
    def kernel(core_ref, in_ref, out_ref):
        for j in range(16):
            even = in_ref[:, 256 * j:256 * j + 128]
            odd = in_ref[:, 256 * j + 128:256 * j + 256]
            first = core_ref[0] == 0
            out_ref[:, 128 * j:128 * j + 128] = jnp.where(first, even, odd)
            out_ref[:, 2048 + 128 * j:2048 + 128 * j + 128] = jnp.where(first, odd, even)

    return pl.pallas_call(
        kernel,
        out_shape=jax.ShapeDtypeStruct(rows.shape, rows.dtype),
        in_specs=[pl.BlockSpec(memory_space=pltpu.SMEM), pl.BlockSpec(memory_space=pltpu.VMEM)],
        out_specs=pl.BlockSpec(memory_space=pltpu.VMEM),
        cost_estimate=SMALL,
        name="own_first",
    )(core.astype(jnp.int32).reshape(1), rows)


def at_rows(start, size):
    return (pl.ds(pl.multiple_of(start, 32), size), slice(None)) if not isinstance(start, int) else (slice(start, start + size), slice(None))


def place_tokens(yi, xh, first, *pieces):
    parts = ((0, 64, 0, 0, 0), (1, 64, 0, 1, 0), (2, 64, 3, 0, 0), (3, 64, 3, 1, 0), (4, 64, 1, 0, 0),
             (5, 64, 1, 1, 0), (6, 32, 2, 0, 0), (7, 32, 2, 0, 32), (8, 32, 2, 1, 0), (9, 32, 2, 1, 32))

    def plan(s):
        moves = []
        for piece, size, turn, other, offset in parts:
            start = ((s[0] + turn) % 4) * 128 + (1 - s[1] if other else s[1]) * 64 + offset
            moves.append((piece, (slice(None), slice(first, first + 2048)), 0, at_rows(start, size)))
        return moves

    return shuffle("place_tokens", [(TOK, 2048)], plan, (yi, xh), *pieces)[0]


def weight_blocks(zi, shifts, keep, theirs, normed, normed_other):
    def kernel(at_ref, a_ref, b_ref, n_ref, m_ref, out_ref):
        def term(r, n):
            return lax.dot_general(r[...], n[...], (((0,), (0,)), ((), ())), preferred_element_type=F32)

        out_ref[0] = term(a_ref, n_ref) + term(b_ref, m_ref)

    columns = pl.BlockSpec((TOK, 256), lambda i, at: (0, at[i]))
    whole = pl.BlockSpec((TOK, CH), lambda i, at: (0, 0))
    return pl.pallas_call(
        kernel,
        grid_spec=pltpu.PrefetchScalarGridSpec(
            num_scalar_prefetch=1,
            grid=(len(shifts),),
            in_specs=[columns, columns, whole, whole],
            out_specs=pl.BlockSpec((1, 256, CH), lambda i, at: (i, 0, 0)),
        ),
        out_shape=jax.ShapeDtypeStruct((len(shifts), 256, CH), F32),
        compiler_params=pltpu.CompilerParams(vmem_limit_bytes=VMEM_LIMIT),
        cost_estimate=SMALL,
        name="weight_blocks",
    )(jnp.stack([(zi + k + 8) % 8 for k in shifts]).astype(jnp.int32), keep, theirs, normed, normed_other)


def ring_step(zi, shift, keep, theirs, normed, normed_other, up, down):
    width = up.shape[1]
    at = CH - width

    def kernel(at_ref, a_ref, b_ref, n_ref, m_ref, up_ref, down_ref, up_out, down_out):
        def term(r, n):
            return lax.dot_general(r[...], n[...], (((0,), (0,)), ((), ())), preferred_element_type=F32)

        total = term(a_ref, n_ref) + term(b_ref, m_ref)

        @pl.when(pl.program_id(0) == 0)
        def _():
            if at:
                up_out[:, :at] = total[:, :at].astype(BF16)
            up_out[:, at:] = (total[:, at:] + up_ref[...].astype(F32)).astype(BF16)

        @pl.when(pl.program_id(0) == 1)
        def _():
            if at:
                down_out[:, width:] = total[:, width:].astype(BF16)
            down_out[:, :width] = (total[:, :width] + down_ref[...].astype(F32)).astype(BF16)

    columns = pl.BlockSpec((TOK, 256), lambda i, at: (0, at[i]))
    whole = pl.BlockSpec((TOK, CH), lambda i, at: (0, 0))
    part = pl.BlockSpec((256, width), lambda i, at: (0, 0))
    full = pl.BlockSpec((256, CH), lambda i, at: (0, 0))
    return pl.pallas_call(
        kernel,
        grid_spec=pltpu.PrefetchScalarGridSpec(
            num_scalar_prefetch=1,
            grid=(2,),
            in_specs=[columns, columns, whole, whole, part, part],
            out_specs=(full, full),
        ),
        out_shape=(jax.ShapeDtypeStruct((256, CH), BF16),) * 2,
        compiler_params=pltpu.CompilerParams(vmem_limit_bytes=VMEM_LIMIT),
        cost_estimate=SMALL,
        name="ring_step",
    )(jnp.stack([(zi + k + 8) % 8 for k in (shift, -shift)]).astype(jnp.int32), keep, theirs, normed, normed_other, up, down)


def back_project(core, keep, give, w):
    def kernel(core_ref, a_ref, b_ref, v_ref, w_ref, out_ref):
        out_ref[...] = dot(a_ref[...], v_ref[...].reshape(2048, 256)) + dot(b_ref[...], w_ref[...].reshape(2048, 256))

    rows = pl.BlockSpec((TOK, 2048), lambda i, core: (0, 0))
    return pl.pallas_call(
        kernel,
        grid_spec=pltpu.PrefetchScalarGridSpec(
            num_scalar_prefetch=1,
            grid=(4,),
            in_specs=[
                rows,
                rows,
                pl.BlockSpec((16, None, 128, 256), lambda i, core: (0, core[0], 0, i)),
                pl.BlockSpec((16, None, 128, 256), lambda i, core: (0, 1 - core[0], 0, i)),
            ],
            out_specs=pl.BlockSpec((TOK, 256), lambda i, core: (0, i)),
        ),
        out_shape=jax.ShapeDtypeStruct((TOK, CH), F32),
        compiler_params=pltpu.CompilerParams(vmem_limit_bytes=VMEM_LIMIT),
        cost_estimate=SMALL,
        name="back_project",
    )(core.astype(jnp.int32).reshape(1), keep, give, w, w)


def on_device(grad_out, x, z, b, c, dt, rate, skip, gain, w_out):
    zi, xl, core, yi, xh = (lax.axis_index(a) for a in ("z", "xl", "c", "y", "xh"))
    scan = (x, z, b.reshape(TOK, 128), c.reshape(TOK, 128), dt, rate[None], skip[None], gain[None])

    w = lax.all_gather(w_out, DP, axis=0, tiled=True).reshape(16, 2, 128, CH)

    own = own_first(grad_out, core)
    below, above = both_ways(own, own, "y")
    other = send(own, "xh", 1)
    below, above, other, late = tie((below, above, other, scan[6]))

    b_other, a_other = both_ways(other, other, "y")
    far_b, far_a = both_ways(below[:32], above[32:], "y")
    ys, normed = scan_forward(*scan[:6], late, scan[7])
    b_other, a_other, far_b, far_a, normed = tie((b_other, a_other, far_b, far_a, normed))

    far_other = both_ways(b_other[:32], a_other[32:], "y")
    normed_other = send(normed, "c", 1)
    far_other, normed_other = tie((far_other, normed_other))
    pieces = (own, other, below, b_other, above, a_other, far_b, far_a) + far_other
    give = place_tokens(yi, xh, 2048, *pieces)
    theirs = send(give, "c", 1)
    keep = place_tokens(yi, xh, 0, *tie(pieces, give))
    theirs, keep = tie((theirs, keep))

    def blocks(*shifts):
        return weight_blocks(zi, shifts, keep, theirs, normed, normed_other)

    half = CH // 2
    far = blocks(4)[0].astype(BF16)
    up, down = both_ways(far[:, half:], far[:, :half], "z")
    mine = blocks(0)[0]
    up, down, mine = tie((up, down, mine))

    up, down = both_ways(*ring_step(zi, 3, keep, theirs, normed, normed_other, up, down), "z")
    last = blocks(1, -1)
    w, = tie((w,), last)
    upstream = back_project(core, keep, give, w)
    up, down, last, upstream = tie((up, down, last, upstream))

    up, down = both_ways(*ring_step(zi, 2, keep, theirs, normed, normed_other, up, down), "z")
    dx, dz, db, dc, ddt, small = scan_backward(upstream, ys, *scan)
    up, down, small = tie((up, down, small))

    def halves(r):
        return lax.dynamic_slice_in_dim(r, (1 - xl) * 128, 128, 0), lax.dynamic_slice_in_dim(r, xl * 128, 128, 0)

    up_leave, up_stay = halves((last[0] + up.astype(F32)).astype(BF16))
    down_leave, down_stay = halves((last[1] + down.astype(F32)).astype(BF16))
    up_leave, down_leave = both_ways(up_leave, down_leave, "z")
    up_stay, down_stay = both_ways(up_stay, down_stay, "z")
    small = small + send(small, "c", 1)
    small = small + send(small, "xl", 1)
    small = small + swap(small, "z", 1)
    small = small + swap(small, "z", 2)
    leave, stay = halves(mine)
    up_leave, down_leave, small = tie((up_leave, down_leave, small))
    leave = send(leave + (up_leave.astype(F32) + down_leave.astype(F32)), "xl", 1)
    small = small + swap(small, "z", 4)
    up_stay, down_stay, leave, stay = tie((up_stay, down_stay, leave, stay), small)
    grad_weight = (stay + leave) + (up_stay.astype(F32) + down_stay.astype(F32))
    return (dx, dz, db[:, None], dc[:, None], ddt, small[8, :HEADS], small[9, :HEADS],
            small[:8].reshape(CH), grad_weight)


def solution(mesh):
    fine = jax.sharding.Mesh(mesh.devices.reshape(tuple(AXES.values())), tuple(AXES))
    part = P(DP, TP)
    part3 = P(DP, TP, None)
    head = P(TP)
    return jax.shard_map(
        on_device,
        mesh=fine,
        in_specs=(P(DP + TP, None), part, part, part3, part3, part, head, head, head, part),
        out_specs=(part, part, part3, part3, part, head, head, head, part),
        check_vma=False,
    )
```
